32 devices in a mesh: dp: 8 (over z, y), expert: 4 (over x, core).
Axes of the slice: x: 2, y: 2, z: 4, core: 2. Of those that a mesh axis runs over, the one named last changes fastest.
Arguments:
- tokens: bfloat16 [32768, 384], P(('dp', 'expert')), may hold values from -6 to 6
- cotangent: bfloat16 [32768, 384], P(('dp', 'expert')), may hold values from -6 to 6
- patch_counts: int32 [32, 5], P(('dp', 'expert')), may hold values from 96 to 192
- time_buckets: int32 [32], P(('dp', 'expert')), may hold values from 0 to 999
- image_labels: int32 [32, 5], P(('dp', 'expert')), may hold values from 0 to 1000
- expert_routes: int32 [32, 1024, 2], P(('dp', 'expert')), may hold values from 0 to 15, all different within a row; in each aligned block of 1024 rows (0 to 1023, 1024 to 2047, ..., all dimensions but the last counted through in order) at most 160 rows name the same one
- time_table: bfloat16 [1000, 384], replicated, may hold values from -4 to 4
- label_table: bfloat16 [1001, 384], replicated, may hold values from -4 to 4
- ada_weight: bfloat16 [384, 2304], replicated, may hold values from -0.3125 to 0.3125
- ada_bias: float32 [2304], replicated, may hold values from -2 to 2
- qkv_weight: bfloat16 [384, 1152], replicated, may hold values from -0.3125 to 0.3125
- out_weight: bfloat16 [384, 384], replicated, may hold values from -3.5 to 3.5
- out_bias: float32 [384], replicated, may hold values from -1.5 to 1.5
- router_weight: bfloat16 [384, 16], replicated, may hold values from -0.21875 to 0.21875
- expert_up: bfloat16 [16, 384, 1536], P('expert'), may hold values from -0.3125 to 0.3125
- expert_up_bias: float32 [16, 1536], P('expert'), may hold values from -1.5 to 1.5
- expert_down: bfloat16 [16, 1536, 384], P('expert'), may hold values from -0.15625 to 0.15625
- expert_down_bias: float32 [16, 384], P('expert'), may hold values from -1.5 to 1.5
- shared_up: bfloat16 [2, 384, 1536], replicated, may hold values from -0.3125 to 0.3125
- shared_up_bias: float32 [2, 1536], replicated, may hold values from -1.5 to 1.5
- shared_down: bfloat16 [2, 1536, 384], replicated, may hold values from -0.15625 to 0.15625
- shared_down_bias: float32 [2, 384], replicated, may hold values from -1.5 to 1.5
Outputs:
- layer_out: bfloat16 [32768, 384], P(('dp', 'expert'))
- grad_tokens: float32 [32768, 384], P(('dp', 'expert'))
- rms_stats: float32 [32, 2], P(('dp', 'expert'))
- grad_time_table: float32 [1000, 384], replicated
- grad_label_table: float32 [1001, 384], replicated
- grad_ada_weight: float32 [384, 2304], replicated
- grad_ada_bias: float32 [2304], replicated
- grad_qkv_weight: float32 [384, 1152], replicated
- grad_out_weight: float32 [384, 384], replicated
- grad_out_bias: float32 [384], replicated
- grad_router_weight: float32 [384, 16], replicated
- grad_expert_up: float32 [16, 384, 1536], P('expert', 'dp')
- grad_expert_up_bias: float32 [16, 1536], P('expert', 'dp')
- grad_expert_down: float32 [16, 1536, 384], P('expert', 'dp')
- grad_expert_down_bias: float32 [16, 384], P('expert', 'dp')
- grad_shared_up: float32 [2, 384, 1536], replicated
- grad_shared_up_bias: float32 [2, 1536], replicated
- grad_shared_down: float32 [2, 1536, 384], replicated
- grad_shared_down_bias: float32 [2, 384], replicated
The draws below stay inside these ranges and needn't reach their ends.
Inputs may be any that keep to these rules, and one draw needn't show every extreme that they name: `patch_counts`: the 5 images of a sequence fill its first slots in order; the remaining slots are padding. `expert_routes`: a slot's two experts differ; in each sequence at most 160 slots name one expert, and in some sequence one expert is named by exactly 160 slots.
All inputs are finite; a program needn't handle non-finite values.
Results may differ from the reference program's by a relative error of at most 0.015.
Values may be sent and summed in bfloat16 or wider, within the bound.
A program may use at most 256 MiB of HBM per device.

```python
import math
import jax
import jax.numpy as jnp
import numpy as np
from jax import lax

D = 384
H = 1536
HEADS = 6
HDIM = 64
NBUCK = 1000
NCLASS = 1001
SHARED = 2
SLOTS = 1024
MAXPATCH = 192
CAP = 160
E = 16
IMGS = 5
SEQS = 32
TOKENS = 32768


def with_ends(array, key, low, high):
    place = [jax.random.randint(jax.random.fold_in(key, axis), (), 0, length) for axis, length in enumerate(array.shape)]
    widest = array.shape.index(max(array.shape))
    beside = place[:widest] + [(place[widest] + 1) % array.shape[widest]] + place[widest + 1:]
    return array.at[tuple(place)].set(low).at[tuple(beside)].set(high)


def level_of(key, dims, cuts, low, top_value):
    factor_of = 1.0
    for axis_at, shards_of in cuts:
        draws = jax.random.uniform(jax.random.fold_in(jax.random.fold_in(key, 6), axis_at), (shards_of,), jnp.float32, low / len(cuts), top_value / len(cuts))
        factor_of = factor_of * jnp.repeat(jnp.exp(draws), dims[axis_at] // shards_of).reshape((-1,) + (1,) * (len(dims) - 1 - axis_at))
    return factor_of


def routed_block(stream_key, own, number, rows, count, top, bound, lean):
    order = jax.random.permutation(stream_key, count)
    heavy_load, usual = portions_of(count, rows * top, bound, lean, True), portions_of(count, rows * top, bound, lean, False)
    places = jnp.arange(count)

    def named(lengths, rotation):
        used = int((lengths > 0).sum())
        fixed = max(1, used // 4)
        passed = fixed + (places - fixed + rotation * (used - fixed)) % max(1, count - fixed)
        return jnp.zeros((count,), jnp.int32).at[order[jnp.where(places < fixed, places, passed)]].set(jnp.asarray(lengths, jnp.int32))

    lengths = jnp.where(number % 4 == 0, named(heavy_load, number // 4), named(usual, number - number // 4 - 1))
    mixed = jax.random.permutation(jax.random.fold_in(own, 3), count)
    giver, taker = mixed[0:count // 2 * 2:2], mixed[1:count // 2 * 2:2]
    margin = jnp.minimum(lengths[giver] - 1, bound - lengths[taker]) // 2
    margin = jnp.where((giver == order[0]) | (taker == order[0]) | (lengths[taker] == 0), 0, jnp.maximum(margin, 0))
    passed = jax.random.randint(jax.random.fold_in(own, 4), (count // 2,), 0, 1 << 20) % (margin + 1)
    lengths = lengths.at[giver].add(-passed).at[taker].add(passed)
    items = jnp.searchsorted(jnp.cumsum(lengths), jnp.arange(rows * top), side="right").astype(jnp.int32)
    table = items.reshape(top, rows).T
    table = table[jax.random.permutation(jax.random.fold_in(own, 1), rows)]
    rotation = jax.random.randint(jax.random.fold_in(own, 2), (rows, 1), 0, top)
    return jnp.take_along_axis(table, (jnp.arange(top)[None, :] + rotation) % top, axis=1)


def portions_of(count, total, most, skew, full):
    portions = [(1 << 20) // math.isqrt(rank ** skew) + 1 for rank in range(1, count + 1)]
    largest = most if full else min(most, max(-(-total // count), total * portions[0] // sum(portions)))
    least = 1 if total - largest >= count - 1 else 0
    given, rest = [largest] + [least] * (count - 1), total - largest - least * (count - 1)
    while rest > 0:
        movable = [i for i in range(1, count) if given[i] < largest] or [i for i in range(1, count) if given[i] < most]
        pool, remaining = sum([portions[i] for i in movable]), rest
        for i in movable:
            more = min(most - given[i], max(1, remaining * portions[i] // pool), rest)
            given[i] = given[i] + more
            rest = rest - more
    return np.array(given)


def gaussian(stream_key, shape, scale, bound, shards=(), held_as=jnp.bfloat16):
    gain = level_of(stream_key, shape, shards, -0.22, 0.18) if shards else 1.0
    values = jax.random.normal(stream_key, shape, jnp.float32) * scale * gain
    return jnp.minimum(jnp.maximum(values, -bound), bound).astype(held_as)


def setup_inputs(seed: int = 0) -> dict:
    splits = jax.random.split(jax.random.key(seed), 23)
    tokens = gaussian(splits[0], (TOKENS, D), 1.0, 6.0, ((0, 32),))
    cotangent = gaussian(splits[1], (TOKENS, D), 1.0, 6.0, ((0, 32),))
    patch_counts = with_ends(jax.random.randint(splits[2], (SEQS, IMGS), MAXPATCH // 2, MAXPATCH + 1), jax.random.fold_in(splits[2], 1), MAXPATCH // 2, MAXPATCH).astype(jnp.int32)
    time_buckets = with_ends(jax.random.randint(splits[3], (SEQS,), 0, NBUCK), jax.random.fold_in(splits[3], 1), 0, NBUCK - 1).astype(jnp.int32)
    image_labels = with_ends(jax.random.randint(splits[4], (SEQS, IMGS), 0, NCLASS), jax.random.fold_in(splits[4], 1), 0, NCLASS - 1).astype(jnp.int32)
    expert_routes_keys = jax.random.split(jax.random.fold_in(splits[5], 1), SEQS * SLOTS // SLOTS)
    expert_routes_turns = jax.random.permutation(jax.random.fold_in(splits[5], 3), SEQS * SLOTS // SLOTS)
    expert_routes = jax.vmap(lambda own, number: routed_block(jax.random.fold_in(splits[5], 2), own, number, SLOTS, E, 2, CAP, 1))(expert_routes_keys, expert_routes_turns).reshape((SEQS, SLOTS, 2))
    time_table = gaussian(splits[6], (NBUCK, D), 0.7, 4.0)
    label_table = gaussian(splits[7], (NCLASS, D), 0.7, 4.0)
    ada_weight = gaussian(splits[8], (D, 6 * D), D ** -0.5, 0.3125)
    ada_bias = gaussian(splits[9], (6 * D,), 0.3, 2.0, (), jnp.float32)
    qkv_weight = gaussian(splits[10], (D, 3 * D), D ** -0.5, 0.3125)
    out_weight = gaussian(splits[11], (D, D), (max(D // 128, 1)) ** -0.5, 3.5)
    out_bias = gaussian(splits[12], (D,), 0.2, 1.5, (), jnp.float32)
    router_weight = gaussian(splits[13], (D, E), (2 * D) ** -0.5, 0.21875)
    expert_up = gaussian(splits[14], (E, D, H), D ** -0.5, 0.3125, ((0, 4),))
    expert_up_bias = gaussian(splits[15], (E, H), 0.2, 1.5, ((0, 4),), jnp.float32)
    expert_down = gaussian(splits[16], (E, H, D), H ** -0.5, 0.15625, ((0, 4),))
    expert_down_bias = gaussian(splits[17], (E, D), 0.2, 1.5, ((0, 4),), jnp.float32)
    shared_up = gaussian(splits[18], (SHARED, D, H), D ** -0.5, 0.3125)
    shared_up_bias = gaussian(splits[19], (SHARED, H), 0.2, 1.5, (), jnp.float32)
    shared_down = gaussian(splits[20], (SHARED, H, D), H ** -0.5, 0.15625)
    shared_down_bias = gaussian(splits[21], (SHARED, D), 0.2, 1.5, (), jnp.float32)
    return dict(tokens=tokens, cotangent=cotangent, patch_counts=patch_counts, time_buckets=time_buckets, image_labels=image_labels, expert_routes=expert_routes, time_table=time_table, label_table=label_table, ada_weight=ada_weight, ada_bias=ada_bias, qkv_weight=qkv_weight, out_weight=out_weight, out_bias=out_bias, router_weight=router_weight, expert_up=expert_up, expert_up_bias=expert_up_bias, expert_down=expert_down, expert_down_bias=expert_down_bias, shared_up=shared_up, shared_up_bias=shared_up_bias, shared_down=shared_down, shared_down_bias=shared_down_bias)


@jax.custom_vjp
def low(v):
    return lax.optimization_barrier(v.astype(jnp.bfloat16)).astype(jnp.float32)

@jax.custom_vjp
def low_back(v):
    return v

def low_keep(v):
    return (low(v), None)

def low_pass(kept, grad):
    return (grad,)

def back_keep(v):
    return (v, None)

def back_low(kept, grad):
    return (low(grad),)
low.defvjp(low_keep, low_pass)
low_back.defvjp(back_keep, back_low)
NORM_EPS = 1e-06
MASK_FILL = -1e+30

def matmul(left, right):
    return jnp.dot(left, right, precision=lax.Precision.HIGHEST)

def norm_rows(matrix):
    row_mean = lax.optimization_barrier(jnp.mean(matrix, axis=-1, keepdims=True))
    centred = matrix - row_mean
    row_var = lax.optimization_barrier(jnp.mean(centred * centred, axis=-1, keepdims=True))
    return centred * lax.rsqrt(row_var + NORM_EPS)

def gelu_tanh(matrix):
    return jax.nn.gelu(matrix, approximate=True)

def layout(patch_counts, expert_routes, slot_count, expert_count):
    image_count = patch_counts.shape[0]
    slot_ids = jnp.arange(slot_count, dtype=jnp.int32)
    image_ends = jnp.cumsum(patch_counts).astype(jnp.int32)
    image_starts = image_ends - patch_counts
    member = (slot_ids[:, None] >= image_starts[None, :]) & (slot_ids[:, None] < image_ends[None, :])
    valid_rows = lax.optimization_barrier(jnp.sum(member.astype(jnp.int32), axis=1)).astype(jnp.int32)
    image_ids = jnp.arange(image_count, dtype=jnp.int32)
    segment = lax.optimization_barrier(jnp.sum(jnp.where(member, image_ids[None, :], 0), axis=1)).astype(jnp.int32) + (1 - valid_rows) * (image_count + slot_ids)
    expert_ids = jnp.arange(expert_count, dtype=jnp.int32)
    route_picks = ((expert_routes[:, :, None] == expert_ids[None, None, :]).astype(jnp.int32) * valid_rows[:, None, None]).reshape(2 * slot_count, expert_count)
    earlier = (jnp.cumsum(route_picks, axis=0) - route_picks).astype(jnp.int32)
    position = lax.optimization_barrier(jnp.sum(earlier * route_picks, axis=1)).astype(jnp.int32).reshape(slot_count, 2)
    target = jnp.where(valid_rows[:, None] > 0, expert_routes * CAP + position, -1).astype(jnp.int32)
    return (member, valid_rows, segment, target)

def one_sequence(weights, rows, counts, bucket, labels, routes):
    time_table, label_table, ada_weight, ada_bias, qkv_weight, out_weight, out_bias, router_weight, expert_up, expert_up_bias, expert_down, expert_down_bias, shared_up, shared_up_bias, shared_down, shared_down_bias = weights
    member, valid_rows, segment, target = layout(counts, routes, SLOTS, E)
    member_f = member.astype(jnp.float32)
    valid_f = valid_rows.astype(jnp.float32)[:, None]
    condition = label_table[labels] + time_table[bucket][None, :]
    cond_act = low(jax.nn.silu(condition))
    modulation = matmul(cond_act, ada_weight) + ada_bias
    tok_mod = matmul(member_f, modulation)
    shift_one, scale_one, gate_one, shift_two, scale_two, gate_two = jnp.split(tok_mod, 6, axis=1)
    mixed_in = low(norm_rows(rows) * (1.0 + scale_one) + shift_one)
    qkv_rows = low(low_back(matmul(mixed_in, qkv_weight)))
    queries = qkv_rows[:, :D].reshape(SLOTS, HEADS, HDIM)
    key_rows = qkv_rows[:, D:2 * D].reshape(SLOTS, HEADS, HDIM)
    value_rows = qkv_rows[:, 2 * D:].reshape(SLOTS, HEADS, HDIM)
    scores = low_back(jnp.einsum('qhd,khd->hqk', queries, key_rows, precision=lax.Precision.HIGHEST) * HDIM ** (-0.5))
    allowed = segment[:, None] == segment[None, :]
    scores = jnp.where(allowed[None], scores, MASK_FILL)
    soft_probs = jax.nn.softmax(scores, axis=-1)
    attended = low(low_back(jnp.einsum('hqk,khd->qhd', low(soft_probs), value_rows, precision=lax.Precision.HIGHEST))).reshape(SLOTS, D)
    attn_out = low_back(matmul(attended, out_weight) + out_bias)
    hidden_one = rows + valid_f * gate_one * attn_out
    moe_in = low(norm_rows(hidden_one) * (1.0 + scale_two) + shift_two)
    logits = low_back(matmul(moe_in, router_weight))
    chosen = jnp.take_along_axis(logits, routes, axis=1)
    gate_values = jax.nn.softmax(chosen, axis=1)
    slot_hot = (target[:, :, None] == jnp.arange(E * CAP, dtype=jnp.int32)[None, None, :]).astype(jnp.float32)
    dispatch_hot = slot_hot[:, 0] + slot_hot[:, 1]
    routed_rows = low_back(jnp.einsum('ts,td->sd', dispatch_hot, moe_in, precision=lax.Precision.HIGHEST)).reshape(E, CAP, D)
    expert_pre = low_back(jnp.einsum('ecd,edh->ech', routed_rows, expert_up, precision=lax.Precision.HIGHEST) + expert_up_bias[:, None, :])
    expert_act = low(gelu_tanh(expert_pre))
    expert_res = low(low_back(jnp.einsum('ech,ehd->ecd', expert_act, expert_down, precision=lax.Precision.HIGHEST) + expert_down_bias[:, None, :])).reshape(E * CAP, D)
    picked = jnp.einsum('tks,sd->tkd', slot_hot, expert_res, precision=lax.Precision.HIGHEST)
    routed = lax.optimization_barrier(jnp.sum(gate_values[:, :, None] * picked, axis=1))
    shared_total = jnp.zeros((SLOTS, D), jnp.float32)
    for shared_index in range(SHARED):
        shared_pre = low_back(matmul(moe_in, shared_up[shared_index]) + shared_up_bias[shared_index])
        shared_total = shared_total + matmul(low(gelu_tanh(shared_pre)), shared_down[shared_index]) + shared_down_bias[shared_index]
    branch = low_back(routed + shared_total)
    hidden_two = hidden_one + valid_f * gate_two * branch
    slot_total = jnp.sum(valid_f) * D
    stats = jnp.stack([jnp.sqrt(jnp.sum(valid_f * hidden_two * hidden_two) / slot_total), jnp.sqrt(jnp.sum(valid_f * branch * branch) / slot_total)])
    return (hidden_two, stats)

def reference(tokens, cotangent, patch_counts, time_buckets, image_labels, expert_routes, time_table, label_table, ada_weight, ada_bias, qkv_weight, out_weight, out_bias, router_weight, expert_up, expert_up_bias, expert_down, expert_down_bias, shared_up, shared_up_bias, shared_down, shared_down_bias):
    weights = tuple((item.astype(jnp.float32) for item in (time_table, label_table, ada_weight, ada_bias, qkv_weight, out_weight, out_bias, router_weight, expert_up, expert_up_bias, expert_down, expert_down_bias, shared_up, shared_up_bias, shared_down, shared_down_bias)))
    group = 4 if SEQS % 4 == 0 else 1
    batches = SEQS // group
    token_rows = tokens.astype(jnp.float32).reshape(batches, group, SLOTS, D)
    int_parts = (patch_counts.reshape(batches, group, IMGS), time_buckets.reshape(batches, group), image_labels.reshape(batches, group, IMGS), expert_routes.reshape(batches, group, SLOTS, 2))

    def forward(weights, token_rows):

        def one_batch(packed):
            rows_part, counts_part, bucket_part, label_part, route_part = packed
            return jax.vmap(one_sequence, in_axes=(None, 0, 0, 0, 0, 0))(weights, rows_part, counts_part, bucket_part, label_part, route_part)
        layer, stats = lax.map(jax.checkpoint(one_batch), (token_rows,) + int_parts)
        return (layer, stats)
    layer, pullback, stats = jax.vjp(forward, weights, token_rows, has_aux=True)
    weight_grads, token_grad = pullback(cotangent.astype(jnp.float32).reshape(batches, group, SLOTS, D))
    return (layer.reshape(TOKENS, D).astype(jnp.bfloat16), token_grad.reshape(TOKENS, D), stats.reshape(SEQS, 2), weight_grads[0], weight_grads[1], weight_grads[2], weight_grads[3], weight_grads[4], weight_grads[5], weight_grads[6], weight_grads[7], weight_grads[8], weight_grads[9], weight_grads[10], weight_grads[11], weight_grads[12], weight_grads[13], weight_grads[14], weight_grads[15])
```

```python
import functools

import jax
import jax.numpy as jnp
from jax import lax
from jax.experimental import pallas as pl
from jax.experimental.pallas import tpu as pltpu
from jax.sharding import Mesh, PartitionSpec as P

HEADS = 6
HDIM = 64
CAP = 160
PAD = 16
NORM_EPS = 1e-06
MASK_FILL = -1e30
ROWS_FIRST = (((0,), (0,)), ((), ()))
ROWS_LAST = (((1,), (1,)), ((), ()))
GELU_C = 0.7978845608028654
GELU_K = 0.044715
ALL = ("p0", "p1", "p2", "expert")
GROUP = ("p1", "p2", "expert")
F32 = jnp.float32
BF16 = jnp.bfloat16


def norm_rows(matrix):
    row_mean = jnp.mean(matrix, axis=-1, keepdims=True)
    centred = matrix - row_mean
    row_var = jnp.mean(centred * centred, axis=-1, keepdims=True)
    row_scale = lax.rsqrt(row_var + NORM_EPS)
    return (centred * row_scale, row_scale)


def norm_back(grad_in, normed, row_scale):
    grad_mean = jnp.mean(grad_in, axis=-1, keepdims=True)
    cross_mean = jnp.mean(grad_in * normed, axis=-1, keepdims=True)
    return (grad_in - grad_mean - normed * cross_mean) * row_scale


def high_low(values):
    high = values.astype(BF16)
    return (high, (values - high.astype(F32)).astype(BF16))


def ffn_kernel(
    routed,
    sources,
    row_block,
    pick_ref,
    x_ref,
    g_ref,
    up_ref,
    bu_ref,
    dn_ref,
    bd_ref,
    y_ref,
    dx_ref,
    dup_ref,
    dbu_ref,
    ddn_ref,
    dbd_ref,
    xs,
    gs,
    xt,
    gt,
    acts,
    dpres,
    yacc,
    dxacc,
    gate_rows,
    gate_cols,
):
    net = pl.program_id(0)
    chunk = pl.program_id(1)
    nets = pl.num_programs(0)
    chunks = pl.num_programs(1)
    rows, width = xs.shape

    @pl.when((net == 0) & (chunk == 0))
    def _():
        if routed:
            gate_rows[...] = jnp.zeros_like(gate_rows)
            for s in range(sources):
                xs[s * CAP : (s + 1) * CAP, :] = x_ref[s, :CAP, :]
                tail = x_ref[s, CAP : CAP + PAD, :256].astype(F32)
                gate_rows[s : s + 1, :] = tail[0:1] + tail[1:2]
            gate_cols[...] = gate_rows[...].T
            for s in range(sources):
                gate = gate_cols[:CAP, s : s + 1]
                gs[s * CAP : (s + 1) * CAP, :] = (g_ref[s].astype(F32) * gate).astype(BF16)
        else:
            xs[...] = x_ref[...]
            gs[...] = g_ref[...]
        for r in range(0, rows, 256):
            xt[:width, r : r + 256] = xs[r : r + 256, :].T
            gt[:, r : r + 256] = gs[r : r + 256, :].T
        xt[width:, :] = jnp.ones((xt.shape[0] - width, rows), BF16)
        yacc[...] = jnp.zeros_like(yacc)
        dxacc[...] = jnp.zeros_like(dxacc)
        dbd_ref[...] = jnp.sum(gs[...].astype(F32), axis=0, keepdims=True)

    up = up_ref[0]
    dn = dn_ref[0]
    bu = bu_ref[0]

    def block(i, carry):
        r = pl.ds(pl.multiple_of(i * row_block, row_block), row_block)
        pre = jnp.dot(xs[r, :], up, preferred_element_type=F32) + bu
        dact = lax.dot_general(gs[r, :], dn, ROWS_LAST, preferred_element_type=F32)
        square = pre * pre
        th = jnp.tanh(pre * (GELU_C + (GELU_C * GELU_K) * square))
        half = 0.5 + 0.5 * th
        act = (pre * half).astype(BF16)
        slope = half + (0.5 * pre) * (1.0 - th * th) * (GELU_C + (3 * GELU_C * GELU_K) * square)
        dpre = (dact * slope).astype(BF16)
        acts[r, :] = act
        dpres[r, :] = dpre
        yacc[r, :] += jnp.dot(act, dn, preferred_element_type=F32)
        dxacc[r, :] += lax.dot_general(dpre, up, ROWS_LAST, preferred_element_type=F32)
        return carry

    lax.fori_loop(0, rows // row_block, block, 0)
    dup = jnp.dot(xt[...], dpres[...], preferred_element_type=F32)
    dup_ref[0] = dup[:width].astype(BF16)
    dbu_ref[0] = dup[width : width + 1]
    ddn_ref[0] = jnp.dot(gt[...], acts[...], preferred_element_type=F32).T.astype(BF16)

    @pl.when((net == nets - 1) & (chunk == chunks - 1))
    def _():
        if routed:
            gate_rows[...] = jnp.zeros_like(gate_rows)
            place = lax.broadcasted_iota(jnp.int32, (CAP, 128), 1)
            total = jnp.zeros((CAP, 128), F32)
            for s in range(sources):
                r = slice(s * CAP, (s + 1) * CAP)
                res = (yacc[r, :] + bd_ref[0]).astype(BF16).astype(F32)
                gate = gate_cols[:CAP, s : s + 1]
                y_ref[s] = (res * gate).astype(BF16)
                inner = jnp.sum(res * g_ref[s].astype(F32), axis=1, keepdims=True)
                total = jnp.where(place == s, inner, total)
                dx_ref[s, :CAP, :] = dxacc[r, :].astype(BF16)
            gate_cols[:CAP, :] = total
            gate_rows[...] = gate_cols[...].T
            for s in range(sources):
                row = gate_rows[s : s + 1, :]
                high = row.astype(BF16).astype(F32)
                low = row - high
                rest = jnp.zeros((PAD - 2, 256), F32)
                tail = jnp.concatenate([high, low, rest], axis=0)
                tail = jnp.concatenate([tail, jnp.zeros((PAD, width - 256), F32)], axis=1)
                dx_ref[s, CAP : CAP + PAD, :] = tail.astype(BF16)
        else:
            bias = jnp.sum(bd_ref[...], axis=0)
            y_ref[...] = yacc[...] + bias
            dx_ref[...] = dxacc[...]


def ffn(routed, pick, x, g, up, bias_up, down, bias_down, chunk=256, row_block=320):
    nets = 1 if routed else up.shape[0]
    width, hidden = up.shape[1:]
    if routed:
        sources = x.shape[0]
        rows = sources * CAP
        y_shape = jax.ShapeDtypeStruct((sources, CAP, width), BF16)
        dx_shape = jax.ShapeDtypeStruct((sources, CAP + PAD, width), BF16)
    else:
        sources = 1
        rows = x.shape[0]
        y_shape = jax.ShapeDtypeStruct((rows, width), F32)
        dx_shape = y_shape

    def whole(shape):
        return pl.BlockSpec(shape, lambda n, h, p: (0,) * len(shape))

    flops = 12 * nets * rows * width * hidden
    return pl.pallas_call(
        functools.partial(ffn_kernel, routed, sources, row_block),
        grid_spec=pltpu.PrefetchScalarGridSpec(
            num_scalar_prefetch=1,
            grid=(nets, hidden // chunk),
            in_specs=[
                whole(x.shape),
                whole(g.shape),
                pl.BlockSpec((1, width, chunk), lambda n, h, p: (p[0] + n, 0, h)),
                pl.BlockSpec((1, 1, chunk), lambda n, h, p: (p[0] + n, 0, h)),
                pl.BlockSpec((1, chunk, width), lambda n, h, p: (p[0] + n, h, 0)),
                pl.BlockSpec((nets, 1, width), lambda n, h, p: (p[0], 0, 0)),
            ],
            out_specs=[
                whole(y_shape.shape),
                whole(dx_shape.shape),
                pl.BlockSpec((1, width, chunk), lambda n, h, p: (n, 0, h)),
                pl.BlockSpec((1, 1, chunk), lambda n, h, p: (n, 0, h)),
                pl.BlockSpec((1, chunk, width), lambda n, h, p: (n, h, 0)),
                whole((1, width)),
            ],
            scratch_shapes=[
                pltpu.VMEM((rows, width), BF16),
                pltpu.VMEM((rows, width), BF16),
                pltpu.VMEM((width + 16, rows), BF16),
                pltpu.VMEM((width, rows), BF16),
                pltpu.VMEM((rows, chunk), BF16),
                pltpu.VMEM((rows, chunk), BF16),
                pltpu.VMEM((rows, width), F32),
                pltpu.VMEM((rows, width), F32),
                pltpu.VMEM((128, 256), F32),
                pltpu.VMEM((256, 128), F32),
            ],
        ),
        out_shape=[
            y_shape,
            dx_shape,
            jax.ShapeDtypeStruct((nets, width, hidden), BF16),
            jax.ShapeDtypeStruct((nets, 1, hidden), F32),
            jax.ShapeDtypeStruct((nets, hidden, width), BF16),
            jax.ShapeDtypeStruct((1, width), F32),
        ],
        compiler_params=pltpu.CompilerParams(vmem_limit_bytes=56 * 2**20),
        cost_estimate=pl.CostEstimate(
            flops=flops, bytes_accessed=16 * 2**20, transcendentals=nets * rows * hidden
        ),
        name="routed_net" if routed else "shared_net",
    )(pick, x, g, up, bias_up[:, None, :], down, bias_down[:, None, :])


def exchange(blocks, axes):
    return lax.all_to_all(blocks, axes, split_axis=0, concat_axis=0, tiled=True)


def spread(block, axes):
    count = lax.axis_size(axes)
    return exchange(jnp.broadcast_to(block[None], (count,) + block.shape), axes)


def sum_blocks(blocks):
    return jnp.sum(blocks.astype(F32), axis=0)


def sum_everywhere(payload):
    rows, width = payload.shape
    near = ("p2", "expert")
    far = ("p0", "p1")
    near_count = lax.axis_size(near)
    far_count = lax.axis_size(far)
    piece = rows // near_count
    part = exchange(payload.astype(BF16).reshape(near_count, piece, width), near)
    part = sum_blocks(part).astype(BF16)
    part = part.reshape(piece, far_count, width // far_count).transpose(1, 0, 2)
    part = sum_blocks(exchange(part, far)).astype(BF16)
    part = spread(part, far).transpose(1, 0, 2).reshape(piece, width)
    return spread(part, near).reshape(rows, width)


def layout(patch_counts, expert_routes, slot_count, expert_count):
    image_count = patch_counts.shape[0]
    slot_ids = jnp.arange(slot_count, dtype=jnp.int32)
    image_ends = jnp.cumsum(patch_counts)
    image_starts = image_ends - patch_counts
    member = (slot_ids[:, None] >= image_starts[None, :]) & (
        slot_ids[:, None] < image_ends[None, :]
    )
    valid_rows = jnp.sum(member.astype(jnp.int32), axis=1)
    image_ids = jnp.arange(image_count, dtype=jnp.int32)
    segment = jnp.sum(jnp.where(member, image_ids[None, :], 0), axis=1) + (1 - valid_rows) * (
        image_count + slot_ids
    )
    expert_ids = jnp.arange(expert_count, dtype=jnp.int32)
    route_picks = (
        (expert_routes[:, :, None] == expert_ids[None, None, :]).astype(jnp.int32)
        * valid_rows[:, None, None]
    ).reshape(2 * slot_count, expert_count)
    earlier = jnp.cumsum(route_picks, axis=0) - route_picks
    position = jnp.sum(earlier * route_picks, axis=1).reshape(slot_count, 2)
    return (member, valid_rows, segment, position)


def block_scores(query_rows, key_rows, segment, first_row, row_block, attn_scale):
    scores = (
        jnp.einsum("qhd,khd->hqk", query_rows, key_rows, preferred_element_type=F32) * attn_scale
    )
    allowed = segment[first_row : first_row + row_block, None] == segment[None, :]
    return jnp.where(allowed[None], scores, MASK_FILL)


def attend_forward(queries, key_rows, value_rows, segment, row_block, attn_scale):
    slot_count = queries.shape[0]
    outputs = []
    log_parts = []
    for first_row in range(0, slot_count, row_block):
        scores = block_scores(
            queries[first_row : first_row + row_block],
            key_rows,
            segment,
            first_row,
            row_block,
            attn_scale,
        )
        row_top = jnp.max(scores, axis=-1, keepdims=True)
        expo_scores = jnp.exp(scores - row_top)
        row_total = jnp.sum(expo_scores, axis=-1, keepdims=True)
        soft_probs = (expo_scores / row_total).astype(BF16)
        outputs.append(
            jnp.einsum(
                "hqk,khd->qhd", soft_probs, value_rows, preferred_element_type=F32
            ).astype(BF16)
        )
        log_parts.append(row_top + jnp.log(row_total))
    return (jnp.concatenate(outputs, axis=0), jnp.concatenate(log_parts, axis=1))


def attend_backward(
    queries, key_rows, value_rows, segment, log_totals, grad_attended, row_block, attn_scale
):
    slot_count = queries.shape[0]
    grad_query_parts = []
    grad_keys = jnp.zeros(key_rows.shape, F32)
    grad_values = jnp.zeros(value_rows.shape, F32)
    for first_row in range(0, slot_count, row_block):
        query_rows = queries[first_row : first_row + row_block]
        grad_rows_here = grad_attended[first_row : first_row + row_block]
        scores = block_scores(query_rows, key_rows, segment, first_row, row_block, attn_scale)
        soft_probs = jnp.exp(scores - log_totals[:, first_row : first_row + row_block])
        grad_probs = jnp.einsum(
            "qhd,khd->hqk", grad_rows_here, value_rows, preferred_element_type=F32
        )
        row_inner = jnp.sum(soft_probs * grad_probs, axis=-1, keepdims=True)
        grad_scores = (soft_probs * (grad_probs - row_inner)).astype(BF16)
        grad_query_parts.append(
            jnp.einsum("hqk,khd->qhd", grad_scores, key_rows, preferred_element_type=F32)
            * attn_scale
        )
        grad_keys = (
            grad_keys
            + jnp.einsum("hqk,qhd->khd", grad_scores, query_rows, preferred_element_type=F32)
            * attn_scale
        )
        grad_values = grad_values + jnp.einsum(
            "hqk,qhd->khd", soft_probs.astype(BF16), grad_rows_here, preferred_element_type=F32
        )
    return (jnp.concatenate(grad_query_parts, axis=0), grad_keys, grad_values)


def body(
    tokens,
    cotangent,
    patch_counts,
    time_buckets,
    image_labels,
    expert_routes,
    time_table,
    label_table,
    ada_weight,
    ada_bias,
    qkv_weight,
    out_weight,
    out_bias,
    router_weight,
    expert_up,
    expert_up_bias,
    expert_down,
    expert_down_bias,
    shared_up,
    shared_up_bias,
    shared_down,
    shared_down_bias,
):
    slot_count, width = tokens.shape
    expert_count = router_weight.shape[1]
    local_count, _, hidden = expert_up.shape
    owners = lax.axis_size("expert")
    dp_count = lax.axis_size(("p0", "p1", "p2"))
    outer = lax.axis_size("p0")
    my_pick = lax.axis_index("p1") * lax.axis_size("p2") + lax.axis_index("p2")
    row_block = min(512, slot_count)
    attn_scale = HDIM ** (-0.5)
    routes = expert_routes[0]

    label_rows = jnp.take(label_table, image_labels[0], axis=0).astype(F32)
    time_row = jnp.take(time_table, time_buckets, axis=0).astype(F32)
    condition = label_rows + time_row
    cond_act = jax.nn.silu(condition).astype(BF16)
    modulation = jnp.dot(cond_act, ada_weight, preferred_element_type=F32) + ada_bias
    all_ids = spread(jnp.concatenate([image_labels, time_buckets[:, None]], axis=1), ALL)
    all_labels = all_ids[:, 0, :-1].reshape(-1)
    all_times = all_ids[:, 0, -1]

    member, valid_rows, segment, position = layout(
        patch_counts[0], routes, slot_count, expert_count
    )
    member_f = member.astype(F32)
    valid_f = valid_rows.astype(F32)[:, None]
    tok_mod = jnp.dot(member_f, modulation, precision=lax.Precision.HIGHEST)
    shift_one, scale_one, gate_one, shift_two, scale_two, gate_two = [
        tok_mod[:, part_index * width : (part_index + 1) * width] for part_index in range(6)
    ]

    block_of = (routes % local_count) * owners + routes // local_count
    target = jnp.where(valid_rows[:, None] > 0, block_of * CAP + position, -1)
    slots = jnp.arange(expert_count * CAP, dtype=jnp.int32)[:, None]
    hot = ((slots == target[None, :, 0]) | (slots == target[None, :, 1])).astype(BF16)

    grad_out = cotangent.astype(F32)
    grad_branch = (valid_f * gate_two * grad_out).astype(BF16)
    grad_branch_f = grad_branch.astype(F32)
    branch_rows = jnp.dot(hot, grad_branch, preferred_element_type=F32).astype(BF16)
    owner_branch = exchange(branch_rows.reshape(expert_count, CAP, width), GROUP)

    inputs = tokens.astype(F32)
    normed_one, scale_rows_one = norm_rows(inputs)
    mixed_in = (normed_one * (1.0 + scale_one) + shift_one).astype(BF16)
    qkv_rows = jnp.dot(mixed_in, qkv_weight, preferred_element_type=F32).astype(BF16)
    queries = qkv_rows[:, :width].reshape(slot_count, HEADS, HDIM)
    key_rows = qkv_rows[:, width : 2 * width].reshape(slot_count, HEADS, HDIM)
    value_rows = qkv_rows[:, 2 * width :].reshape(slot_count, HEADS, HDIM)
    attended, log_totals = attend_forward(
        queries, key_rows, value_rows, segment, row_block, attn_scale
    )
    attended_flat = attended.reshape(slot_count, width)
    attn_out = jnp.dot(attended_flat, out_weight, preferred_element_type=F32) + out_bias
    hidden_one = inputs + valid_f * gate_one * attn_out
    normed_two, scale_rows_two = norm_rows(hidden_one)
    moe_in = (normed_two * (1.0 + scale_two) + shift_two).astype(BF16)
    logits = jnp.dot(moe_in, router_weight, preferred_element_type=F32)
    expert_ids = jnp.arange(expert_count, dtype=jnp.int32)
    chosen = (routes[:, 0:1] == expert_ids) | (routes[:, 1:2] == expert_ids)
    gates = jax.nn.softmax(jnp.where(chosen, logits, -jnp.inf), axis=1)

    block_experts = (expert_ids % owners) * local_count + expert_ids // owners
    moe_rows = jnp.dot(hot, moe_in, preferred_element_type=F32).astype(BF16)
    gate_high, gate_low = high_low(gates[:, block_experts])

    def gate_slots(part):
        values = jnp.dot(hot, part, preferred_element_type=F32)
        values = values.reshape(expert_count, CAP, expert_count)
        return jnp.einsum("jpj->jp", values).astype(BF16)

    gate_tail = jnp.stack([gate_slots(gate_high), gate_slots(gate_low)], axis=1)
    gate_tail = jnp.pad(gate_tail, ((0, 0), (0, PAD - 2), (0, width - CAP)))
    send_rows = jnp.concatenate([moe_rows.reshape(expert_count, CAP, width), gate_tail], axis=1)
    owner_rows = exchange(send_rows, GROUP)

    no_pick = jnp.zeros((1,), jnp.int32)
    shared_total, grad_moe_in, grad_sup, grad_sup_bias, grad_sdown, grad_sdown_bias = ffn(
        False,
        no_pick,
        moe_in,
        grad_branch,
        shared_up,
        shared_up_bias,
        shared_down,
        shared_down_bias,
        chunk=768,
        row_block=1024,
    )
    shared_payload = jnp.concatenate(
        [grad_sup.reshape(-1, hidden), grad_sdown.reshape(-1, hidden)], axis=0
    )
    shared_sums = sum_everywhere(shared_payload).astype(F32)

    pick = jnp.full((1,), my_pick, jnp.int32)
    owner_res, owner_grads, grad_eup, grad_eup_bias, grad_edown, grad_edown_bias = ffn(
        True,
        pick,
        owner_rows,
        owner_branch,
        expert_up,
        expert_up_bias,
        expert_down,
        expert_down_bias,
        chunk=768,
        row_block=640,
    )
    returned = exchange(owner_res, GROUP).reshape(expert_count * CAP, width)
    returned_grads = exchange(owner_grads, GROUP)

    up_blocks = exchange(grad_eup.reshape(outer, width // outer, hidden), "p0")
    up_part = sum_blocks(up_blocks).astype(BF16).reshape(-1, width // dp_count, hidden)
    sum_eup = exchange(up_part, ("p1", "p2")).astype(F32)
    side = jnp.concatenate(
        [grad_eup_bias.reshape(dp_count, -1), grad_edown_bias.reshape(dp_count, -1)], axis=1
    )
    side_width = side.shape[1]
    side = jnp.pad(side.astype(BF16)[:, None, :], ((0, 0), (0, PAD - 1), (0, width - side_width)))
    down_payload = jnp.concatenate(
        [grad_edown.reshape(dp_count, hidden // dp_count, width), side], axis=1
    )
    down_rows = down_payload.shape[1]
    down_blocks = exchange(down_payload.reshape(outer, -1, down_rows, width), "p0")
    down_part = exchange(sum_blocks(down_blocks).astype(BF16), ("p1", "p2")).astype(F32)
    sum_edown = down_part[:, : hidden // dp_count]
    side_sums = down_part[:, hidden // dp_count]
    sum_eup_bias = side_sums[:, : hidden // dp_count]
    sum_edown_bias = side_sums[:, hidden // dp_count : side_width]

    routed = lax.dot_general(hot, returned, ROWS_FIRST, preferred_element_type=F32)
    branch = routed + shared_total
    hidden_two = hidden_one + valid_f * gate_two * branch
    slot_total = jnp.sum(valid_f) * width
    rms_stats = jnp.stack(
        [
            jnp.sqrt(jnp.sum(valid_f * hidden_two * hidden_two) / slot_total),
            jnp.sqrt(jnp.sum(valid_f * branch * branch) / slot_total),
        ]
    )[None, :]
    grad_gate_two = valid_f * grad_out * branch

    grad_rows = returned_grads[:, :CAP].reshape(expert_count * CAP, width)
    grad_moe_in = grad_moe_in + lax.dot_general(
        hot, grad_rows, ROWS_FIRST, preferred_element_type=F32
    )
    gate_grads = returned_grads[:, CAP : CAP + 2, :CAP].astype(F32)
    gate_grads = gate_grads[:, 0] + gate_grads[:, 1]
    hot_blocks = hot.reshape(expert_count, CAP, slot_count).astype(F32)
    grad_gates = jnp.einsum(
        "jpt,jp->tj", hot_blocks, gate_grads, precision=lax.Precision.HIGHEST
    )
    grad_gates = grad_gates.reshape(slot_count, local_count, owners)
    grad_gates = grad_gates.transpose(0, 2, 1).reshape(slot_count, expert_count)
    gate_inner = jnp.sum(gates * grad_gates, axis=1, keepdims=True)
    grad_logits = (gates * (grad_gates - gate_inner)).astype(BF16)
    grad_router = lax.dot_general(moe_in, grad_logits, ROWS_FIRST, preferred_element_type=F32)
    grad_moe_in = grad_moe_in + lax.dot_general(
        grad_logits, router_weight, ROWS_LAST, preferred_element_type=F32
    )
    grad_scale_two = grad_moe_in * normed_two
    grad_hidden_one = grad_out + norm_back(
        grad_moe_in * (1.0 + scale_two), normed_two, scale_rows_two
    )
    grad_attn = (valid_f * gate_one * grad_hidden_one).astype(BF16)
    grad_gate_one = valid_f * grad_hidden_one * attn_out
    grad_out_bias = jnp.sum(grad_attn.astype(F32), axis=0)
    grad_out_weight = lax.dot_general(
        attended_flat, grad_attn, ROWS_FIRST, preferred_element_type=F32
    )
    grad_attended = (
        lax.dot_general(grad_attn, out_weight, ROWS_LAST, preferred_element_type=F32)
        .astype(BF16)
        .reshape(slot_count, HEADS, HDIM)
    )
    grad_queries, grad_keys, grad_values = attend_backward(
        queries, key_rows, value_rows, segment, log_totals, grad_attended, row_block, attn_scale
    )
    grad_qkv = jnp.concatenate(
        [
            grad_queries.reshape(slot_count, width),
            grad_keys.reshape(slot_count, width),
            grad_values.reshape(slot_count, width),
        ],
        axis=1,
    ).astype(BF16)
    grad_qkv_weight = lax.dot_general(mixed_in, grad_qkv, ROWS_FIRST, preferred_element_type=F32)
    grad_mixed_in = lax.dot_general(grad_qkv, qkv_weight, ROWS_LAST, preferred_element_type=F32)
    grad_scale_one = grad_mixed_in * normed_one
    grad_tokens = grad_hidden_one + norm_back(
        grad_mixed_in * (1.0 + scale_one), normed_one, scale_rows_one
    )
    grad_tok_mod = jnp.concatenate(
        [grad_mixed_in, grad_scale_one, grad_gate_one, grad_moe_in, grad_scale_two, grad_gate_two],
        axis=1,
    )
    grad_modulation = lax.dot_general(
        member_f, grad_tok_mod, ROWS_FIRST, precision=lax.Precision.HIGHEST
    )
    grad_cond_act = lax.dot_general(
        grad_modulation, ada_weight.astype(F32), ROWS_LAST, precision=lax.Precision.HIGHEST
    )
    grad_condition = jax.vjp(jax.nn.silu, condition)[1](grad_cond_act)[0]

    image_count = grad_condition.shape[0]
    rows_out = jnp.concatenate([grad_modulation, grad_condition], axis=1).astype(BF16)
    rows_out = jnp.concatenate([rows_out, cond_act], axis=1)
    all_rows = spread(rows_out, ALL).reshape(-1, 8 * width)
    all_modulation = all_rows[:, : 6 * width]
    all_condition = all_rows[:, 6 * width : 7 * width]
    all_cond_act = all_rows[:, 7 * width :]
    sum_ada = lax.dot_general(
        all_cond_act, all_modulation, ROWS_FIRST, preferred_element_type=F32
    )
    sum_ada_bias = jnp.sum(all_modulation.astype(F32), axis=0)
    label_hot = (
        all_labels[:, None] == jnp.arange(label_table.shape[0], dtype=jnp.int32)[None, :]
    ).astype(BF16)
    sum_label = lax.dot_general(label_hot, all_condition, ROWS_FIRST, preferred_element_type=F32)
    time_hot = (
        jnp.repeat(all_times, image_count)[:, None]
        == jnp.arange(time_table.shape[0], dtype=jnp.int32)[None, :]
    ).astype(BF16)
    sum_time = lax.dot_general(time_hot, all_condition, ROWS_FIRST, preferred_element_type=F32)

    tail = jnp.concatenate(
        [
            jnp.concatenate([grad_qkv_weight, grad_out_weight], axis=1),
            grad_router.reshape(-1, hidden),
            grad_sup_bias.reshape(-1, hidden),
            jnp.pad(
                jnp.concatenate([grad_out_bias, grad_sdown_bias[0]])[None],
                ((0, 0), (0, hidden - 2 * width)),
            ),
        ],
        axis=0,
    )
    used = tail.shape[0]
    near_count = lax.axis_size(("p2", "expert"))
    tail = jnp.pad(tail, ((0, -used % (16 * near_count)), (0, 0)))
    tail = sum_everywhere(tail).astype(F32)
    router_rows = width * expert_count // hidden
    shared_count = shared_up.shape[0]
    sum_qkv = tail[:width, : 3 * width]
    sum_out_weight = tail[:width, 3 * width :]
    place = width + router_rows
    sum_router = tail[width:place].reshape(width, expert_count)
    sum_sup_bias = tail[place : place + shared_count]
    sum_out_bias = tail[place + shared_count, :width]
    sum_sdown_bias = jnp.broadcast_to(
        tail[place + shared_count, width : 2 * width][None], (shared_count, width)
    )
    half = grad_sup.size // hidden
    sum_sup = shared_sums[:half].reshape(grad_sup.shape)
    sum_sdown = shared_sums[half:].reshape(grad_sdown.shape)
    return (
        hidden_two.astype(BF16),
        grad_tokens,
        rms_stats,
        sum_time,
        sum_label,
        sum_ada,
        sum_ada_bias,
        sum_qkv,
        sum_out_weight,
        sum_out_bias,
        sum_router,
        sum_eup,
        sum_eup_bias,
        sum_edown,
        sum_edown_bias,
        sum_sup,
        sum_sup_bias,
        sum_sdown,
        sum_sdown_bias,
    )


def solution(mesh):
    dp_count = mesh.shape["dp"]
    owners = mesh.shape["expert"]
    split = Mesh(mesh.devices.reshape(dp_count // 4, 2, 2, owners), ALL)
    dp = ("p0", "p1", "p2")
    in_specs = (
        P(ALL, None),
        P(ALL, None),
        P(ALL, None),
        P(ALL),
        P(ALL, None),
        P(ALL, None, None),
        P(),
        P(),
        P(),
        P(),
        P(),
        P(),
        P(),
        P(),
        P("expert", None, None),
        P("expert", None),
        P("expert", None, None),
        P("expert", None),
        P(),
        P(),
        P(),
        P(),
    )
    out_specs = (
        P(ALL, None),
        P(ALL, None),
        P(ALL, None),
        P(),
        P(),
        P(),
        P(),
        P(),
        P(),
        P(),
        P(),
        P("expert", dp, None),
        P("expert", dp),
        P("expert", dp, None),
        P("expert", dp),
        P(),
        P(),
        P(),
        P(),
    )
    return jax.shard_map(body, mesh=split, in_specs=in_specs, out_specs=out_specs, check_vma=False)
```

```python
import functools

import jax
import jax.numpy as jnp
from jax import lax
from jax.experimental import pallas as pl
from jax.experimental.pallas import tpu as pltpu
from jax.sharding import Mesh, PartitionSpec as P

HEADS = 6
HDIM = 64
CAP = 160
PAD = 16
WINDOW = 192
BLOCK = 128
SPAN = BLOCK + 2 * WINDOW
TILE = 256
NORM_EPS = 1e-06
MASK_FILL = -1e30
ROWS_FIRST = (((0,), (0,)), ((), ()))
ROWS_LAST = (((1,), (1,)), ((), ()))
GELU_C = 0.7978845608028654
GELU_K = 0.044715
ALL = ("p0", "p1", "p2", "expert")
GROUP = ("p1", "p2", "expert")
MESH = pl.DeviceIdType.MESH
F32 = jnp.float32
BF16 = jnp.bfloat16
VMEM_BYTES = 56 * 2**20


def norm_rows(matrix):
    row_mean = jnp.mean(matrix, axis=-1, keepdims=True)
    centred = matrix - row_mean
    row_var = jnp.mean(centred * centred, axis=-1, keepdims=True)
    row_scale = lax.rsqrt(row_var + NORM_EPS)
    return (centred * row_scale, row_scale)


def norm_back(grad_in, normed, row_scale):
    grad_mean = jnp.mean(grad_in, axis=-1, keepdims=True)
    cross_mean = jnp.mean(grad_in * normed, axis=-1, keepdims=True)
    return (grad_in - grad_mean - normed * cross_mean) * row_scale


def high_low(values):
    high = values.astype(BF16)
    return (high, (values - high.astype(F32)).astype(BF16))


def iota(shape, dim):
    return lax.broadcasted_iota(jnp.int32, shape, dim)


def dot(left, right):
    return jnp.dot(left, right, preferred_element_type=F32)


def dot_t(left, right):
    return lax.dot_general(left, right, ROWS_LAST, preferred_element_type=F32)


def in_vmem():
    return pl.BlockSpec(memory_space=pltpu.VMEM)


def in_smem():
    return pl.BlockSpec(memory_space=pltpu.SMEM)


def anywhere():
    return pl.BlockSpec(memory_space=pl.ANY)


def like(shape, dtype):
    return jax.ShapeDtypeStruct(shape, dtype)


def image_bounds(counts_ref):
    bounds = []
    start = 0
    for image in range(counts_ref.shape[1]):
        end = start + counts_ref[0, image]
        bounds.append((start, end))
        start = end
    return bounds


def member_block(bounds, first, rows):
    lane = iota((1, 128), 1)
    low = jnp.zeros((1, 128), jnp.int32)
    high = jnp.zeros((1, 128), jnp.int32)
    for image, (start, end) in enumerate(bounds):
        hit = (lane == image) | (lane == 8 + image)
        low = jnp.where(hit, start, low)
        high = jnp.where(hit, end, high)
    slot = first + iota((rows, 128), 0)
    return ((slot >= low) & (slot < high)).astype(F32).astype(BF16)


def stack_modulation(mod, stack):
    high, low = high_low(mod)
    stack[...] = jnp.zeros_like(stack)
    stack[0:16, :] = jnp.concatenate([high.astype(F32), low.astype(F32)], axis=0).astype(BF16)


def segments(bounds, slot):
    total = bounds[-1][1]
    image = jnp.zeros(slot.shape, jnp.int32)
    for _, end in bounds[:-1]:
        image = image + (slot >= end).astype(jnp.int32)
    image = jnp.where(slot >= total, len(bounds) + slot, image)
    return jnp.where(slot < 0, -1, image)


def front_kernel(
    owners,
    local_count,
    counts_ref,
    labels_ref,
    time_ref,
    routes_ref,
    time_table_ref,
    label_table_ref,
    ada_ref,
    ada_bias_ref,
    cot_ref,
    mod_ref,
    cond_ref,
    act_ref,
    pos_ref,
    tgt_ref,
    gb_ref,
    rows_ref,
    stack,
    hot,
    lines,
):
    slots, width = cot_ref.shape
    experts = owners * local_count
    bounds = image_bounds(counts_ref)
    total = bounds[-1][1]

    label_count = label_table_ref.shape[0]
    time_count = time_table_ref.shape[0]
    row = iota((8, label_count), 0)
    wanted = jnp.full((8, label_count), -1, jnp.int32)
    for image in range(len(bounds)):
        wanted = jnp.where(row == image, labels_ref[0, image], wanted)
    label_hot = (iota((8, label_count), 1) == wanted).astype(F32).astype(BF16)
    time_hot = (iota((8, time_count), 1) == time_ref[0]).astype(F32).astype(BF16)
    condition = dot(label_hot, label_table_ref[...]) + dot(time_hot, time_table_ref[...])
    act = (condition / (1.0 + jnp.exp(-condition))).astype(BF16)
    mod = dot(act, ada_ref[...]) + ada_bias_ref[...]
    cond_ref[...] = condition
    act_ref[...] = act
    mod_ref[...] = mod
    stack_modulation(mod[:, 5 * width :], stack)

    first = routes_ref[0:1, :]
    second = routes_ref[1:2, :]
    expert = iota((experts, slots), 0)
    valid = iota((experts, slots), 1) < total
    hit_first = (first == expert) & valid
    hit_second = (second == expert) & valid
    picks = (hit_first | hit_second).astype(F32)
    earlier = (iota((128, 128), 0) < iota((128, 128), 1)).astype(F32).astype(BF16)
    carry = jnp.zeros((experts, 1), F32)
    parts = []
    for lane in range(0, slots, 128):
        part = picks[:, lane : lane + 128]
        parts.append(dot(part.astype(BF16), earlier) + carry)
        carry = carry + jnp.sum(part, axis=1, keepdims=True)
    place = jnp.concatenate(parts, axis=1)
    pos_ref[...] = jnp.where(picks > 0.0, place, -1.0)
    base = (expert % local_count) * owners + expert // local_count
    slot_of = (base * CAP).astype(F32) + place
    lines[...] = jnp.full(lines.shape, -1.0, F32)
    lines[0:1, :] = jnp.sum(jnp.where(hit_first, slot_of + 1.0, 0.0), axis=0, keepdims=True) - 1.0
    lines[1:2, :] = jnp.sum(jnp.where(hit_second, slot_of + 1.0, 0.0), axis=0, keepdims=True) - 1.0
    tgt_ref[...] = lines[...].T

    def gradient(i, carry):
        r = pl.ds(pl.multiple_of(i * TILE, TILE), TILE)
        gate = dot(member_block(bounds, i * TILE, TILE), stack[...])
        gb_ref[r, :] = (gate * cot_ref[r, :].astype(F32)).astype(BF16)
        return carry

    lax.fori_loop(0, slots // TILE, gradient, 0)
    row = iota((CAP, slots), 0).astype(F32)
    for j in range(experts):
        expert = (j % owners) * local_count + j // owners
        line = pos_ref[expert : expert + 1, :]
        hot[...] = (row == line).astype(F32).astype(BF16)
        rows_ref[j] = dot(hot[...], gb_ref[...]).astype(BF16)


def front(owners, counts, labels, times, routes, time_table, label_table, ada, ada_bias, cot, experts):
    slots, width = cot.shape
    return pl.pallas_call(
        functools.partial(front_kernel, owners, experts // owners),
        in_specs=[in_smem()] * 3 + [in_vmem()] * 6,
        out_specs=[in_vmem()] * 7,
        out_shape=[
            like((8, 6 * width), F32),
            like((8, width), F32),
            like((8, width), BF16),
            like((experts, slots), F32),
            like((slots, 128), F32),
            like((slots, width), BF16),
            like((experts, CAP, width), BF16),
        ],
        scratch_shapes=[
            pltpu.VMEM((128, width), BF16),
            pltpu.VMEM((CAP, slots), BF16),
            pltpu.VMEM((128, slots), F32),
        ],
        compiler_params=pltpu.CompilerParams(vmem_limit_bytes=VMEM_BYTES),
        name="front",
    )(counts, labels, times, routes, time_table, label_table, ada, ada_bias[None], cot)


def attention_kernel(
    owners,
    local_count,
    counts_ref,
    tokens_ref,
    mod_ref,
    qkv_w_ref,
    out_w_ref,
    out_b_ref,
    router_ref,
    routes_ref,
    pos_ref,
    qkv_ref,
    att_ref,
    lse_ref,
    hidden_ref,
    moe_ref,
    gates_ref,
    send_ref,
    stack,
    values_t,
    hot,
    lines,
    columns,
):
    slots, width = tokens_ref.shape
    experts = owners * local_count
    padded = qkv_ref.shape[0]
    bounds = image_bounds(counts_ref)
    stack_modulation(mod_ref[...], stack)
    scale = HDIM ** (-0.5)

    def part(member, index):
        return dot(member, stack[:, index * width : (index + 1) * width])

    qkv_ref[0:WINDOW, :] = jnp.zeros((WINDOW, 3 * width), BF16)
    qkv_ref[padded - WINDOW :, :] = jnp.zeros((WINDOW, 3 * width), BF16)

    def project(i, carry):
        r = pl.ds(pl.multiple_of(i * TILE, TILE), TILE)
        member = member_block(bounds, i * TILE, TILE)
        normed, _ = norm_rows(tokens_ref[r, :].astype(F32))
        mixed = (normed * (1.0 + part(member, 1)) + part(member, 0)).astype(BF16)
        to = pl.ds(pl.multiple_of(i * TILE + WINDOW, 64), TILE)
        qkv_ref[to, :] = dot(mixed, qkv_w_ref[...]).astype(BF16)
        return carry

    lax.fori_loop(0, slots // TILE, project, 0)
    for r in range(0, padded, BLOCK):
        values_t[:, r : r + BLOCK] = qkv_ref[r : r + BLOCK, 2 * width :].T

    first_half = iota((BLOCK, 128), 1) < HDIM

    def attend(i, carry):
        q_rows = pl.ds(pl.multiple_of(i * BLOCK + WINDOW, 64), BLOCK)
        k_rows = pl.ds(pl.multiple_of(i * BLOCK, BLOCK), SPAN)
        o_rows = pl.ds(pl.multiple_of(i * BLOCK, BLOCK), BLOCK)
        key_segment = segments(bounds, i * BLOCK - WINDOW + iota((SPAN, BLOCK), 0))
        query_segment = segments(bounds, i * BLOCK + iota((1, BLOCK), 1))
        allowed = key_segment == query_segment
        allowed = jnp.concatenate([allowed, allowed], axis=1)
        for pair in range(HEADS // 2):
            lanes = slice(pair * 128, (pair + 1) * 128)
            q = qkv_ref[q_rows, lanes]
            k = qkv_ref[k_rows, width + pair * 128 : width + (pair + 1) * 128]
            zero = jnp.zeros_like(q)
            q = jnp.concatenate(
                [jnp.where(first_half, q, zero), jnp.where(first_half, zero, q)], axis=0
            )
            scores = jnp.where(allowed, dot_t(k, q) * scale, MASK_FILL)
            top = jnp.max(scores, axis=0, keepdims=True)
            expo = jnp.exp(scores - top)
            total = jnp.sum(expo, axis=0, keepdims=True)
            out = dot(values_t[lanes, k_rows], expo.astype(BF16)) / total
            out = jnp.concatenate([out[:HDIM, :BLOCK], out[HDIM:, BLOCK:]], axis=0)
            att_ref[o_rows, lanes] = out.T.astype(BF16)
            log_total = top + jnp.log(total)
            lse_ref[2 * pair : 2 * pair + 1, o_rows] = log_total[:, :BLOCK]
            lse_ref[2 * pair + 1 : 2 * pair + 2, o_rows] = log_total[:, BLOCK:]
        return carry

    lax.fori_loop(0, slots // BLOCK, attend, 0)

    def mix(i, carry):
        r = pl.ds(pl.multiple_of(i * TILE, TILE), TILE)
        member = member_block(bounds, i * TILE, TILE)
        attn_out = dot(att_ref[r, :], out_w_ref[...]) + out_b_ref[...]
        hidden = tokens_ref[r, :].astype(F32) + part(member, 2) * attn_out
        hidden_ref[r, :] = hidden
        normed, _ = norm_rows(hidden)
        moe_ref[r, :] = (normed * (1.0 + part(member, 4)) + part(member, 3)).astype(BF16)
        return carry

    lax.fori_loop(0, slots // TILE, mix, 0)

    logits = dot_t(router_ref[...], moe_ref[...])
    expert = iota((experts, slots), 0)
    chosen = (routes_ref[0:1, :] == expert) | (routes_ref[1:2, :] == expert)
    top = jnp.max(jnp.where(chosen, logits, MASK_FILL), axis=0, keepdims=True)
    expo = jnp.where(chosen, jnp.exp(logits - top), 0.0)
    gates_ref[...] = expo / jnp.sum(expo, axis=0, keepdims=True)

    row = iota((CAP, slots), 0).astype(F32)
    lane = iota((CAP, 128), 1)
    table = jnp.zeros((CAP, 128), F32)
    for j in range(experts):
        expert = (j % owners) * local_count + j // owners
        match = row == pos_ref[expert : expert + 1, :]
        hot[...] = match.astype(F32).astype(BF16)
        gate = jnp.sum(
            jnp.where(match, gates_ref[expert : expert + 1, :], 0.0), axis=1, keepdims=True
        )
        table = jnp.where(lane == j, gate, table)
        send_ref[j, :CAP, :] = dot(hot[...], moe_ref[...]).astype(BF16)
    columns[...] = jnp.zeros_like(columns)
    columns[:CAP, :] = table
    lines[...] = columns[...].T
    for j in range(experts):
        send_ref[j, CAP:, :] = tail_rows(lines[j : j + 1, :], width)


def tail_rows(line, width):
    high = line.astype(BF16).astype(F32)
    row = iota((PAD, line.shape[1]), 0)
    tail = jnp.where(row == 0, high, jnp.where(row == 1, line - high, 0.0))
    rest = jnp.zeros((PAD, width - line.shape[1]), F32)
    return jnp.concatenate([tail, rest], axis=1).astype(BF16)


def attention(owners, counts, tokens, mod, qkv_weight, out_weight, out_bias, router, routes, pos):
    slots, width = tokens.shape
    experts = pos.shape[0]
    padded = slots + 2 * WINDOW
    return pl.pallas_call(
        functools.partial(attention_kernel, owners, experts // owners),
        in_specs=[in_smem()] + [in_vmem()] * 8,
        out_specs=[in_vmem()] * 7,
        out_shape=[
            like((padded, 3 * width), BF16),
            like((slots, width), BF16),
            like((8, slots), F32),
            like((slots, width), F32),
            like((slots, width), BF16),
            like((experts, slots), F32),
            like((experts, CAP + PAD, width), BF16),
        ],
        scratch_shapes=[
            pltpu.VMEM((128, 6 * width), BF16),
            pltpu.VMEM((width, padded), BF16),
            pltpu.VMEM((CAP, slots), BF16),
            pltpu.VMEM((128, 256), F32),
            pltpu.VMEM((256, 128), F32),
        ],
        compiler_params=pltpu.CompilerParams(vmem_limit_bytes=VMEM_BYTES),
        name="attention",
    )(counts, tokens, mod, qkv_weight, out_weight, out_bias[None], router, routes, pos)


def group_partner(owners, a, b, c):
    first = lax.rem(lax.axis_index("p1") + a, 2)
    second = lax.rem(lax.axis_index("p2") + b, 2)
    third = lax.rem(lax.axis_index("expert") + c, owners)
    device = (lax.axis_index("p0"), first, second, third)
    return device, (first * 2 + second) * owners + third


def group_offsets(owners):
    return [(a, b, c) for a in range(2) for b in range(2) for c in range(owners)]


def greet(devices):
    barrier = pltpu.get_barrier_semaphore()
    for device in devices:
        pl.semaphore_signal(barrier, inc=1, device_id=device, device_id_type=MESH)
    pl.semaphore_wait(barrier, len(devices))


def group_copy(owners, index, offsets, source, target, send_sems, recv_sems):
    device, place = group_partner(owners, *offsets)
    _, me = group_partner(owners, 0, 0, 0)
    return pltpu.make_async_remote_copy(
        src_ref=source.at[place],
        dst_ref=target.at[me],
        send_sem=send_sems.at[index],
        recv_sem=recv_sems.at[index],
        device_id=device,
        device_id_type=MESH,
    )


def gelu_parts(pre, grad):
    square = pre * pre
    th = jnp.tanh(pre * (GELU_C + (GELU_C * GELU_K) * square))
    half = 0.5 + 0.5 * th
    slope = half + (0.5 * pre) * (1.0 - th * th) * (GELU_C + (3 * GELU_C * GELU_K) * square)
    return (pre * half).astype(BF16), (grad * slope).astype(BF16)


def shared_kernel(
    owners,
    x_ref,
    g_ref,
    up_ref,
    bu_ref,
    dn_ref,
    bd_ref,
    rows_ref,
    y_ref,
    dx_ref,
    dup_ref,
    dbu_ref,
    ddn_ref,
    dbd_ref,
    owner_ref,
    xt,
    gt,
    send_sems,
    recv_sems,
    own_sem,
):
    net = pl.program_id(0)
    chunk = pl.program_id(1)
    rows, width = x_ref.shape
    offsets = group_offsets(owners)
    copies = [
        group_copy(owners, index, offset, rows_ref, owner_ref, send_sems, recv_sems)
        for index, offset in enumerate(offsets)
        if index
    ]
    _, me = group_partner(owners, 0, 0, 0)
    own = pltpu.make_async_copy(rows_ref.at[me], owner_ref.at[me], own_sem)

    @pl.when((net == 0) & (chunk == 0))
    def _():
        greet([group_partner(owners, *offset)[0] for offset in offsets[1:]])
        own.start()
        for copy in copies:
            copy.start()
        for r in range(0, rows, 256):
            xt[:width, r : r + 256] = x_ref[r : r + 256, :].T
            gt[:, r : r + 256] = g_ref[r : r + 256, :].T
        xt[width:, :] = jnp.ones((xt.shape[0] - width, rows), BF16)
        y_ref[...] = jnp.zeros_like(y_ref)
        dx_ref[...] = jnp.zeros_like(dx_ref)
        dbd_ref[...] = jnp.sum(g_ref[...].astype(F32), axis=0, keepdims=True)

    up = up_ref[0]
    dn = dn_ref[0]
    pre = dot(x_ref[...], up) + bu_ref[0]
    act, dpre = gelu_parts(pre, dot_t(g_ref[...], dn))
    y_ref[...] += dot(act, dn)
    dx_ref[...] += dot_t(dpre, up)
    dup = dot(xt[...], dpre)
    dup_ref[0] = dup[:width].astype(BF16)
    dbu_ref[0] = dup[width : width + 1]
    ddn_ref[0] = dot(gt[...], act).T.astype(BF16)

    @pl.when((net == pl.num_programs(0) - 1) & (chunk == pl.num_programs(1) - 1))
    def _():
        y_ref[...] += jnp.sum(bd_ref[...], axis=0)
        own.wait()
        for copy in copies:
            copy.wait()


def shared_nets(owners, x, g, up, bias_up, down, bias_down, rows_out, chunk=768):
    nets, width, hidden = up.shape
    rows = x.shape[0]
    count = rows_out.shape[0]

    def whole(shape):
        return pl.BlockSpec(shape, lambda n, h: (0,) * len(shape))

    return pl.pallas_call(
        functools.partial(shared_kernel, owners),
        grid=(nets, hidden // chunk),
        in_specs=[
            whole(x.shape),
            whole(g.shape),
            pl.BlockSpec((1, width, chunk), lambda n, h: (n, 0, h)),
            pl.BlockSpec((1, 1, chunk), lambda n, h: (n, 0, h)),
            pl.BlockSpec((1, chunk, width), lambda n, h: (n, h, 0)),
            whole((nets, 1, width)),
            anywhere(),
        ],
        out_specs=[
            whole((rows, width)),
            whole((rows, width)),
            pl.BlockSpec((1, width, chunk), lambda n, h: (n, 0, h)),
            pl.BlockSpec((1, 1, chunk), lambda n, h: (n, 0, h)),
            pl.BlockSpec((1, chunk, width), lambda n, h: (n, h, 0)),
            whole((1, width)),
            anywhere(),
        ],
        out_shape=[
            like((rows, width), F32),
            like((rows, width), F32),
            like((nets, width, hidden), BF16),
            like((nets, 1, hidden), F32),
            like((nets, hidden, width), BF16),
            like((1, width), F32),
            like(rows_out.shape, BF16),
        ],
        scratch_shapes=[
            pltpu.VMEM((width + 16, rows), BF16),
            pltpu.VMEM((width, rows), BF16),
            pltpu.SemaphoreType.DMA((count,)),
            pltpu.SemaphoreType.DMA((count,)),
            pltpu.SemaphoreType.DMA,
        ],
        compiler_params=pltpu.CompilerParams(
            vmem_limit_bytes=VMEM_BYTES, collective_id=1, has_side_effects=True
        ),
        name="shared_nets",
    )(x, g, up, bias_up[:, None, :], down, bias_down[:, None, :], rows_out)


def routed_kernel(
    owners,
    x_ref,
    g_ref,
    up_any,
    bu_ref,
    dn_any,
    bd_ref,
    y_ref,
    dup_ref,
    dbu_ref,
    ddn_ref,
    dbd_ref,
    back_ref,
    up,
    dn,
    xt,
    gt,
    acts,
    dpres,
    outgoing,
    lines,
    columns,
    load_sems,
    send_sems,
    recv_sems,
    own_sem,
):
    width, hidden = up.shape
    chunk = 768
    pick = lax.axis_index("p1") * 2 + lax.axis_index("p2")
    loads = [
        pltpu.make_async_copy(up_any.at[pick], up, load_sems.at[0]),
        pltpu.make_async_copy(dn_any.at[pick], dn, load_sems.at[1]),
    ]
    for load in loads:
        load.start()
    offsets = group_offsets(owners)
    places = [group_partner(owners, *offset)[1] for offset in offsets]
    greet([group_partner(owners, *offset)[0] for offset in offsets[1:]])
    copies = [
        group_copy(owners, index, offset, outgoing, back_ref, send_sems, recv_sems)
        if index
        else pltpu.make_async_copy(outgoing.at[places[0]], back_ref.at[places[0]], own_sem)
        for index, offset in enumerate(offsets)
    ]

    lines[...] = jnp.zeros_like(lines)
    for index, place in enumerate(places):
        tail = x_ref[place, CAP:, :256].astype(F32)
        lines[index : index + 1, :] = tail[0:1] + tail[1:2]
    columns[...] = lines[...].T
    gates = columns[:CAP, :]
    for load in loads:
        load.wait()
    bu = bu_ref[pick]
    bd = bd_ref[pick]
    lane = iota((CAP, 128), 1)
    group = owners
    size = group * CAP
    xt[width:, :] = jnp.ones((xt.shape[0] - width, xt.shape[1]), BF16)
    dbd = jnp.zeros((1, width), F32)
    for first in range(0, len(offsets), group):
        members = range(first, first + group)
        span = slice(first * CAP, first * CAP + size)
        x = jnp.concatenate([x_ref[places[k], :CAP, :] for k in members], axis=0)
        raw = [g_ref[places[k]].astype(F32) for k in members]
        g = jnp.concatenate([raw[k - first] * gates[:, k : k + 1] for k in members], axis=0)
        g = g.astype(BF16)
        dbd = dbd + jnp.sum(g.astype(F32), axis=0, keepdims=True)
        xt[:width, span] = x.T
        gt[:, span] = g.T
        y = jnp.zeros((size, width), F32)
        dx = jnp.zeros((size, width), F32)
        for h in range(0, hidden, chunk):
            pre = dot(x, up[:, h : h + chunk]) + bu[:, h : h + chunk]
            act, dpre = gelu_parts(pre, dot_t(g, dn[h : h + chunk, :]))
            acts[span, h : h + chunk] = act
            dpres[span, h : h + chunk] = dpre
            y = y + dot(act, dn[h : h + chunk, :])
            dx = dx + dot_t(dpre, up[:, h : h + chunk])
        table = jnp.zeros((CAP, 128), F32)
        for k in members:
            r = slice((k - first) * CAP, (k - first + 1) * CAP)
            res = (y[r] + bd).astype(BF16).astype(F32)
            y_ref[places[k]] = (res * gates[:, k : k + 1]).astype(BF16)
            inner = jnp.sum(res * raw[k - first], axis=1, keepdims=True)
            table = jnp.where(lane == k - first, inner, table)
            outgoing[places[k], :CAP, :] = dx[r].astype(BF16)
        columns[:CAP, :] = table
        lines[...] = columns[...].T
        for k in members:
            outgoing[places[k], CAP:, :] = tail_rows(lines[k - first : k - first + 1, :], width)
            copies[k].start()
    dbd_ref[...] = dbd
    for h in range(0, hidden, 512):
        dup = dot(xt[...], dpres[:, h : h + 512])
        dup_ref[:, h : h + 512] = dup[:width].astype(BF16)
        dbu_ref[:, h : h + 512] = dup[width : width + 1]
        ddn_ref[h : h + 512, :] = dot(gt[...], acts[:, h : h + 512]).T.astype(BF16)
    for copy in copies:
        copy.wait()


def routed_net(owners, x, g, up, bias_up, down, bias_down):
    count = x.shape[0]
    rows = count * CAP
    width, hidden = up.shape[1:]
    return pl.pallas_call(
        functools.partial(routed_kernel, owners),
        in_specs=[in_vmem(), in_vmem(), anywhere(), in_vmem(), anywhere(), in_vmem()],
        out_specs=[in_vmem()] * 5 + [anywhere()],
        out_shape=[
            like((count, CAP, width), BF16),
            like((width, hidden), BF16),
            like((1, hidden), F32),
            like((hidden, width), BF16),
            like((1, width), F32),
            like((count, CAP + PAD, width), BF16),
        ],
        scratch_shapes=[
            pltpu.VMEM((width, hidden), BF16),
            pltpu.VMEM((hidden, width), BF16),
            pltpu.VMEM((width + 16, rows), BF16),
            pltpu.VMEM((width, rows), BF16),
            pltpu.VMEM((rows, hidden), BF16),
            pltpu.VMEM((rows, hidden), BF16),
            pltpu.VMEM((count, CAP + PAD, width), BF16),
            pltpu.VMEM((128, 256), F32),
            pltpu.VMEM((256, 128), F32),
            pltpu.SemaphoreType.DMA((2,)),
            pltpu.SemaphoreType.DMA((count,)),
            pltpu.SemaphoreType.DMA((count,)),
            pltpu.SemaphoreType.DMA,
        ],
        compiler_params=pltpu.CompilerParams(
            vmem_limit_bytes=VMEM_BYTES, collective_id=2, has_side_effects=True
        ),
        name="routed_net",
    )(x, g, up, bias_up[:, None, :], down, bias_down[:, None, :])


def member_rows(bounds, first, rows):
    image = iota((16, rows), 0)
    slot = first + iota((16, rows), 1)
    low = jnp.zeros((16, rows), jnp.int32)
    high = jnp.zeros((16, rows), jnp.int32)
    for index, (start, end) in enumerate(bounds):
        low = jnp.where(image == index, start, low)
        high = jnp.where(image == index, end, high)
    return ((slot >= low) & (slot < high)).astype(F32).astype(BF16)


def backward_kernel(
    owners,
    local_count,
    counts_ref,
    labels_ref,
    time_ref,
    tokens_ref,
    cot_ref,
    mod_ref,
    cond_ref,
    act_ref,
    qkv_ref,
    att_ref,
    lse_ref,
    hidden_ref,
    moe_ref,
    gates_ref,
    tgt_ref,
    shared_ref,
    dmoe_ref,
    grads_ref,
    res_ref,
    qkv_w_ref,
    out_w_ref,
    out_b_ref,
    router_ref,
    ada_ref,
    layer_ref,
    dtok_ref,
    rms_ref,
    dqkv_w_ref,
    dout_w_ref,
    dout_b_ref,
    drouter_ref,
    note_ref,
    stack,
    hot,
    rows_ext,
    gate_cols,
    ghid,
    gatt,
    kt,
    dkeys,
    dvals,
    dqkv,
    turned,
    dlog,
    sums,
    lines,
    columns,
    router,
):
    slots, width = tokens_ref.shape
    experts = owners * local_count
    padded = qkv_ref.shape[0]
    blocks = slots // TILE
    bounds = image_bounds(counts_ref)
    total = bounds[-1][1]
    scale = HDIM ** (-0.5)
    stack_modulation(mod_ref[...], stack)
    sums[...] = jnp.zeros_like(sums)

    def part(member, index):
        return dot(member, stack[:, index * width : (index + 1) * width])

    def collect(turned_member, index, values):
        sums[:, index * width : (index + 1) * width] += dot(turned_member, values.astype(BF16))

    lines[...] = jnp.zeros_like(lines)
    for j in range(experts):
        tail = grads_ref[j, CAP:, :256].astype(F32)
        lines[j : j + 1, :] = tail[0:1] + tail[1:2]
    columns[...] = lines[...].T
    lane = iota((CAP, 128), 1)
    for j in range(experts):
        expert = (j % owners) * local_count + j // owners
        r = slice(j * CAP, (j + 1) * CAP)
        rows_ext[r, :width] = grads_ref[j, :CAP, :]
        inner = columns[:CAP, j : j + 1]
        high = inner.astype(BF16).astype(F32)
        spread_out = jnp.where(
            lane == expert, high, jnp.where(lane == experts + expert, inner - high, 0.0)
        )
        rows_ext[r, width:] = spread_out.astype(BF16)
    gate_cols[...] = jnp.zeros_like(gate_cols)
    gate_cols[:experts, :] = gates_ref[...]
    router[...] = jnp.zeros_like(router)
    router[:experts, :] = router_ref[...]

    def routing(i, carry):
        r = pl.ds(pl.multiple_of(i * TILE, TILE), TILE)
        first = tgt_ref[r, 0:1]
        second = tgt_ref[r, 1:2]
        slot = iota((TILE, hot.shape[1]), 1).astype(F32)
        hot[r, :] = ((slot == first) | (slot == second)).astype(F32).astype(BF16)
        back = dot(hot[r, :], rows_ext[...])
        inner = back[:, width : width + experts] + back[:, width + experts : width + 2 * experts]
        gates = gate_cols[:, r].T[:, :experts]
        grad = gates * (inner - jnp.sum(gates * inner, axis=1, keepdims=True))
        grad = jnp.concatenate([grad, jnp.zeros((TILE, 128 - experts), F32)], axis=1)
        grad = grad.astype(BF16)
        dlog[:, r] = grad.T
        gmoe = dmoe_ref[r, :] + back[:, :width] + dot(grad, router[...])
        member = member_block(bounds, i * TILE, TILE)
        turned_member = member_rows(bounds, i * TILE, TILE)
        normed, row_scale = norm_rows(hidden_ref[r, :])
        collect(turned_member, 3, gmoe)
        collect(turned_member, 4, gmoe * normed)
        grad_hidden = cot_ref[r, :].astype(F32) + norm_back(
            gmoe * (1.0 + part(member, 4)), normed, row_scale
        )
        ghid[r, :] = grad_hidden
        grad_attn = (part(member, 2) * grad_hidden).astype(BF16)
        attn_out = dot(att_ref[r, :], out_w_ref[...]) + out_b_ref[...]
        collect(turned_member, 2, grad_hidden * attn_out)
        to = pl.ds(pl.multiple_of(i * TILE, TILE), TILE)
        gatt[to, :] = dot_t(grad_attn, out_w_ref[...]).astype(BF16)
        dqkv[r, :width] = grad_attn
        turned[:, r] = att_ref[r, :].T
        return carry

    lax.fori_loop(0, blocks, routing, 0)
    drouter_ref[...] = dot(dlog[...], moe_ref[...])[:experts]
    dout_w_ref[...] = dot(turned[...], dqkv[:, :width])
    dout_b_ref[...] = jnp.sum(dqkv[:, :width].astype(F32), axis=0, keepdims=True)

    for r in range(0, padded, BLOCK):
        kt[:, r : r + BLOCK] = qkv_ref[r : r + BLOCK, width : 2 * width].T
    dkeys[...] = jnp.zeros_like(dkeys)
    dvals[...] = jnp.zeros_like(dvals)
    first_half = iota((BLOCK, 128), 1) < HDIM

    def split(pair_rows):
        zero = jnp.zeros_like(pair_rows)
        return jnp.concatenate(
            [jnp.where(first_half, pair_rows, zero), jnp.where(first_half, zero, pair_rows)],
            axis=0,
        )

    def attend(i, carry):
        q_rows = pl.ds(pl.multiple_of(i * BLOCK + WINDOW, 64), BLOCK)
        k_rows = pl.ds(pl.multiple_of(i * BLOCK, BLOCK), SPAN)
        o_rows = pl.ds(pl.multiple_of(i * BLOCK, BLOCK), BLOCK)
        key_segment = segments(bounds, i * BLOCK - WINDOW + iota((SPAN, BLOCK), 0))
        query_segment = segments(bounds, i * BLOCK + iota((1, BLOCK), 1))
        allowed = key_segment == query_segment
        allowed = jnp.concatenate([allowed, allowed], axis=1)
        for pair in range(HEADS // 2):
            lanes = slice(pair * 128, (pair + 1) * 128)
            q = split(qkv_ref[q_rows, lanes])
            out_grad = split(gatt[o_rows, lanes])
            k = qkv_ref[k_rows, width + pair * 128 : width + (pair + 1) * 128]
            v = qkv_ref[k_rows, 2 * width + pair * 128 : 2 * width + (pair + 1) * 128]
            log_total = jnp.concatenate(
                [lse_ref[2 * pair : 2 * pair + 1, o_rows], lse_ref[2 * pair + 1 : 2 * pair + 2, o_rows]],
                axis=1,
            )
            probs = jnp.exp(jnp.where(allowed, dot_t(k, q) * scale, MASK_FILL) - log_total)
            grad_probs = dot_t(v, out_grad)
            inner = jnp.sum(probs * grad_probs, axis=0, keepdims=True)
            grad_scores = (probs * (grad_probs - inner)).astype(BF16)
            dvals[k_rows, lanes] += dot(probs.astype(BF16), out_grad)
            dkeys[k_rows, lanes] += dot(grad_scores, q) * scale
            turned_query = dot(kt[lanes, k_rows], grad_scores) * scale
            turned_query = jnp.concatenate(
                [turned_query[:HDIM, :BLOCK], turned_query[HDIM:, BLOCK:]], axis=0
            )
            dqkv[o_rows, lanes] = turned_query.T.astype(BF16)
        return carry

    lax.fori_loop(0, slots // BLOCK, attend, 0)

    def finish(i, carry):
        r = pl.ds(pl.multiple_of(i * TILE, TILE), TILE)
        from_rows = pl.ds(pl.multiple_of(i * TILE + WINDOW, 64), TILE)
        dqkv[r, width : 2 * width] = dkeys[from_rows, :].astype(BF16)
        dqkv[r, 2 * width :] = dvals[from_rows, :].astype(BF16)
        member = member_block(bounds, i * TILE, TILE)
        turned_member = member_rows(bounds, i * TILE, TILE)
        gmix = dot_t(dqkv[r, :], qkv_w_ref[...])
        normed, row_scale = norm_rows(tokens_ref[r, :].astype(F32))
        gain = 1.0 + part(member, 1)
        turned[:, r] = (normed * gain + part(member, 0)).astype(BF16).T
        collect(turned_member, 0, gmix)
        collect(turned_member, 1, gmix * normed)
        dtok_ref[r, :] = ghid[r, :] + norm_back(gmix * gain, normed, row_scale)
        return carry

    lax.fori_loop(0, blocks, finish, 0)
    dqkv_w_ref[...] = dot(turned[...], dqkv[...])

    def result(i, carry):
        r = pl.ds(pl.multiple_of(i * TILE, TILE), TILE)
        member = member_block(bounds, i * TILE, TILE)
        branch = dot(hot[r, :], res_ref[...]) + shared_ref[r, :]
        layer = hidden_ref[r, :] + part(member, 5) * branch
        layer_ref[r, :] = layer.astype(BF16)
        valid = (i * TILE + iota((TILE, width), 0)) < total
        collect(member_rows(bounds, i * TILE, TILE), 5, cot_ref[r, :].astype(F32) * branch)
        one = jnp.sum(jnp.where(valid, layer * layer, 0.0), axis=0, keepdims=True)
        two = jnp.sum(jnp.where(valid, branch * branch, 0.0), axis=0, keepdims=True)
        return (carry[0] + one, carry[1] + two)

    zero = jnp.zeros((1, width), F32)
    one, two = lax.fori_loop(0, blocks, result, (zero, zero))
    count = jnp.full((1, 1), total * width, jnp.int32).astype(F32)
    one = jnp.sqrt(jnp.sum(one, axis=1, keepdims=True) / count)
    two = jnp.sqrt(jnp.sum(two, axis=1, keepdims=True) / count)
    rms_ref[...] = jnp.where(iota((1, 128), 1) == 0, one, two)

    grad_mod = sums[0:8, :]
    high, low = high_low(grad_mod)
    grad_act = dot_t(high, ada_ref[...]) + dot_t(low, ada_ref[...])
    condition = cond_ref[...]
    sigmoid = 1.0 / (1.0 + jnp.exp(-condition))
    grad_cond = grad_act * (sigmoid * (1.0 + condition * (1.0 - sigmoid)))
    row = iota((8, 128), 0)
    lane = iota((8, 128), 1)
    label = jnp.zeros((8, 128), jnp.int32)
    for image in range(len(bounds)):
        label = jnp.where(row == image, labels_ref[0, image], label)
    time = jnp.full((8, 128), time_ref[0], jnp.int32)
    pieces = [label // 32, label % 32, time // 32, time % 32]
    marks = jnp.zeros((8, 128), jnp.int32)
    for index, piece in enumerate(pieces):
        marks = jnp.where(lane == index, piece, marks)
    real = row < len(bounds)
    marks = jnp.where(real, marks, jnp.where(lane < 4, 255, 0)).astype(F32)
    keep = (iota((8, width), 0) < len(bounds)).astype(F32)
    note = jnp.concatenate(
        [grad_mod, grad_cond * keep, act_ref[...].astype(F32) * keep, marks], axis=1
    )
    note_ref[...] = jnp.concatenate([note, jnp.zeros_like(note)], axis=0).astype(BF16)


def backward(owners, *args):
    tokens, mod, qkv_pad, gates = args[3], args[5], args[8], args[13]
    slots, width = tokens.shape
    padded = qkv_pad.shape[0]
    experts = gates.shape[0]
    return pl.pallas_call(
        functools.partial(backward_kernel, owners, experts // owners),
        in_specs=[in_smem()] * 3 + [in_vmem()] * (len(args) - 3),
        out_specs=[in_vmem()] * 8,
        out_shape=[
            like((slots, width), BF16),
            like((slots, width), F32),
            like((1, 128), F32),
            like((width, 3 * width), F32),
            like((width, width), F32),
            like((1, width), F32),
            like((experts, width), F32),
            like((16, 8 * width + 128), BF16),
        ],
        scratch_shapes=[
            pltpu.VMEM((128, 6 * width), BF16),
            pltpu.VMEM((slots, experts * CAP), BF16),
            pltpu.VMEM((experts * CAP, width + 128), BF16),
            pltpu.VMEM((128, slots), F32),
            pltpu.VMEM((slots, width), F32),
            pltpu.VMEM((slots, width), BF16),
            pltpu.VMEM((width, padded), BF16),
            pltpu.VMEM((padded, width), F32),
            pltpu.VMEM((padded, width), F32),
            pltpu.VMEM((slots, 3 * width), BF16),
            pltpu.VMEM((width, slots), BF16),
            pltpu.VMEM((128, slots), BF16),
            pltpu.VMEM((16, 6 * width), F32),
            pltpu.VMEM((128, 256), F32),
            pltpu.VMEM((256, 128), F32),
            pltpu.VMEM((128, width), BF16),
        ],
        compiler_params=pltpu.CompilerParams(vmem_limit_bytes=VMEM_BYTES),
        name="backward",
    )(*args)


def exchange(blocks, axes):
    return lax.all_to_all(blocks, axes, split_axis=0, concat_axis=0, tiled=True)


def spread(block, axes):
    count = lax.axis_size(axes)
    return exchange(jnp.broadcast_to(block[None], (count,) + block.shape), axes)


def sum_blocks(blocks):
    return jnp.sum(blocks.astype(F32), axis=0)


def sum_everywhere(payload):
    rows, width = payload.shape
    near = ("p2", "expert")
    far = ("p0", "p1")
    near_count = lax.axis_size(near)
    far_count = lax.axis_size(far)
    piece = rows // near_count
    part = exchange(payload.astype(BF16).reshape(near_count, piece, width), near)
    part = sum_blocks(part).astype(BF16)
    part = part.reshape(piece, far_count, width // far_count).transpose(1, 0, 2)
    part = sum_blocks(exchange(part, far)).astype(BF16)
    part = spread(part, far).transpose(1, 0, 2).reshape(piece, width)
    return spread(part, near).reshape(rows, width)


def body(
    tokens,
    cotangent,
    patch_counts,
    time_buckets,
    image_labels,
    expert_routes,
    time_table,
    label_table,
    ada_weight,
    ada_bias,
    qkv_weight,
    out_weight,
    out_bias,
    router_weight,
    expert_up,
    expert_up_bias,
    expert_down,
    expert_down_bias,
    shared_up,
    shared_up_bias,
    shared_down,
    shared_down_bias,
):
    slot_count, width = tokens.shape
    expert_count = router_weight.shape[1]
    local_count, _, hidden = expert_up.shape
    owners = lax.axis_size("expert")
    dp_count = lax.axis_size(("p0", "p1", "p2"))
    outer = lax.axis_size("p0")
    routes = expert_routes[0].T
    router_turned = router_weight.T
    modulation, condition, cond_act, place, targets, grad_branch, branch_rows = front(
        owners,
        patch_counts,
        image_labels,
        time_buckets,
        routes,
        time_table,
        label_table,
        ada_weight,
        ada_bias,
        cotangent,
        expert_count,
    )
    owner_branch = exchange(branch_rows, GROUP)
    qkv_pad, attended_flat, log_totals, hidden_one, moe_in, gates_t, send_rows = attention(
        owners,
        patch_counts,
        tokens,
        modulation,
        qkv_weight,
        out_weight,
        out_bias,
        router_turned,
        routes,
        place,
    )
    (
        shared_total,
        grad_moe_in,
        grad_sup,
        grad_sup_bias,
        grad_sdown,
        grad_sdown_bias,
        owner_rows,
    ) = shared_nets(
        owners,
        moe_in,
        grad_branch,
        shared_up,
        shared_up_bias,
        shared_down,
        shared_down_bias,
        send_rows,
    )
    shared_payload = jnp.concatenate(
        [grad_sup.reshape(-1, hidden), grad_sdown.reshape(-1, hidden)], axis=0
    )
    shared_sums = sum_everywhere(shared_payload).astype(F32)
    owner_res, grad_eup, grad_eup_bias, grad_edown, grad_edown_bias, returned_grads = routed_net(
        owners,
        owner_rows,
        owner_branch,
        expert_up,
        expert_up_bias,
        expert_down,
        expert_down_bias,
    )
    returned = exchange(owner_res, GROUP).reshape(expert_count * CAP, width)

    up_blocks = exchange(grad_eup.reshape(outer, width // outer, hidden), "p0")
    up_part = sum_blocks(up_blocks).astype(BF16).reshape(-1, width // dp_count, hidden)
    sum_eup = exchange(up_part, ("p1", "p2")).astype(F32)
    side = jnp.concatenate(
        [grad_eup_bias.reshape(dp_count, -1), grad_edown_bias.reshape(dp_count, -1)], axis=1
    )
    side_width = side.shape[1]
    side = jnp.pad(side.astype(BF16)[:, None, :], ((0, 0), (0, PAD - 1), (0, width - side_width)))
    down_payload = jnp.concatenate(
        [grad_edown.reshape(dp_count, hidden // dp_count, width), side], axis=1
    )
    down_rows = down_payload.shape[1]
    down_blocks = exchange(down_payload.reshape(outer, -1, down_rows, width), "p0")
    down_part = exchange(sum_blocks(down_blocks).astype(BF16), ("p1", "p2")).astype(F32)
    sum_edown = down_part[:, : hidden // dp_count]
    side_sums = down_part[:, hidden // dp_count]
    sum_eup_bias = side_sums[:, : hidden // dp_count]
    sum_edown_bias = side_sums[:, hidden // dp_count : side_width]

    (
        layer_out,
        grad_tokens,
        rms_row,
        grad_qkv_weight,
        grad_out_weight,
        grad_out_bias,
        grad_router,
        note,
    ) = backward(
        owners,
        patch_counts,
        image_labels,
        time_buckets,
        tokens,
        cotangent,
        modulation,
        condition,
        cond_act,
        qkv_pad,
        attended_flat,
        log_totals,
        hidden_one,
        moe_in,
        gates_t,
        targets,
        shared_total,
        grad_moe_in,
        returned_grads,
        returned,
        qkv_weight,
        out_weight,
        out_bias[None],
        router_turned,
        ada_weight,
    )

    all_rows = spread(note[:8], ALL).reshape(-1, note.shape[1])
    all_modulation = all_rows[:, : 6 * width]
    all_condition = all_rows[:, 6 * width : 7 * width]
    all_cond_act = all_rows[:, 7 * width : 8 * width]
    marks = all_rows[:, 8 * width : 8 * width + 4].astype(jnp.int32)
    sum_ada = lax.dot_general(all_cond_act, all_modulation, ROWS_FIRST, preferred_element_type=F32)
    sum_ada_bias = jnp.sum(all_modulation.astype(F32), axis=0)
    label_ids = jnp.arange(label_table.shape[0], dtype=jnp.int32)
    label_hot = ((marks[:, 0:1] * 32 + marks[:, 1:2]) == label_ids).astype(BF16)
    sum_label = lax.dot_general(label_hot, all_condition, ROWS_FIRST, preferred_element_type=F32)
    time_ids = jnp.arange(time_table.shape[0], dtype=jnp.int32)
    time_hot = ((marks[:, 2:3] * 32 + marks[:, 3:4]) == time_ids).astype(BF16)
    sum_time = lax.dot_general(time_hot, all_condition, ROWS_FIRST, preferred_element_type=F32)

    tail = jnp.concatenate(
        [
            jnp.concatenate([grad_qkv_weight, grad_out_weight], axis=1),
            grad_router.reshape(-1, hidden),
            grad_sup_bias.reshape(-1, hidden),
            jnp.pad(
                jnp.concatenate([grad_out_bias, grad_sdown_bias], axis=1),
                ((0, 0), (0, hidden - 2 * width)),
            ),
        ],
        axis=0,
    )
    used = tail.shape[0]
    near_count = lax.axis_size(("p2", "expert"))
    tail = jnp.pad(tail, ((0, -used % (16 * near_count)), (0, 0)))
    tail = sum_everywhere(tail).astype(F32)
    router_rows = width * expert_count // hidden
    shared_count = shared_up.shape[0]
    sum_qkv = tail[:width, : 3 * width]
    sum_out_weight = tail[:width, 3 * width :]
    place = width + router_rows
    sum_router = tail[width:place].reshape(expert_count, width).T
    sum_sup_bias = tail[place : place + shared_count]
    sum_out_bias = tail[place + shared_count, :width]
    sum_sdown_bias = jnp.broadcast_to(
        tail[place + shared_count, width : 2 * width][None], (shared_count, width)
    )
    half = grad_sup.size // hidden
    sum_sup = shared_sums[:half].reshape(grad_sup.shape)
    sum_sdown = shared_sums[half:].reshape(grad_sdown.shape)
    return (
        layer_out,
        grad_tokens,
        rms_row[:, :2],
        sum_time,
        sum_label,
        sum_ada,
        sum_ada_bias,
        sum_qkv,
        sum_out_weight,
        sum_out_bias,
        sum_router,
        sum_eup,
        sum_eup_bias,
        sum_edown,
        sum_edown_bias,
        sum_sup,
        sum_sup_bias,
        sum_sdown,
        sum_sdown_bias,
    )


def solution(mesh):
    dp_count = mesh.shape["dp"]
    owners = mesh.shape["expert"]
    split = Mesh(mesh.devices.reshape(dp_count // 4, 2, 2, owners), ALL)
    dp = ("p0", "p1", "p2")
    in_specs = (
        P(ALL, None),
        P(ALL, None),
        P(ALL, None),
        P(ALL),
        P(ALL, None),
        P(ALL, None, None),
        P(),
        P(),
        P(),
        P(),
        P(),
        P(),
        P(),
        P(),
        P("expert", None, None),
        P("expert", None),
        P("expert", None, None),
        P("expert", None),
        P(),
        P(),
        P(),
        P(),
    )
    out_specs = (
        P(ALL, None),
        P(ALL, None),
        P(ALL, None),
        P(),
        P(),
        P(),
        P(),
        P(),
        P(),
        P(),
        P(),
        P("expert", dp, None),
        P("expert", dp),
        P("expert", dp, None),
        P("expert", dp),
        P(),
        P(),
        P(),
        P(),
    )
    return jax.shard_map(body, mesh=split, in_specs=in_specs, out_specs=out_specs, check_vma=False)
```

```python
import functools

import jax
import jax.numpy as jnp
from jax import lax
from jax.experimental import pallas as pl
from jax.experimental.pallas import tpu as pltpu
from jax.sharding import Mesh, PartitionSpec as P

HEADS = 6
HDIM = 64
CAP = 160
PAD = 16
WINDOW = 192
BLOCK = 128
SPAN = BLOCK + 2 * WINDOW
TILE = 256
NORM_EPS = 1e-06
MASK_FILL = -1e30
ROWS_FIRST = (((0,), (0,)), ((), ()))
ROWS_LAST = (((1,), (1,)), ((), ()))
GELU_C = 0.7978845608028654
GELU_K = 0.044715
ALL = ("p0", "p1", "p2", "expert")
GROUP = ("p1", "p2", "expert")
MESH = pl.DeviceIdType.MESH
F32 = jnp.float32
BF16 = jnp.bfloat16
VMEM_BYTES = 56 * 2**20


def norm_rows(matrix):
    row_mean = jnp.mean(matrix, axis=-1, keepdims=True)
    centred = matrix - row_mean
    row_var = jnp.mean(centred * centred, axis=-1, keepdims=True)
    row_scale = lax.rsqrt(row_var + NORM_EPS)
    return (centred * row_scale, row_scale)


def norm_back(grad_in, normed, row_scale):
    grad_mean = jnp.mean(grad_in, axis=-1, keepdims=True)
    cross_mean = jnp.mean(grad_in * normed, axis=-1, keepdims=True)
    return (grad_in - grad_mean - normed * cross_mean) * row_scale


def high_low(values):
    high = values.astype(BF16)
    return (high, (values - high.astype(F32)).astype(BF16))


def iota(shape, dim):
    return lax.broadcasted_iota(jnp.int32, shape, dim)


def dot(left, right):
    return jnp.dot(left, right, preferred_element_type=F32)


def dot_t(left, right):
    return lax.dot_general(left, right, ROWS_LAST, preferred_element_type=F32)


def in_vmem():
    return pl.BlockSpec(memory_space=pltpu.VMEM)


def in_smem():
    return pl.BlockSpec(memory_space=pltpu.SMEM)


def anywhere():
    return pl.BlockSpec(memory_space=pl.ANY)


def like(shape, dtype):
    return jax.ShapeDtypeStruct(shape, dtype)


def image_bounds(counts_ref):
    bounds = []
    start = 0
    for image in range(counts_ref.shape[1]):
        end = start + counts_ref[0, image]
        bounds.append((start, end))
        start = end
    return bounds


def member_block(bounds, first, rows):
    lane = iota((1, 128), 1)
    low = jnp.zeros((1, 128), jnp.int32)
    high = jnp.zeros((1, 128), jnp.int32)
    for image, (start, end) in enumerate(bounds):
        hit = (lane == image) | (lane == 8 + image)
        low = jnp.where(hit, start, low)
        high = jnp.where(hit, end, high)
    slot = first + iota((rows, 128), 0)
    return ((slot >= low) & (slot < high)).astype(F32).astype(BF16)


def stack_modulation(mod, stack):
    high, low = high_low(mod)
    stack[...] = jnp.zeros_like(stack)
    stack[0:16, :] = jnp.concatenate([high.astype(F32), low.astype(F32)], axis=0).astype(BF16)


def segments(bounds, slot):
    total = bounds[-1][1]
    image = jnp.zeros(slot.shape, jnp.int32)
    for _, end in bounds[:-1]:
        image = image + (slot >= end).astype(jnp.int32)
    image = jnp.where(slot >= total, len(bounds) + slot, image)
    return jnp.where(slot < 0, -1, image)


def front_kernel(
    owners,
    local_count,
    counts_ref,
    labels_ref,
    time_ref,
    routes_ref,
    time_table_ref,
    label_table_ref,
    ada_ref,
    ada_bias_ref,
    cot_ref,
    mod_ref,
    cond_ref,
    act_ref,
    pos_ref,
    tgt_ref,
    gb_ref,
    rows_ref,
    stack,
    hot,
    lines,
):
    slots, width = cot_ref.shape
    experts = owners * local_count
    bounds = image_bounds(counts_ref)
    total = bounds[-1][1]

    label_count = label_table_ref.shape[0]
    time_count = time_table_ref.shape[0]
    row = iota((8, label_count), 0)
    wanted = jnp.full((8, label_count), -1, jnp.int32)
    for image in range(len(bounds)):
        wanted = jnp.where(row == image, labels_ref[0, image], wanted)
    label_hot = (iota((8, label_count), 1) == wanted).astype(F32).astype(BF16)
    time_hot = (iota((8, time_count), 1) == time_ref[0]).astype(F32).astype(BF16)
    condition = dot(label_hot, label_table_ref[...]) + dot(time_hot, time_table_ref[...])
    act = (condition / (1.0 + jnp.exp(-condition))).astype(BF16)
    mod = dot(act, ada_ref[...]) + ada_bias_ref[...]
    cond_ref[...] = condition
    act_ref[...] = act
    mod_ref[...] = mod
    stack_modulation(mod[:, 5 * width :], stack)

    first = routes_ref[0:1, :]
    second = routes_ref[1:2, :]
    expert = iota((experts, slots), 0)
    valid = iota((experts, slots), 1) < total
    hit_first = (first == expert) & valid
    hit_second = (second == expert) & valid
    picks = (hit_first | hit_second).astype(F32)
    earlier = (iota((128, 128), 0) < iota((128, 128), 1)).astype(F32).astype(BF16)
    carry = jnp.zeros((experts, 1), F32)
    parts = []
    for lane in range(0, slots, 128):
        part = picks[:, lane : lane + 128]
        parts.append(dot(part.astype(BF16), earlier) + carry)
        carry = carry + jnp.sum(part, axis=1, keepdims=True)
    place = jnp.concatenate(parts, axis=1)
    pos_ref[...] = jnp.where(picks > 0.0, place, -1.0)
    base = (expert % local_count) * owners + expert // local_count
    slot_of = (base * CAP).astype(F32) + place
    lines[...] = jnp.full(lines.shape, -1.0, F32)
    lines[0:1, :] = jnp.sum(jnp.where(hit_first, slot_of + 1.0, 0.0), axis=0, keepdims=True) - 1.0
    lines[1:2, :] = jnp.sum(jnp.where(hit_second, slot_of + 1.0, 0.0), axis=0, keepdims=True) - 1.0
    tgt_ref[...] = lines[...].T

    def gradient(i, carry):
        r = pl.ds(pl.multiple_of(i * TILE, TILE), TILE)
        gate = dot(member_block(bounds, i * TILE, TILE), stack[...])
        gb_ref[r, :] = (gate * cot_ref[r, :].astype(F32)).astype(BF16)
        return carry

    lax.fori_loop(0, slots // TILE, gradient, 0)
    row = iota((CAP, slots), 0).astype(F32)
    for j in range(experts):
        expert = (j % owners) * local_count + j // owners
        line = pos_ref[expert : expert + 1, :]
        hot[...] = (row == line).astype(F32).astype(BF16)
        rows_ref[j] = dot(hot[...], gb_ref[...]).astype(BF16)


def front(owners, counts, labels, times, routes, time_table, label_table, ada, ada_bias, cot, experts):
    slots, width = cot.shape
    return pl.pallas_call(
        functools.partial(front_kernel, owners, experts // owners),
        in_specs=[in_smem()] * 3 + [in_vmem()] * 6,
        out_specs=[in_vmem()] * 7,
        out_shape=[
            like((8, 6 * width), F32),
            like((8, width), F32),
            like((8, width), BF16),
            like((experts, slots), F32),
            like((slots, 128), F32),
            like((slots, width), BF16),
            like((experts, CAP, width), BF16),
        ],
        scratch_shapes=[
            pltpu.VMEM((128, width), BF16),
            pltpu.VMEM((CAP, slots), BF16),
            pltpu.VMEM((128, slots), F32),
        ],
        compiler_params=pltpu.CompilerParams(vmem_limit_bytes=VMEM_BYTES),
        name="front",
    )(counts, labels, times, routes, time_table, label_table, ada, ada_bias[None], cot)


def attention_kernel(
    owners,
    local_count,
    counts_ref,
    tokens_ref,
    mod_ref,
    qkv_w_ref,
    out_w_ref,
    out_b_ref,
    router_ref,
    routes_ref,
    pos_ref,
    qkv_ref,
    att_ref,
    lse_ref,
    hidden_ref,
    moe_ref,
    gates_ref,
    send_ref,
    stack,
    values_t,
    hot,
    lines,
    columns,
):
    slots, width = tokens_ref.shape
    experts = owners * local_count
    padded = qkv_ref.shape[0]
    bounds = image_bounds(counts_ref)
    stack_modulation(mod_ref[...], stack)
    scale = HDIM ** (-0.5)

    def part(member, index):
        return dot(member, stack[:, index * width : (index + 1) * width])

    qkv_ref[0:WINDOW, :] = jnp.zeros((WINDOW, 3 * width), BF16)
    qkv_ref[padded - WINDOW :, :] = jnp.zeros((WINDOW, 3 * width), BF16)

    def project(i, carry):
        r = pl.ds(pl.multiple_of(i * TILE, TILE), TILE)
        member = member_block(bounds, i * TILE, TILE)
        normed, _ = norm_rows(tokens_ref[r, :].astype(F32))
        mixed = (normed * (1.0 + part(member, 1)) + part(member, 0)).astype(BF16)
        to = pl.ds(pl.multiple_of(i * TILE + WINDOW, 64), TILE)
        qkv_ref[to, :] = dot(mixed, qkv_w_ref[...]).astype(BF16)
        return carry

    lax.fori_loop(0, slots // TILE, project, 0)
    for r in range(0, padded, BLOCK):
        values_t[:, r : r + BLOCK] = qkv_ref[r : r + BLOCK, 2 * width :].T

    first_half = iota((BLOCK, 128), 1) < HDIM

    def attend(i, carry):
        q_rows = pl.ds(pl.multiple_of(i * BLOCK + WINDOW, 64), BLOCK)
        k_rows = pl.ds(pl.multiple_of(i * BLOCK, BLOCK), SPAN)
        o_rows = pl.ds(pl.multiple_of(i * BLOCK, BLOCK), BLOCK)
        key_segment = segments(bounds, i * BLOCK - WINDOW + iota((SPAN, BLOCK), 0))
        query_segment = segments(bounds, i * BLOCK + iota((1, BLOCK), 1))
        allowed = key_segment == query_segment
        allowed = jnp.concatenate([allowed, allowed], axis=1)
        for pair in range(HEADS // 2):
            lanes = slice(pair * 128, (pair + 1) * 128)
            q = qkv_ref[q_rows, lanes]
            k = qkv_ref[k_rows, width + pair * 128 : width + (pair + 1) * 128]
            zero = jnp.zeros_like(q)
            q = jnp.concatenate(
                [jnp.where(first_half, q, zero), jnp.where(first_half, zero, q)], axis=0
            )
            scores = jnp.where(allowed, dot_t(k, q) * scale, MASK_FILL)
            top = jnp.max(scores, axis=0, keepdims=True)
            expo = jnp.exp(scores - top)
            total = jnp.sum(expo, axis=0, keepdims=True)
            out = dot(values_t[lanes, k_rows], expo.astype(BF16)) / total
            out = jnp.concatenate([out[:HDIM, :BLOCK], out[HDIM:, BLOCK:]], axis=0)
            att_ref[o_rows, lanes] = out.T.astype(BF16)
            log_total = top + jnp.log(total)
            lse_ref[2 * pair : 2 * pair + 1, o_rows] = log_total[:, :BLOCK]
            lse_ref[2 * pair + 1 : 2 * pair + 2, o_rows] = log_total[:, BLOCK:]
        return carry

    lax.fori_loop(0, slots // BLOCK, attend, 0)

    def mix(i, carry):
        r = pl.ds(pl.multiple_of(i * TILE, TILE), TILE)
        member = member_block(bounds, i * TILE, TILE)
        attn_out = dot(att_ref[r, :], out_w_ref[...]) + out_b_ref[...]
        hidden = tokens_ref[r, :].astype(F32) + part(member, 2) * attn_out
        hidden_ref[r, :] = hidden
        normed, _ = norm_rows(hidden)
        moe_ref[r, :] = (normed * (1.0 + part(member, 4)) + part(member, 3)).astype(BF16)
        return carry

    lax.fori_loop(0, slots // TILE, mix, 0)

    logits = dot_t(router_ref[...], moe_ref[...])
    expert = iota((experts, slots), 0)
    chosen = (routes_ref[0:1, :] == expert) | (routes_ref[1:2, :] == expert)
    top = jnp.max(jnp.where(chosen, logits, MASK_FILL), axis=0, keepdims=True)
    expo = jnp.where(chosen, jnp.exp(logits - top), 0.0)
    gates_ref[...] = expo / jnp.sum(expo, axis=0, keepdims=True)

    row = iota((CAP, slots), 0).astype(F32)
    lane = iota((CAP, 128), 1)
    table = jnp.zeros((CAP, 128), F32)
    for j in range(experts):
        expert = (j % owners) * local_count + j // owners
        match = row == pos_ref[expert : expert + 1, :]
        hot[...] = match.astype(F32).astype(BF16)
        gate = jnp.sum(
            jnp.where(match, gates_ref[expert : expert + 1, :], 0.0), axis=1, keepdims=True
        )
        table = jnp.where(lane == j, gate, table)
        send_ref[j, :CAP, :] = dot(hot[...], moe_ref[...]).astype(BF16)
    columns[...] = jnp.zeros_like(columns)
    columns[:CAP, :] = table
    lines[...] = columns[...].T
    for j in range(experts):
        send_ref[j, CAP:, :] = tail_rows(lines[j : j + 1, :], width)


def tail_rows(line, width):
    high = line.astype(BF16).astype(F32)
    row = iota((PAD, line.shape[1]), 0)
    tail = jnp.where(row == 0, high, jnp.where(row == 1, line - high, 0.0))
    rest = jnp.zeros((PAD, width - line.shape[1]), F32)
    return jnp.concatenate([tail, rest], axis=1).astype(BF16)


def attention(owners, counts, tokens, mod, qkv_weight, out_weight, out_bias, router, routes, pos):
    slots, width = tokens.shape
    experts = pos.shape[0]
    padded = slots + 2 * WINDOW
    return pl.pallas_call(
        functools.partial(attention_kernel, owners, experts // owners),
        in_specs=[in_smem()] + [in_vmem()] * 8,
        out_specs=[in_vmem()] * 7,
        out_shape=[
            like((padded, 3 * width), BF16),
            like((slots, width), BF16),
            like((8, slots), F32),
            like((slots, width), F32),
            like((slots, width), BF16),
            like((experts, slots), F32),
            like((experts, CAP + PAD, width), BF16),
        ],
        scratch_shapes=[
            pltpu.VMEM((128, 6 * width), BF16),
            pltpu.VMEM((width, padded), BF16),
            pltpu.VMEM((CAP, slots), BF16),
            pltpu.VMEM((128, 256), F32),
            pltpu.VMEM((256, 128), F32),
        ],
        compiler_params=pltpu.CompilerParams(vmem_limit_bytes=VMEM_BYTES),
        name="attention",
    )(counts, tokens, mod, qkv_weight, out_weight, out_bias[None], router, routes, pos)


def axes_here():
    return [lax.axis_index(name) for name in ALL]


def group_partner(owners, a, b, c):
    zero, one, two, three = axes_here()
    first = lax.rem(one + a, 2)
    second = lax.rem(two + b, 2)
    third = lax.rem(three + c, owners)
    return (zero, first, second, third), (first * 2 + second) * owners + third


def group_offsets(owners):
    offsets = [(a, b, c) for a in range(2) for b in range(2) for c in range(owners)]
    return sorted(offsets, key=lambda o: -(o[0] + o[1] + (2 * o[2] >= owners)))


def sibling():
    zero, one, two, three = axes_here()
    odd = lax.rem(three, 2)
    return (zero, one, two, three + 1 - 2 * odd)


def plane_partner(b, h):
    zero, one, two, three = axes_here()
    odd = lax.rem(three, 2)
    second = lax.rem(two + b, 2)
    half = lax.rem(three // 2 + h, 2)
    return (zero, one, second, half * 2 + odd), second, half


def line_partner(a, b):
    zero, one, two, three = axes_here()
    first = lax.rem(zero + a, 2)
    second = lax.rem(one + b, 2)
    return (first, second, two, three), first * 2 + second


def owner_partner(a, b):
    zero, one, two, three = axes_here()
    first = lax.rem(one + a, 2)
    second = lax.rem(two + b, 2)
    return (zero, first, second, three), first * 2 + second


def column_partner(a, b, c):
    zero, one, two, three = axes_here()
    first = lax.rem(zero + a, 2)
    second = lax.rem(one + b, 2)
    third = lax.rem(two + c, 2)
    return (first, second, third, three), (first * 2 + second) * 2 + third


OTHERS = [(1, 1), (0, 1), (1, 0)]
COLUMN = [(1, 1, 1), (1, 1, 0), (1, 0, 1), (1, 0, 0), (0, 1, 1), (0, 1, 0), (0, 0, 1)]


def greet(devices):
    barrier = pltpu.get_barrier_semaphore()
    for device in devices:
        pl.semaphore_signal(barrier, inc=1, device_id=device, device_id_type=MESH)
    pl.semaphore_wait(barrier, len(devices))


def push(source, target, send_sem, recv_sem, device):
    copy = pltpu.make_async_remote_copy(
        src_ref=source,
        dst_ref=target,
        send_sem=send_sem,
        recv_sem=recv_sem,
        device_id=device,
        device_id_type=MESH,
    )
    copy.start()
    return copy


def finish_all(copies):
    for copy in copies:
        copy.wait()


def group_copy(owners, index, offsets, source, target, send_sems, recv_sems):
    device, place = group_partner(owners, *offsets)
    _, me = group_partner(owners, 0, 0, 0)
    return pltpu.make_async_remote_copy(
        src_ref=source.at[place],
        dst_ref=target.at[me],
        send_sem=send_sems.at[index],
        recv_sem=recv_sems.at[index],
        device_id=device,
        device_id_type=MESH,
    )


def gelu_parts(pre, grad):
    square = pre * pre
    th = jnp.tanh(pre * (GELU_C + (GELU_C * GELU_K) * square))
    half = 0.5 + 0.5 * th
    slope = half + (0.5 * pre) * (1.0 - th * th) * (GELU_C + (3 * GELU_C * GELU_K) * square)
    return (pre * half).astype(BF16), (grad * slope).astype(BF16)


def shared_kernel(
    owners,
    x_ref,
    g_ref,
    up_ref,
    bu_ref,
    dn_ref,
    bd_ref,
    rows_ref,
    y_ref,
    dx_ref,
    wire_ref,
    dbu_ref,
    dbd_ref,
    owner_ref,
    xt,
    gt,
    send_sems,
    recv_sems,
    own_sem,
):
    net = pl.program_id(0)
    chunk = pl.program_id(1)
    rows, width = x_ref.shape
    offsets = group_offsets(owners)
    copies = [
        group_copy(owners, index, offset, rows_ref, owner_ref, send_sems, recv_sems)
        for index, offset in enumerate(offsets)
        if any(offset)
    ]
    _, me = group_partner(owners, 0, 0, 0)
    own = pltpu.make_async_copy(rows_ref.at[me], owner_ref.at[me], own_sem)

    @pl.when((net == 0) & (chunk == 0))
    def _():
        greet([group_partner(owners, *offset)[0] for offset in offsets if any(offset)])
        own.start()
        for copy in copies:
            copy.start()
        for r in range(0, rows, 256):
            xt[:width, r : r + 256] = x_ref[r : r + 256, :].T
            gt[:, r : r + 256] = g_ref[r : r + 256, :].T
        xt[width:, :] = jnp.ones((xt.shape[0] - width, rows), BF16)
        y_ref[...] = jnp.zeros_like(y_ref)
        dx_ref[...] = jnp.zeros_like(dx_ref)
        dbd_ref[...] = jnp.sum(g_ref[...].astype(F32), axis=0, keepdims=True)

    up = up_ref[0]
    dn = dn_ref[0]
    pre = dot(x_ref[...], up) + bu_ref[0]
    act, dpre = gelu_parts(pre, dot_t(g_ref[...], dn))
    y_ref[...] += dot(act, dn)
    dx_ref[...] += dot_t(dpre, up)
    dup = dot(xt[...], dpre)
    wire_ref[0, 0] = dup[:width].astype(BF16)
    dbu_ref[0] = dup[width : width + 1]
    wire_ref[1, 0] = dot(gt[...], act).astype(BF16)

    @pl.when((net == pl.num_programs(0) - 1) & (chunk == pl.num_programs(1) - 1))
    def _():
        y_ref[...] += jnp.sum(bd_ref[...], axis=0)
        own.wait()
        for copy in copies:
            copy.wait()


def shared_nets(owners, x, g, up, bias_up, down, bias_down, rows_out, chunk=768):
    nets, width, hidden = up.shape
    rows = x.shape[0]
    count = rows_out.shape[0]

    def whole(shape):
        return pl.BlockSpec(shape, lambda n, h: (0,) * len(shape))

    return pl.pallas_call(
        functools.partial(shared_kernel, owners),
        grid=(nets, hidden // chunk),
        in_specs=[
            whole(x.shape),
            whole(g.shape),
            pl.BlockSpec((1, width, chunk), lambda n, h: (n, 0, h)),
            pl.BlockSpec((1, 1, chunk), lambda n, h: (n, 0, h)),
            pl.BlockSpec((1, chunk, width), lambda n, h: (n, h, 0)),
            whole((nets, 1, width)),
            anywhere(),
        ],
        out_specs=[
            whole((rows, width)),
            whole((rows, width)),
            pl.BlockSpec((2, 1, width, chunk), lambda n, h: (0, n, 0, h)),
            pl.BlockSpec((1, 1, chunk), lambda n, h: (n, 0, h)),
            whole((1, width)),
            anywhere(),
        ],
        out_shape=[
            like((rows, width), F32),
            like((rows, width), F32),
            like((2, nets, width, hidden), BF16),
            like((nets, 1, hidden), F32),
            like((1, width), F32),
            like(rows_out.shape, BF16),
        ],
        scratch_shapes=[
            pltpu.VMEM((width + 16, rows), BF16),
            pltpu.VMEM((width, rows), BF16),
            pltpu.SemaphoreType.DMA((count,)),
            pltpu.SemaphoreType.DMA((count,)),
            pltpu.SemaphoreType.DMA,
        ],
        compiler_params=pltpu.CompilerParams(
            vmem_limit_bytes=VMEM_BYTES, collective_id=1, has_side_effects=True
        ),
        name="shared_nets",
    )(x, g, up, bias_up[:, None, :], down, bias_down[:, None, :], rows_out)


def routed_kernel(
    owners,
    reduce,
    x_ref,
    g_ref,
    up_any,
    bu_ref,
    dn_any,
    bd_ref,
    wire_any,
    y_ref,
    dup_ref,
    ddn_ref,
    side_ref,
    back_ref,
    part_ref,
    rest_ref,
    up,
    dn,
    xt,
    gt,
    acts,
    dpres,
    outgoing,
    lines,
    columns,
    load_sems,
    send_sems,
    recv_sems,
    own_sem,
    keep,
    got,
    pieces,
    keep_sem,
    sum_sends,
    sum_recvs,
):
    width, hidden = up.shape
    chunk = 768
    pick = lax.axis_index("p1") * 2 + lax.axis_index("p2")
    loads = [
        pltpu.make_async_copy(up_any.at[pick], up, load_sems.at[0]),
        pltpu.make_async_copy(dn_any.at[pick], dn, load_sems.at[1]),
    ]
    for load in loads:
        load.start()
    offsets = group_offsets(owners)
    places = [group_partner(owners, *offset)[1] for offset in offsets]
    greet([group_partner(owners, *offset)[0] for offset in offsets if any(offset)])
    copies = [
        group_copy(owners, index, offset, outgoing, back_ref, send_sems, recv_sems)
        if any(offset)
        else pltpu.make_async_copy(outgoing.at[places[index]], back_ref.at[places[index]], own_sem)
        for index, offset in enumerate(offsets)
    ]
    sums = []
    if reduce:
        odd = lax.rem(lax.axis_index("expert"), 2)
        mine = pltpu.make_async_copy(wire_any.at[odd], keep, keep_sem)
        mine.start()
        swap = push(wire_any.at[1 - odd], got, sum_sends.at[3], sum_recvs.at[3], sibling())

    lines[...] = jnp.zeros_like(lines)
    for index, place in enumerate(places):
        tail = x_ref[place, CAP:, :256].astype(F32)
        lines[index : index + 1, :] = tail[0:1] + tail[1:2]
    columns[...] = lines[...].T
    gates = columns[:CAP, :]
    for load in loads:
        load.wait()
    bu = bu_ref[pick]
    bd = bd_ref[pick]
    lane = iota((CAP, 128), 1)
    group = owners
    size = group * CAP
    xt[width:, :] = jnp.ones((xt.shape[0] - width, xt.shape[1]), BF16)
    dbd = jnp.zeros((1, width), F32)
    for first in range(0, len(offsets), group):
        members = range(first, first + group)
        span = slice(first * CAP, first * CAP + size)
        x = jnp.concatenate([x_ref[places[k], :CAP, :] for k in members], axis=0)
        raw = [g_ref[places[k]].astype(F32) for k in members]
        g = jnp.concatenate([raw[k - first] * gates[:, k : k + 1] for k in members], axis=0)
        g = g.astype(BF16)
        dbd = dbd + jnp.sum(g.astype(F32), axis=0, keepdims=True)
        xt[:width, span] = x.T
        gt[:, span] = g.T
        y = jnp.zeros((size, width), F32)
        dx = jnp.zeros((size, width), F32)
        for h in range(0, hidden, chunk):
            pre = dot(x, up[:, h : h + chunk]) + bu[:, h : h + chunk]
            act, dpre = gelu_parts(pre, dot_t(g, dn[h : h + chunk, :]))
            acts[span, h : h + chunk] = act
            dpres[span, h : h + chunk] = dpre
            y = y + dot(act, dn[h : h + chunk, :])
            dx = dx + dot_t(dpre, up[:, h : h + chunk])
        table = jnp.zeros((CAP, 128), F32)
        for k in members:
            r = slice((k - first) * CAP, (k - first + 1) * CAP)
            res = (y[r] + bd).astype(BF16).astype(F32)
            y_ref[places[k]] = (res * gates[:, k : k + 1]).astype(BF16)
            inner = jnp.sum(res * raw[k - first], axis=1, keepdims=True)
            table = jnp.where(lane == k - first, inner, table)
            outgoing[places[k], :CAP, :] = dx[r].astype(BF16)
        columns[:CAP, :] = table
        lines[...] = columns[...].T
        for k in members:
            outgoing[places[k], CAP:, :] = tail_rows(lines[k - first : k - first + 1, :], width)
            copies[k].start()
        if reduce and first == 0:
            mine.wait()
            swap.wait()
            for net in range(keep.shape[0]):
                for r in range(0, width, 64):
                    rows = slice(r, r + 64)
                    total = keep[net, rows].astype(F32) + got[net, rows].astype(F32)
                    keep[net, rows] = total.astype(BF16)
            for index, (b, h) in enumerate(OTHERS):
                device, net, half = plane_partner(b, h)
                source = keep.at[net, pl.ds(half * (width // 2), width // 2), pl.ds(0, hidden // 2)]
                sums.append(
                    push(source, pieces.at[index], sum_sends.at[index], sum_recvs.at[index], device)
                )
    side_ref[...] = jnp.zeros_like(side_ref)
    side_ref[1:2, :width] = dbd
    for h in range(0, hidden, 512):
        dup = dot(xt[...], dpres[:, h : h + 512])
        dup_ref[:, h : h + 512] = dup[:width].astype(BF16)
        side_ref[0:1, h : h + 512] = dup[width : width + 1]
        ddn_ref[h : h + 512, :] = dot(gt[...], acts[:, h : h + 512]).T.astype(BF16)
    if reduce:
        finish_all(sums)
        _, net, half = plane_partner(0, 0)
        own = pl.ds(pl.multiple_of(half * (width // 2), 64), width // 2)
        total = keep[net, own, : hidden // 2].astype(F32)
        for index in range(len(OTHERS)):
            total = total + pieces[index].astype(F32)
        part_ref[...] = total.astype(BF16)
        rest_ref[...] = keep[:, :, hidden // 2 :]
    finish_all(copies)


def routed_net(owners, reduce, x, g, up, bias_up, down, bias_down, wire):
    count = x.shape[0]
    rows = count * CAP
    width, hidden = up.shape[1:]
    nets = wire.shape[1]
    half = (nets, width, hidden) if reduce else (1, 16, 128)
    piece = (width // 2, hidden // 2) if reduce else (16, 128)
    later = (nets, width, hidden // 2) if reduce else (1, 16, 128)
    return pl.pallas_call(
        functools.partial(routed_kernel, owners, reduce),
        in_specs=[in_vmem(), in_vmem(), anywhere(), in_vmem(), anywhere(), in_vmem(), anywhere()],
        out_specs=[in_vmem()] * 4 + [anywhere(), in_vmem(), in_vmem()],
        out_shape=[
            like((count, CAP, width), BF16),
            like((width, hidden), BF16),
            like((hidden, width), BF16),
            like((8, hidden), F32),
            like((count, CAP + PAD, width), BF16),
            like(piece, BF16),
            like(later, BF16),
        ],
        scratch_shapes=[
            pltpu.VMEM((width, hidden), BF16),
            pltpu.VMEM((hidden, width), BF16),
            pltpu.VMEM((width + 16, rows), BF16),
            pltpu.VMEM((width, rows), BF16),
            pltpu.VMEM((rows, hidden), BF16),
            pltpu.VMEM((rows, hidden), BF16),
            pltpu.VMEM((count, CAP + PAD, width), BF16),
            pltpu.VMEM((128, 256), F32),
            pltpu.VMEM((256, 128), F32),
            pltpu.SemaphoreType.DMA((2,)),
            pltpu.SemaphoreType.DMA((count,)),
            pltpu.SemaphoreType.DMA((count,)),
            pltpu.SemaphoreType.DMA,
            pltpu.VMEM(half, BF16),
            pltpu.VMEM(half, BF16),
            pltpu.VMEM((3,) + piece, BF16),
            pltpu.SemaphoreType.DMA,
            pltpu.SemaphoreType.DMA((4,)),
            pltpu.SemaphoreType.DMA((4,)),
        ],
        compiler_params=pltpu.CompilerParams(
            vmem_limit_bytes=VMEM_BYTES, collective_id=2, has_side_effects=True
        ),
        name="routed_net",
    )(x, g, up, bias_up[:, None, :], down, bias_down[:, None, :], wire)


def member_rows(bounds, first, rows):
    image = iota((16, rows), 0)
    slot = first + iota((16, rows), 1)
    low = jnp.zeros((16, rows), jnp.int32)
    high = jnp.zeros((16, rows), jnp.int32)
    for index, (start, end) in enumerate(bounds):
        low = jnp.where(image == index, start, low)
        high = jnp.where(image == index, end, high)
    return ((slot >= low) & (slot < high)).astype(F32).astype(BF16)


def backward_kernel(
    owners,
    local_count,
    reduce,
    counts_ref,
    labels_ref,
    time_ref,
    tokens_ref,
    cot_ref,
    mod_ref,
    cond_ref,
    qkv_ref,
    att_ref,
    lse_ref,
    hidden_ref,
    moe_ref,
    gates_ref,
    tgt_ref,
    shared_ref,
    dmoe_ref,
    grads_ref,
    res_ref,
    qkv_w_ref,
    out_w_ref,
    out_b_ref,
    router_ref,
    ada_ref,
    part_ref,
    later_ref,
    eup_any,
    layer_ref,
    dtok_ref,
    rms_ref,
    dqkv_w_ref,
    dout_w_ref,
    dout_b_ref,
    drouter_ref,
    note_ref,
    quarter_ref,
    next_ref,
    eup_ref,
    stack,
    hot,
    rows_ext,
    gate_cols,
    ghid,
    gatt,
    kt,
    dkeys,
    dvals,
    dqkv,
    turned,
    dlog,
    sums,
    lines,
    columns,
    router,
    res,
    send_sems,
    recv_sems,
    own_sem,
    zgot,
    zsum,
    pieces,
    zsends,
    zrecvs,
):
    slots, width = tokens_ref.shape
    experts = owners * local_count
    padded = qkv_ref.shape[0]
    blocks = slots // TILE
    offsets = group_offsets(owners)
    near = [group_partner(owners, *offset)[0] for offset in offsets if any(offset)]
    if reduce:
        near = near + [line_partner(1, 1)[0], line_partner(1, 0)[0]]
    greet(near)
    line_rows = zsum.shape[0]
    line_sums = []
    later = []
    if reduce:
        zero = lax.axis_index("p0")
        for index, offset in enumerate(OTHERS):
            device, place = line_partner(*offset)
            source = part_ref.at[pl.ds(place * line_rows, line_rows)]
            line_sums.append(
                push(source, zgot.at[index], zsends.at[index], zrecvs.at[index], device)
            )
    _, me = group_partner(owners, 0, 0, 0)
    own = pltpu.make_async_copy(res_ref.at[me], res.at[me], own_sem)
    own.start()
    copies = [
        group_copy(owners, index, offset, res_ref, res, send_sems, recv_sems)
        for index, offset in enumerate(offsets)
        if any(offset)
    ]
    for copy in copies:
        copy.start()
    if reduce:
        eup_rows = eup_ref.shape[0]
        later.append(
            push(
                eup_any.at[pl.ds((1 - zero) * eup_rows, eup_rows)],
                eup_ref,
                zsends.at[6],
                zrecvs.at[6],
                line_partner(1, 0)[0],
            )
        )
        half_rows = next_ref.shape[0]
        for index, offset in enumerate(OTHERS):
            device, net, half = plane_partner(*offset)
            source = later_ref.at[net, pl.ds(half * half_rows, half_rows)]
            later.append(
                push(source, pieces.at[index], zsends.at[7 + index], zrecvs.at[7 + index], device)
            )
    bounds = image_bounds(counts_ref)
    total = bounds[-1][1]
    scale = HDIM ** (-0.5)
    stack_modulation(mod_ref[...], stack)
    sums[...] = jnp.zeros_like(sums)

    def part(member, index):
        return dot(member, stack[:, index * width : (index + 1) * width])

    def collect(turned_member, index, values):
        sums[:, index * width : (index + 1) * width] += dot(turned_member, values.astype(BF16))

    lines[...] = jnp.zeros_like(lines)
    for j in range(experts):
        tail = grads_ref[j, CAP:, :256].astype(F32)
        lines[j : j + 1, :] = tail[0:1] + tail[1:2]
    columns[...] = lines[...].T
    lane = iota((CAP, 128), 1)
    for j in range(experts):
        expert = (j % owners) * local_count + j // owners
        r = slice(j * CAP, (j + 1) * CAP)
        rows_ext[r, :width] = grads_ref[j, :CAP, :]
        inner = columns[:CAP, j : j + 1]
        high = inner.astype(BF16).astype(F32)
        spread_out = jnp.where(
            lane == expert, high, jnp.where(lane == experts + expert, inner - high, 0.0)
        )
        rows_ext[r, width:] = spread_out.astype(BF16)
    gate_cols[...] = jnp.zeros_like(gate_cols)
    gate_cols[:experts, :] = gates_ref[...]
    router[...] = jnp.zeros_like(router)
    router[:experts, :] = router_ref[...]

    def routing(i, carry):
        r = pl.ds(pl.multiple_of(i * TILE, TILE), TILE)
        first = tgt_ref[r, 0:1]
        second = tgt_ref[r, 1:2]
        slot = iota((TILE, hot.shape[1]), 1).astype(F32)
        hot[r, :] = ((slot == first) | (slot == second)).astype(F32).astype(BF16)
        back = dot(hot[r, :], rows_ext[...])
        inner = back[:, width : width + experts] + back[:, width + experts : width + 2 * experts]
        gates = gate_cols[:, r].T[:, :experts]
        grad = gates * (inner - jnp.sum(gates * inner, axis=1, keepdims=True))
        grad = jnp.concatenate([grad, jnp.zeros((TILE, 128 - experts), F32)], axis=1)
        grad = grad.astype(BF16)
        dlog[:, r] = grad.T
        gmoe = dmoe_ref[r, :] + back[:, :width] + dot(grad, router[...])
        member = member_block(bounds, i * TILE, TILE)
        turned_member = member_rows(bounds, i * TILE, TILE)
        normed, row_scale = norm_rows(hidden_ref[r, :])
        collect(turned_member, 3, gmoe)
        collect(turned_member, 4, gmoe * normed)
        grad_hidden = cot_ref[r, :].astype(F32) + norm_back(
            gmoe * (1.0 + part(member, 4)), normed, row_scale
        )
        ghid[r, :] = grad_hidden
        grad_attn = (part(member, 2) * grad_hidden).astype(BF16)
        attn_out = dot(att_ref[r, :], out_w_ref[...]) + out_b_ref[...]
        collect(turned_member, 2, grad_hidden * attn_out)
        to = pl.ds(pl.multiple_of(i * TILE, TILE), TILE)
        gatt[to, :] = dot_t(grad_attn, out_w_ref[...]).astype(BF16)
        dqkv[r, :width] = grad_attn
        turned[:, r] = att_ref[r, :].T
        return carry

    lax.fori_loop(0, blocks, routing, 0)
    line_all = []
    if reduce:
        finish_all(line_sums)
        _, place = line_partner(0, 0)
        here = pl.ds(pl.multiple_of(place * line_rows, 16), line_rows)
        summed = part_ref[here].astype(F32)
        for index in range(len(OTHERS)):
            summed = summed + zgot[index].astype(F32)
        zsum[...] = summed.astype(BF16)
        quarter_ref[here] = zsum[...]
        target = quarter_ref.at[pl.ds(place * line_rows, line_rows)]
        for index, offset in enumerate(OTHERS):
            device, _ = line_partner(*offset)
            line_all.append(
                push(zsum, target, zsends.at[3 + index], zrecvs.at[3 + index], device)
            )
    drouter_ref[...] = dot(dlog[...], moe_ref[...])[:experts]
    dout_w_ref[...] = dot(turned[...], dqkv[:, :width])
    dout_b_ref[...] = jnp.sum(dqkv[:, :width].astype(F32), axis=0, keepdims=True)

    for r in range(0, padded, BLOCK):
        kt[:, r : r + BLOCK] = qkv_ref[r : r + BLOCK, width : 2 * width].T
    dkeys[...] = jnp.zeros_like(dkeys)
    dvals[...] = jnp.zeros_like(dvals)
    first_half = iota((BLOCK, 128), 1) < HDIM

    def split(pair_rows):
        zero = jnp.zeros_like(pair_rows)
        return jnp.concatenate(
            [jnp.where(first_half, pair_rows, zero), jnp.where(first_half, zero, pair_rows)],
            axis=0,
        )

    def attend(i, carry):
        q_rows = pl.ds(pl.multiple_of(i * BLOCK + WINDOW, 64), BLOCK)
        k_rows = pl.ds(pl.multiple_of(i * BLOCK, BLOCK), SPAN)
        o_rows = pl.ds(pl.multiple_of(i * BLOCK, BLOCK), BLOCK)
        key_segment = segments(bounds, i * BLOCK - WINDOW + iota((SPAN, BLOCK), 0))
        query_segment = segments(bounds, i * BLOCK + iota((1, BLOCK), 1))
        allowed = key_segment == query_segment
        allowed = jnp.concatenate([allowed, allowed], axis=1)
        for pair in range(HEADS // 2):
            lanes = slice(pair * 128, (pair + 1) * 128)
            q = split(qkv_ref[q_rows, lanes])
            out_grad = split(gatt[o_rows, lanes])
            k = qkv_ref[k_rows, width + pair * 128 : width + (pair + 1) * 128]
            v = qkv_ref[k_rows, 2 * width + pair * 128 : 2 * width + (pair + 1) * 128]
            log_total = jnp.concatenate(
                [lse_ref[2 * pair : 2 * pair + 1, o_rows], lse_ref[2 * pair + 1 : 2 * pair + 2, o_rows]],
                axis=1,
            )
            probs = jnp.exp(jnp.where(allowed, dot_t(k, q) * scale, MASK_FILL) - log_total)
            grad_probs = dot_t(v, out_grad)
            inner = jnp.sum(probs * grad_probs, axis=0, keepdims=True)
            grad_scores = (probs * (grad_probs - inner)).astype(BF16)
            dvals[k_rows, lanes] += dot(probs.astype(BF16), out_grad)
            dkeys[k_rows, lanes] += dot(grad_scores, q) * scale
            turned_query = dot(kt[lanes, k_rows], grad_scores) * scale
            turned_query = jnp.concatenate(
                [turned_query[:HDIM, :BLOCK], turned_query[HDIM:, BLOCK:]], axis=0
            )
            dqkv[o_rows, lanes] = turned_query.T.astype(BF16)
        return carry

    lax.fori_loop(0, slots // BLOCK, attend, 0)

    def finish(i, carry):
        r = pl.ds(pl.multiple_of(i * TILE, TILE), TILE)
        from_rows = pl.ds(pl.multiple_of(i * TILE + WINDOW, 64), TILE)
        dqkv[r, width : 2 * width] = dkeys[from_rows, :].astype(BF16)
        dqkv[r, 2 * width :] = dvals[from_rows, :].astype(BF16)
        member = member_block(bounds, i * TILE, TILE)
        turned_member = member_rows(bounds, i * TILE, TILE)
        gmix = dot_t(dqkv[r, :], qkv_w_ref[...])
        normed, row_scale = norm_rows(tokens_ref[r, :].astype(F32))
        gain = 1.0 + part(member, 1)
        turned[:, r] = (normed * gain + part(member, 0)).astype(BF16).T
        collect(turned_member, 0, gmix)
        collect(turned_member, 1, gmix * normed)
        dtok_ref[r, :] = ghid[r, :] + norm_back(gmix * gain, normed, row_scale)
        return carry

    lax.fori_loop(0, blocks, finish, 0)
    dqkv_w_ref[...] = dot(turned[...], dqkv[...])

    own.wait()
    finish_all(copies)
    for j in range(experts):
        rows_ext[j * CAP : (j + 1) * CAP, :width] = res[j]

    def result(i, carry):
        r = pl.ds(pl.multiple_of(i * TILE, TILE), TILE)
        member = member_block(bounds, i * TILE, TILE)
        branch = dot(hot[r, :], rows_ext[:, :width]) + shared_ref[r, :]
        layer = hidden_ref[r, :] + part(member, 5) * branch
        layer_ref[r, :] = layer.astype(BF16)
        valid = (i * TILE + iota((TILE, width), 0)) < total
        collect(member_rows(bounds, i * TILE, TILE), 5, cot_ref[r, :].astype(F32) * branch)
        one = jnp.sum(jnp.where(valid, layer * layer, 0.0), axis=0, keepdims=True)
        two = jnp.sum(jnp.where(valid, branch * branch, 0.0), axis=0, keepdims=True)
        return (carry[0] + one, carry[1] + two)

    zero = jnp.zeros((1, width), F32)
    one, two = lax.fori_loop(0, blocks, result, (zero, zero))
    count = jnp.full((1, 1), total * width, jnp.int32).astype(F32)
    one = jnp.sqrt(jnp.sum(one, axis=1, keepdims=True) / count)
    two = jnp.sqrt(jnp.sum(two, axis=1, keepdims=True) / count)
    rms_ref[...] = jnp.where(iota((1, 128), 1) == 0, one, two)

    grad_mod = sums[0:8, :]
    high, low = high_low(grad_mod)
    grad_act = dot_t(high, ada_ref[...]) + dot_t(low, ada_ref[...])
    condition = cond_ref[...]
    sigmoid = 1.0 / (1.0 + jnp.exp(-condition))
    grad_cond = grad_act * (sigmoid * (1.0 + condition * (1.0 - sigmoid)))
    row = iota((8, 128), 0)
    lane = iota((8, 128), 1)
    label = jnp.zeros((8, 128), jnp.int32)
    for image in range(len(bounds)):
        label = jnp.where(row == image, labels_ref[0, image], label)
    time = jnp.full((8, 128), time_ref[0], jnp.int32)
    digits = [label // 32, label % 32, time // 32, time % 32]
    marks = jnp.zeros((8, 128), jnp.int32)
    for index, piece in enumerate(digits):
        marks = jnp.where(lane == index, piece, marks)
    real = row < len(bounds)
    marks = jnp.where(real, marks, jnp.where(lane < 4, 255, 0)).astype(F32)
    keep = (iota((8, width), 0) < len(bounds)).astype(F32)
    note = jnp.concatenate([grad_mod, grad_cond * keep, marks], axis=1)
    middle = note.shape[1] // 2
    note_ref[...] = jnp.concatenate([note[:, :middle], note[:, middle:]], axis=0).astype(BF16)
    finish_all(line_all)
    finish_all(later)
    if reduce:
        _, net, half = plane_partner(0, 0)
        own_rows = pl.ds(pl.multiple_of(half * half_rows, 64), half_rows)
        summed = later_ref[net, own_rows].astype(F32)
        for index in range(len(OTHERS)):
            summed = summed + pieces[index].astype(F32)
        next_ref[...] = summed.astype(BF16)


def backward(owners, reduce, *args):
    tokens, mod, qkv_pad, gates, res, part = (args[k] for k in (3, 5, 7, 12, 17, 23))
    slots, width = tokens.shape
    padded = qkv_pad.shape[0]
    experts = gates.shape[0]
    quarter = part.shape
    sub = (quarter[0] // 4, quarter[1]) if reduce else (16, 128)
    in_specs = [in_smem()] * 3 + [in_vmem()] * (len(args) - 3)
    in_specs[17] = anywhere()
    in_specs[25] = anywhere()
    eup = (args[25].shape[0] // 2, args[25].shape[1]) if reduce else (16, 128)
    return pl.pallas_call(
        functools.partial(backward_kernel, owners, experts // owners, reduce),
        in_specs=in_specs,
        out_specs=[in_vmem()] * 11,
        out_shape=[
            like((slots, width), BF16),
            like((slots, width), F32),
            like((1, 128), F32),
            like((width, 3 * width), F32),
            like((width, width), F32),
            like((1, width), F32),
            like((experts, width), F32),
            like((16, (7 * width + 128) // 2), BF16),
            like(quarter, BF16),
            like(quarter, BF16),
            like(eup, BF16),
        ],
        scratch_shapes=[
            pltpu.VMEM((128, 6 * width), BF16),
            pltpu.VMEM((slots, experts * CAP), BF16),
            pltpu.VMEM((experts * CAP, width + 128), BF16),
            pltpu.VMEM((128, slots), F32),
            pltpu.VMEM((slots, width), F32),
            pltpu.VMEM((slots, width), BF16),
            pltpu.VMEM((width, padded), BF16),
            pltpu.VMEM((padded, width), F32),
            pltpu.VMEM((padded, width), F32),
            pltpu.VMEM((slots, 3 * width), BF16),
            pltpu.VMEM((width, slots), BF16),
            pltpu.VMEM((128, slots), BF16),
            pltpu.VMEM((16, 6 * width), F32),
            pltpu.VMEM((128, 256), F32),
            pltpu.VMEM((256, 128), F32),
            pltpu.VMEM((128, width), BF16),
            pltpu.VMEM((experts, CAP, width), BF16),
            pltpu.SemaphoreType.DMA((experts,)),
            pltpu.SemaphoreType.DMA((experts,)),
            pltpu.SemaphoreType.DMA,
            pltpu.VMEM((3,) + sub, BF16),
            pltpu.VMEM(sub, BF16),
            pltpu.VMEM((3,) + quarter, BF16),
            pltpu.SemaphoreType.DMA((10,)),
            pltpu.SemaphoreType.DMA((10,)),
        ],
        compiler_params=pltpu.CompilerParams(
            vmem_limit_bytes=VMEM_BYTES, collective_id=3, has_side_effects=True
        ),
        name="backward",
    )(*args)


def tail_kernel(
    dqkv_w_ref,
    dout_w_ref,
    drouter_ref,
    dout_b_ref,
    sup_b_ref,
    sdn_b_ref,
    quarter_ref,
    part_ref,
    note_ref,
    side_ref,
    eup_got_ref,
    eup_any,
    edn_any,
    full_a,
    full_b,
    done,
    notes,
    up_got,
    dn_got,
    sides,
    load,
    keep,
    got,
    pieces,
    zslots,
    zgot,
    zsum,
    quarter_b,
    up_sum,
    up_mine,
    dn_sum,
    dn_mine,
    side,
    sends,
    recvs,
    locals_,
):
    zero, one, two, three = axes_here()
    odd = lax.rem(three, 2)
    width = dout_w_ref.shape[0]
    rows, hidden = load.shape[1], 2 * load.shape[2]
    lanes = hidden // 2
    quarter_rows = rows // 2
    quarter_lanes = lanes // 2
    _, _, half_here = plane_partner(0, 0)
    _, line_here = line_partner(0, 0)
    _, owner_here = owner_partner(0, 0)
    _, column_here = column_partner(0, 0, 0)
    counter = iter(range(sends.shape[0]))

    def give(source, target, device):
        index = next(counter)
        return push(source, target, sends.at[index], recvs.at[index], device)

    up_rows = up_sum.shape[0]
    dn_rows = dn_sum.shape[0]
    half_rows = quarter_ref.shape[0]
    shared_rows = pl.ds(half_here * half_rows, half_rows)
    loads = [
        pltpu.make_async_copy(eup_any.at[pl.ds(zero * up_rows, up_rows)], up_mine, locals_.at[0]),
        pltpu.make_async_copy(edn_any.at[pl.ds(zero * dn_rows, dn_rows)], dn_mine, locals_.at[1]),
        pltpu.make_async_copy(quarter_ref, full_a.at[odd, two, shared_rows], locals_.at[2]),
    ]
    for copy in loads:
        copy.start()

    top = jnp.concatenate([dqkv_w_ref[...], dout_w_ref[...]], axis=1).astype(BF16)
    router = drouter_ref[...]
    router = jnp.concatenate(
        [router, jnp.zeros((router.shape[0], hidden - width), F32)], axis=1
    )
    vectors = jnp.concatenate(
        [dout_b_ref[...], sdn_b_ref[...], jnp.zeros((1, hidden - 2 * width), F32)], axis=1
    )
    nets = sup_b_ref.shape[0]
    filler = jnp.zeros((rows - width - router.shape[0] - nets - 1, hidden), F32)
    bottom = jnp.concatenate(
        [router] + [sup_b_ref[n] for n in range(nets)] + [vectors, filler], axis=0
    ).astype(BF16)
    for part in range(2):
        load[part, :width] = top[:, part * lanes : (part + 1) * lanes]
        load[part, width:] = bottom[:, part * lanes : (part + 1) * lanes]
    side[...] = jnp.concatenate([side_ref[...], jnp.zeros_like(side_ref)], axis=0).astype(BF16)

    greet(
        [column_partner(*offset)[0] for offset in COLUMN]
        + [sibling(), plane_partner(0, 1)[0], plane_partner(1, 1)[0]]
    )
    swap = give(load.at[1 - odd], got, sibling())
    note_line = [
        give(note_ref, notes.at[odd, two, half_here, line_here], line_partner(*o)[0]) for o in OTHERS
    ]
    notes[odd, two, half_here, line_here] = note_ref[...]
    line_rows = zsum.shape[0]
    shared_line = []
    for index, offset in enumerate(OTHERS):
        device, place = line_partner(*offset)
        source = part_ref.at[pl.ds(place * line_rows, line_rows)]
        shared_line.append(give(source, zgot.at[index], device))

    swap.wait()
    keep[...] = (load[odd].astype(F32) + got[...].astype(F32)).astype(BF16)
    plane_sums = []
    for index, offset in enumerate(OTHERS):
        device, second, half = plane_partner(*offset)
        source = keep.at[
            pl.ds(second * quarter_rows, quarter_rows),
            pl.ds(pl.multiple_of(half * quarter_lanes, 128), quarter_lanes),
        ]
        plane_sums.append(give(source, pieces.at[index], device))

    finish_all(shared_line)
    here = pl.ds(pl.multiple_of(line_here * line_rows, 16), line_rows)
    total = part_ref[here].astype(F32)
    for index in range(len(OTHERS)):
        total = total + zgot[index].astype(F32)
    zsum[...] = total.astype(BF16)
    quarter_b[here] = zsum[...]
    shared_all = [
        give(zsum, quarter_b.at[pl.ds(line_here * line_rows, line_rows)], line_partner(*o)[0])
        for o in OTHERS
    ]
    finish_all(note_line)
    note_plane = [
        give(
            notes.at[odd, two, half_here],
            notes.at[odd, two, half_here],
            plane_partner(*o)[0],
        )
        for o in OTHERS
    ]

    down_swap = give(
        edn_any.at[pl.ds((1 - zero) * dn_rows, dn_rows)], dn_sum, line_partner(1, 0)[0]
    )
    side_all = [give(side, sides.at[column_here], column_partner(*o)[0]) for o in COLUMN]
    sides[column_here] = side[...]
    loads[0].wait()
    step = 64
    for r in range(0, up_rows, step):
        s = slice(r, r + step)
        up_sum[s] = (up_mine[s].astype(F32) + eup_got_ref[s].astype(F32)).astype(BF16)
    up_part = up_rows // 4
    dn_part = dn_rows // 4
    spread_rows = []
    for offset in OTHERS:
        device, place = owner_partner(*offset)
        spread_rows.append(
            give(up_sum.at[pl.ds(place * up_part, up_part)], up_got.at[owner_here], device)
        )
    up_got[owner_here] = up_sum[pl.ds(pl.multiple_of(owner_here * up_part, 16), up_part)]

    finish_all(plane_sums)
    shared_a = full_a.at[odd, two, shared_rows]
    plane_a = [give(quarter_ref, shared_a, plane_partner(*o)[0]) for o in OTHERS]
    here_rows = pl.ds(pl.multiple_of(two * quarter_rows, 16), quarter_rows)
    here_lanes = pl.ds(pl.multiple_of(half_here * quarter_lanes, 128), quarter_lanes)
    total = keep[here_rows, here_lanes].astype(F32)
    for index in range(len(OTHERS)):
        total = total + pieces[index].astype(F32)
    zslots[line_here] = total.astype(BF16)
    line_sums = [
        give(zslots.at[line_here], zslots.at[line_here], line_partner(*o)[0]) for o in OTHERS
    ]
    finish_all(note_plane)
    note_swap = give(notes.at[odd], notes.at[odd], sibling())

    finish_all(shared_all)
    shared_b = full_b.at[odd, two, shared_rows]
    own_b = pltpu.make_async_copy(quarter_b, shared_b, locals_.at[3])
    own_b.start()

    finish_all(line_sums)
    total = zslots[0].astype(F32)
    for index in range(1, 4):
        total = total + zslots[index].astype(F32)
    done[odd, here_rows, here_lanes] = total.astype(BF16)
    place = done.at[
        odd,
        pl.ds(two * quarter_rows, quarter_rows),
        pl.ds(pl.multiple_of(half_here * quarter_lanes, 128), quarter_lanes),
    ]
    plane_all = [give(place, place, plane_partner(*o)[0]) for o in OTHERS]
    plane_b = [give(quarter_b, shared_b, plane_partner(*o)[0]) for o in OTHERS]

    down_swap.wait()
    loads[1].wait()
    for r in range(0, dn_rows, step):
        s = slice(r, r + step)
        dn_sum[s] = (dn_mine[s].astype(F32) + dn_sum[s].astype(F32)).astype(BF16)
    for offset in OTHERS:
        device, place = owner_partner(*offset)
        spread_rows.append(
            give(dn_sum.at[pl.ds(place * dn_part, dn_part)], dn_got.at[owner_here], device)
        )
    dn_got[owner_here] = dn_sum[pl.ds(pl.multiple_of(owner_here * dn_part, 16), dn_part)]

    loads[2].wait()
    finish_all(plane_a)
    last = [give(full_a.at[odd], full_a.at[odd], sibling())]
    finish_all(plane_all)
    last.append(give(done.at[odd], done.at[odd], sibling()))
    own_b.wait()
    finish_all(plane_b)
    last.append(give(full_b.at[odd], full_b.at[odd], sibling()))
    note_swap.wait()
    finish_all(side_all)
    finish_all(spread_rows)
    finish_all(last)


def tail(*args):
    dqkv_w, quarter, note, edown = args[0], args[6], args[8], args[12]
    width = dqkv_w.shape[0]
    hidden = edown.shape[0]
    nets = args[4].shape[0]
    rows = width + 32
    lanes = hidden // 2
    half_rows = quarter.shape[0]
    full = like((2, nets, 2 * half_rows, lanes), BF16)
    return pl.pallas_call(
        tail_kernel,
        in_specs=[in_vmem()] * 11 + [anywhere()] * 2,
        out_specs=[anywhere()] * 2 + [in_vmem()] * 5,
        out_shape=[
            full,
            full,
            like((2, rows, lanes), BF16),
            like((2, 2, 2, 4) + note.shape, BF16),
            like((4, width // 8, hidden), BF16),
            like((4, hidden // 8, width), BF16),
            like((8, 16, hidden), BF16),
        ],
        scratch_shapes=[
            pltpu.VMEM((2, rows, lanes), BF16),
            pltpu.VMEM((rows, lanes), BF16),
            pltpu.VMEM((rows, lanes), BF16),
            pltpu.VMEM((3, rows // 2, lanes // 2), BF16),
            pltpu.VMEM((4, rows // 2, lanes // 2), BF16),
            pltpu.VMEM((3, half_rows // 4, lanes), BF16),
            pltpu.VMEM((half_rows // 4, lanes), BF16),
            pltpu.VMEM((half_rows, lanes), BF16),
            pltpu.VMEM((width // 2, hidden), BF16),
            pltpu.VMEM((width // 2, hidden), BF16),
            pltpu.VMEM((hidden // 2, width), BF16),
            pltpu.VMEM((hidden // 2, width), BF16),
            pltpu.VMEM((16, hidden), BF16),
            pltpu.SemaphoreType.DMA((48,)),
            pltpu.SemaphoreType.DMA((48,)),
            pltpu.SemaphoreType.DMA((4,)),
        ],
        compiler_params=pltpu.CompilerParams(
            vmem_limit_bytes=VMEM_BYTES, collective_id=4, has_side_effects=True
        ),
        name="tail",
    )(*args)


def finish_kernel(
    nets,
    dp_count,
    full_a_any,
    full_b_any,
    done_ref,
    notes_ref,
    up_ref,
    dn_ref,
    sides_ref,
    time_table_ref,
    label_table_ref,
    time_any,
    label_any,
    ada_any,
    ada_b_ref,
    qkv_any,
    out_any,
    out_b_ref,
    router_ref,
    eup_any,
    eup_b_ref,
    edn_any,
    edn_b_ref,
    sup_any,
    sup_b_ref,
    sdn_any,
    sdn_b_ref,
    full_a,
    full_b,
    time_out,
    label_out,
    ada_out,
    qkv_out,
    weight_out,
    eup_out,
    edn_out,
    sup_out,
    sdn_out,
    in_sems,
    out_sems,
):
    width = out_any.shape[0]
    lanes = done_ref.shape[2]
    experts = router_ref.shape[1]
    ins = [
        pltpu.make_async_copy(full_a_any, full_a, in_sems.at[0]),
        pltpu.make_async_copy(full_b_any, full_b, in_sems.at[1]),
    ]
    for copy in ins:
        copy.start()
    outs = []

    def write(source, target):
        copy = pltpu.make_async_copy(source, target, out_sems.at[len(outs)])
        copy.start()
        outs.append(copy)

    eup_out[...] = up_ref[...].astype(F32)
    write(eup_out, eup_any)
    edn_out[...] = dn_ref[...].astype(F32)
    write(edn_out, edn_any)
    rest = qkv_any.shape[1] - lanes
    qkv_out[:, :lanes] = done_ref[0, :width].astype(F32)
    qkv_out[:, lanes:] = done_ref[1, :width, :rest].astype(F32)
    write(qkv_out, qkv_any)
    weight_out[...] = done_ref[1, :width, rest:].astype(F32)
    write(weight_out, out_any)

    for index, half in enumerate((full_a, full_b)):
        ins[index].wait()
        for net in range(nets):
            first = index * lanes
            sup_out[net, :, first : first + lanes] = half[0, net].astype(F32)
            sdn_out[net, first : first + lanes, :] = half[1, net].astype(F32).T
            write(
                sdn_out.at[net, pl.ds(first, lanes)], sdn_any.at[net, pl.ds(first, lanes)]
            )
    write(sup_out, sup_any)

    notes = notes_ref[...].reshape(-1, notes_ref.shape[4], notes_ref.shape[5])
    high = notes[:, 0:8, :].reshape(-1, notes.shape[2])
    low = notes[:, 8:16, :].reshape(-1, notes.shape[2])
    rows = jnp.concatenate([high, low], axis=1)
    count = rows.shape[0]
    grad_mod = rows[:, : 6 * width]
    grad_cond = rows[:, 6 * width : 7 * width]
    marks = rows[:, 7 * width :].astype(F32)
    label = marks[:, 0:1] * 32.0 + marks[:, 1:2]
    time = marks[:, 2:3] * 32.0 + marks[:, 3:4]

    def table(marked, out_ref):
        line = jnp.broadcast_to(marked, (count, 128)).T[0:1, :]
        tall = (iota((out_ref.shape[0], count), 0).astype(F32) == line).astype(F32).astype(BF16)
        out_ref[...] = dot(tall, grad_cond)

    table(label, label_out)
    write(label_out, label_any)
    table(time, time_out)
    write(time_out, time_any)
    label_hot = (iota((count, label_table_ref.shape[0]), 1).astype(F32) == label).astype(F32)
    time_hot = (iota((count, time_table_ref.shape[0]), 1).astype(F32) == time).astype(F32)
    condition = dot(label_hot.astype(BF16), label_table_ref[...])
    condition = condition + dot(time_hot.astype(BF16), time_table_ref[...])
    act = condition / (1.0 + jnp.exp(-condition))
    ada_out[...] = dot(act.T.astype(BF16), grad_mod)
    write(ada_out, ada_any)
    ada_b_ref[...] = jnp.sum(grad_mod.astype(F32), axis=0, keepdims=True)

    rest_a = done_ref[0, width:].astype(F32)
    rest_b = done_ref[1, width:].astype(F32)
    router = jnp.concatenate(
        [rest_a[:experts, :width], jnp.zeros((128 - experts, width), F32)], axis=0
    )
    router_ref[...] = router.T[:, :experts]
    sup_b_ref[:, :lanes] = rest_a[experts : experts + nets]
    sup_b_ref[:, lanes:] = rest_b[experts : experts + nets]
    last = rest_a[experts + nets : experts + nets + 1]
    out_b_ref[...] = last[:, :width]
    sdn_b_ref[...] = jnp.broadcast_to(last[:, width:], sdn_b_ref.shape)
    place = lax.axis_index(("p0", "p1", "p2"))
    for index in range(4):
        total = sides_ref[index, 0:8].astype(F32) + sides_ref[4 + index, 0:8].astype(F32)
        size = total.shape[1]
        up_rows = eup_b_ref.shape[1]
        dn_rows = edn_b_ref.shape[1]
        turned = pltpu.roll(total, size - place * up_rows, 1)
        eup_b_ref[index : index + 1, :] = turned[0:1, :up_rows]
        turned = pltpu.roll(total, size - place * dn_rows, 1)
        edn_b_ref[index : index + 1, :] = turned[1:2, :dn_rows]
    finish_all(outs)


def finish(gathered, time_table, label_table, experts, width, hidden, nets, dp_count):
    time_shape = time_table.shape
    label_shape = label_table.shape
    shapes = [
        time_shape,
        label_shape,
        (width, 6 * width),
        (1, 6 * width),
        (width, 3 * width),
        (width, width),
        (1, width),
        (width, experts),
        (4, width // 8, hidden),
        (4, hidden // dp_count),
        (4, hidden // 8, width),
        (4, width // dp_count),
        (nets, width, hidden),
        (nets, hidden),
        (nets, hidden, width),
        (nets, width),
    ]
    large = (0, 1, 2, 4, 5, 8, 10, 12, 14)
    specs = [anywhere() if index in large else in_vmem() for index in range(len(shapes))]
    return pl.pallas_call(
        functools.partial(finish_kernel, nets, dp_count),
        in_specs=[anywhere()] * 2 + [in_vmem()] * 7,
        out_specs=specs,
        out_shape=[like(shape, F32) for shape in shapes],
        scratch_shapes=[pltpu.VMEM(gathered[0].shape, BF16), pltpu.VMEM(gathered[1].shape, BF16)]
        + [pltpu.VMEM(shapes[index], F32) for index in large]
        + [pltpu.SemaphoreType.DMA((2,)), pltpu.SemaphoreType.DMA((16,))],
        compiler_params=pltpu.CompilerParams(vmem_limit_bytes=VMEM_BYTES),
        name="finish",
    )(*gathered, time_table, label_table)


def exchange(blocks, axes):
    return lax.all_to_all(blocks, axes, split_axis=0, concat_axis=0, tiled=True)


def spread(block, axes):
    count = lax.axis_size(axes)
    return exchange(jnp.broadcast_to(block[None], (count,) + block.shape), axes)


def sum_blocks(blocks):
    return jnp.sum(blocks.astype(F32), axis=0)


def sum_everywhere(payload):
    rows, width = payload.shape
    near = ("p2", "expert")
    far = ("p0", "p1")
    near_count = lax.axis_size(near)
    far_count = lax.axis_size(far)
    piece = rows // near_count
    part = exchange(payload.astype(BF16).reshape(near_count, piece, width), near)
    part = sum_blocks(part).astype(BF16)
    part = part.reshape(piece, far_count, width // far_count).transpose(1, 0, 2)
    part = sum_blocks(exchange(part, far)).astype(BF16)
    part = spread(part, far).transpose(1, 0, 2).reshape(piece, width)
    return spread(part, near).reshape(rows, width)


def body(
    tokens,
    cotangent,
    patch_counts,
    time_buckets,
    image_labels,
    expert_routes,
    time_table,
    label_table,
    ada_weight,
    ada_bias,
    qkv_weight,
    out_weight,
    out_bias,
    router_weight,
    expert_up,
    expert_up_bias,
    expert_down,
    expert_down_bias,
    shared_up,
    shared_up_bias,
    shared_down,
    shared_down_bias,
):
    slot_count, width = tokens.shape
    expert_count = router_weight.shape[1]
    local_count, _, hidden = expert_up.shape
    nets = shared_up.shape[0]
    owners = lax.axis_size("expert")
    outer = lax.axis_size("p0")
    dp_count = lax.axis_size(("p0", "p1", "p2"))
    dp_here = lax.axis_index(("p0", "p1", "p2"))
    small = outer == 2 and owners == 4

    routes = expert_routes[0].T
    router_turned = router_weight.T
    modulation, condition, cond_act, place, targets, grad_branch, branch_rows = front(
        owners,
        patch_counts,
        image_labels,
        time_buckets,
        routes,
        time_table,
        label_table,
        ada_weight,
        ada_bias,
        cotangent,
        expert_count,
    )
    owner_branch = exchange(branch_rows, GROUP)
    qkv_pad, attended, log_totals, hidden_one, moe_in, gates, send_rows = attention(
        owners,
        patch_counts,
        tokens,
        modulation,
        qkv_weight,
        out_weight,
        out_bias,
        router_turned,
        routes,
        place,
    )
    shared_total, grad_moe_in, wire, grad_sup_bias, grad_sdown_bias, owner_rows = shared_nets(
        owners,
        moe_in,
        grad_branch,
        shared_up,
        shared_up_bias,
        shared_down,
        shared_down_bias,
        send_rows,
    )
    owner_res, grad_eup, grad_edown, side, returned_grads, part, later = routed_net(
        owners,
        small,
        owner_rows,
        owner_branch,
        expert_up,
        expert_up_bias,
        expert_down,
        expert_down_bias,
        wire,
    )
    (
        layer_out,
        grad_tokens,
        rms_row,
        grad_qkv_weight,
        grad_out_weight,
        grad_out_bias,
        grad_router,
        note,
        quarter,
        part_next,
        eup_got,
    ) = backward(
        owners,
        small,
        patch_counts,
        image_labels,
        time_buckets,
        tokens,
        cotangent,
        modulation,
        condition,
        qkv_pad,
        attended,
        log_totals,
        hidden_one,
        moe_in,
        gates,
        targets,
        shared_total,
        grad_moe_in,
        returned_grads,
        owner_res,
        qkv_weight,
        out_weight,
        out_bias[None],
        router_turned,
        ada_weight,
        part,
        later,
        grad_eup,
    )
    if small:
        gathered = tail(
            grad_qkv_weight,
            grad_out_weight,
            grad_router,
            grad_out_bias,
            grad_sup_bias,
            grad_sdown_bias,
            quarter,
            part_next,
            note,
            side,
            eup_got,
            grad_eup,
            grad_edown,
        )
        (
            sum_time,
            sum_label,
            sum_ada,
            sum_ada_bias,
            sum_qkv,
            sum_out_weight,
            sum_out_bias,
            sum_router,
            sum_eup,
            sum_eup_bias,
            sum_edown,
            sum_edown_bias,
            sum_sup,
            sum_sup_bias,
            sum_sdown,
            sum_sdown_bias,
        ) = finish(
            gathered, time_table, label_table, expert_count, width, hidden, nets, dp_count
        )
        sum_ada_bias = sum_ada_bias[0]
        sum_out_bias = sum_out_bias[0]
    else:
        up_blocks = exchange(grad_eup.reshape(outer, width // outer, hidden), "p0")
        up_part = sum_blocks(up_blocks).astype(BF16).reshape(-1, width // dp_count, hidden)
        sum_eup = exchange(up_part, ("p1", "p2")).astype(F32)
        down_blocks = exchange(grad_edown.reshape(outer, hidden // outer, width), "p0")
        down_part = sum_blocks(down_blocks).astype(BF16).reshape(-1, hidden // dp_count, width)
        sum_edown = exchange(down_part, ("p1", "p2")).astype(F32)
        sides = lax.psum(side, "p0")
        sides = spread(sides, ("p1", "p2"))
        side_up = sides[:, 0]
        side_down = sides[:, 1, :width]

        shared_sums = sum_everywhere(wire.reshape(-1, hidden)).astype(F32).reshape(wire.shape)
        sum_sup = shared_sums[0]
        sum_sdown = shared_sums[1].transpose(0, 2, 1)

        all_rows = spread(jnp.concatenate([note[:8], note[8:]], axis=1), ALL)
        all_rows = all_rows.reshape(-1, 2 * note.shape[1])
        all_modulation = all_rows[:, : 6 * width]
        all_condition = all_rows[:, 6 * width : 7 * width]
        marks = all_rows[:, 7 * width : 7 * width + 4].astype(jnp.int32)
        label_ids = jnp.arange(label_table.shape[0], dtype=jnp.int32)
        label_hot = ((marks[:, 0:1] * 32 + marks[:, 1:2]) == label_ids).astype(BF16)
        time_ids = jnp.arange(time_table.shape[0], dtype=jnp.int32)
        time_hot = ((marks[:, 2:3] * 32 + marks[:, 3:4]) == time_ids).astype(BF16)
        all_act = jax.nn.silu(
            jnp.dot(label_hot, label_table, preferred_element_type=F32)
            + jnp.dot(time_hot, time_table, preferred_element_type=F32)
        ).astype(BF16)
        sum_ada = lax.dot_general(all_act, all_modulation, ROWS_FIRST, preferred_element_type=F32)
        sum_ada_bias = jnp.sum(all_modulation.astype(F32), axis=0)
        sum_label = lax.dot_general(
            label_hot, all_condition, ROWS_FIRST, preferred_element_type=F32
        )
        sum_time = lax.dot_general(time_hot, all_condition, ROWS_FIRST, preferred_element_type=F32)

        last = jnp.concatenate(
            [
                jnp.concatenate([grad_qkv_weight, grad_out_weight], axis=1),
                jnp.pad(grad_router, ((0, 0), (0, hidden - width))),
                grad_sup_bias.reshape(nets, hidden),
                jnp.pad(
                    jnp.concatenate([grad_out_bias, grad_sdown_bias], axis=1),
                    ((0, 0), (0, hidden - 2 * width)),
                ),
            ],
            axis=0,
        )
        near_count = lax.axis_size(("p2", "expert"))
        last = jnp.pad(last, ((0, -last.shape[0] % (16 * near_count)), (0, 0)))
        last = sum_everywhere(last).astype(F32)
        sum_qkv = last[:width, : 3 * width]
        sum_out_weight = last[:width, 3 * width :]
        rest = last[width:]
        sum_eup_bias = lax.dynamic_slice_in_dim(
            side_up, dp_here * (hidden // dp_count), hidden // dp_count, 1
        )
        sum_edown_bias = lax.dynamic_slice_in_dim(
            side_down, dp_here * (width // dp_count), width // dp_count, 1
        )
        sum_router = rest[:expert_count, :width].T
        sum_sup_bias = rest[expert_count : expert_count + nets]
        sum_out_bias = rest[expert_count + nets, :width]
        sum_sdown_bias = jnp.broadcast_to(
            rest[expert_count + nets, width : 2 * width][None], (nets, width)
        )
    return (
        layer_out,
        grad_tokens,
        rms_row[:, :2],
        sum_time,
        sum_label,
        sum_ada,
        sum_ada_bias,
        sum_qkv,
        sum_out_weight,
        sum_out_bias,
        sum_router,
        sum_eup,
        sum_eup_bias,
        sum_edown,
        sum_edown_bias,
        sum_sup,
        sum_sup_bias,
        sum_sdown,
        sum_sdown_bias,
    )


def solution(mesh):
    dp_count = mesh.shape["dp"]
    owners = mesh.shape["expert"]
    split = Mesh(mesh.devices.reshape(dp_count // 4, 2, 2, owners), ALL)
    dp = ("p0", "p1", "p2")
    in_specs = (
        P(ALL, None),
        P(ALL, None),
        P(ALL, None),
        P(ALL),
        P(ALL, None),
        P(ALL, None, None),
        P(),
        P(),
        P(),
        P(),
        P(),
        P(),
        P(),
        P(),
        P("expert", None, None),
        P("expert", None),
        P("expert", None, None),
        P("expert", None),
        P(),
        P(),
        P(),
        P(),
    )
    out_specs = (
        P(ALL, None),
        P(ALL, None),
        P(ALL, None),
        P(),
        P(),
        P(),
        P(),
        P(),
        P(),
        P(),
        P(),
        P("expert", dp, None),
        P("expert", dp),
        P("expert", dp, None),
        P("expert", dp),
        P(),
        P(),
        P(),
        P(),
    )
    return jax.shard_map(body, mesh=split, in_specs=in_specs, out_specs=out_specs, check_vma=False)
```

```python
import functools

import jax
import jax.numpy as jnp
from jax import lax
from jax.experimental import pallas as pl
from jax.experimental.pallas import tpu as pltpu
from jax.sharding import Mesh, PartitionSpec as P

HEADS = 6
HDIM = 64
CAP = 160
PAD = 16
WINDOW = 192
BLOCK = 128
SPAN = BLOCK + 2 * WINDOW
TILE = 256
NORM_EPS = 1e-06
MASK_FILL = -1e30
ROWS_FIRST = (((0,), (0,)), ((), ()))
ROWS_LAST = (((1,), (1,)), ((), ()))
GELU_C = 0.7978845608028654
GELU_K = 0.044715
ALL = ("p0", "p1", "p2", "expert")
GROUP = ("p1", "p2", "expert")
MESH = pl.DeviceIdType.MESH
F32 = jnp.float32
BF16 = jnp.bfloat16
VMEM_BYTES = 56 * 2**20


def norm_rows(matrix):
    row_mean = jnp.mean(matrix, axis=-1, keepdims=True)
    centred = matrix - row_mean
    row_var = jnp.mean(centred * centred, axis=-1, keepdims=True)
    row_scale = lax.rsqrt(row_var + NORM_EPS)
    return (centred * row_scale, row_scale)


def norm_back(grad_in, normed, row_scale):
    grad_mean = jnp.mean(grad_in, axis=-1, keepdims=True)
    cross_mean = jnp.mean(grad_in * normed, axis=-1, keepdims=True)
    return (grad_in - grad_mean - normed * cross_mean) * row_scale


def high_low(values):
    high = values.astype(BF16)
    return (high, (values - high.astype(F32)).astype(BF16))


def iota(shape, dim):
    return lax.broadcasted_iota(jnp.int32, shape, dim)


def dot(left, right):
    return jnp.dot(left, right, preferred_element_type=F32)


def dot_t(left, right):
    return lax.dot_general(left, right, ROWS_LAST, preferred_element_type=F32)


def in_vmem():
    return pl.BlockSpec(memory_space=pltpu.VMEM)


def in_smem():
    return pl.BlockSpec(memory_space=pltpu.SMEM)


def anywhere():
    return pl.BlockSpec(memory_space=pl.ANY)


def like(shape, dtype):
    return jax.ShapeDtypeStruct(shape, dtype)


def image_bounds(counts_ref):
    bounds = []
    start = 0
    for image in range(counts_ref.shape[1]):
        end = start + counts_ref[0, image]
        bounds.append((start, end))
        start = end
    return bounds


def member_block(bounds, first, rows):
    lane = iota((1, 128), 1)
    low = jnp.zeros((1, 128), jnp.int32)
    high = jnp.zeros((1, 128), jnp.int32)
    for image, (start, end) in enumerate(bounds):
        hit = (lane == image) | (lane == 8 + image)
        low = jnp.where(hit, start, low)
        high = jnp.where(hit, end, high)
    slot = first + iota((rows, 128), 0)
    return ((slot >= low) & (slot < high)).astype(F32).astype(BF16)


def stack_modulation(mod, stack):
    high, low = high_low(mod)
    stack[...] = jnp.zeros_like(stack)
    stack[0:16, :] = jnp.concatenate([high.astype(F32), low.astype(F32)], axis=0).astype(BF16)


def segments(bounds, slot):
    total = bounds[-1][1]
    image = jnp.zeros(slot.shape, jnp.int32)
    for _, end in bounds[:-1]:
        image = image + (slot >= end).astype(jnp.int32)
    image = jnp.where(slot >= total, len(bounds) + slot, image)
    return jnp.where(slot < 0, -1, image)


def front_kernel(
    owners,
    local_count,
    counts_ref,
    labels_ref,
    time_ref,
    routes_ref,
    time_table_ref,
    label_table_ref,
    ada_ref,
    ada_bias_ref,
    cot_ref,
    mod_ref,
    cond_ref,
    act_ref,
    pos_ref,
    tgt_ref,
    gb_ref,
    rows_ref,
    stack,
    hot,
    lines,
):
    slots, width = cot_ref.shape
    experts = owners * local_count
    bounds = image_bounds(counts_ref)
    total = bounds[-1][1]

    label_count = label_table_ref.shape[0]
    time_count = time_table_ref.shape[0]
    row = iota((8, label_count), 0)
    wanted = jnp.full((8, label_count), -1, jnp.int32)
    for image in range(len(bounds)):
        wanted = jnp.where(row == image, labels_ref[0, image], wanted)
    label_hot = (iota((8, label_count), 1) == wanted).astype(F32).astype(BF16)
    time_hot = (iota((8, time_count), 1) == time_ref[0]).astype(F32).astype(BF16)
    condition = dot(label_hot, label_table_ref[...]) + dot(time_hot, time_table_ref[...])
    act = (condition / (1.0 + jnp.exp(-condition))).astype(BF16)
    mod = dot(act, ada_ref[...]) + ada_bias_ref[...].reshape(1, -1)
    cond_ref[...] = condition
    act_ref[...] = act
    mod_ref[...] = mod
    stack_modulation(mod[:, 5 * width :], stack)

    first = routes_ref[0:1, :]
    second = routes_ref[1:2, :]
    expert = iota((experts, slots), 0)
    valid = iota((experts, slots), 1) < total
    hit_first = (first == expert) & valid
    hit_second = (second == expert) & valid
    picks = (hit_first | hit_second).astype(F32)
    earlier = (iota((128, 128), 0) < iota((128, 128), 1)).astype(F32).astype(BF16)
    carry = jnp.zeros((experts, 1), F32)
    parts = []
    for lane in range(0, slots, 128):
        part = picks[:, lane : lane + 128]
        parts.append(dot(part.astype(BF16), earlier) + carry)
        carry = carry + jnp.sum(part, axis=1, keepdims=True)
    place = jnp.concatenate(parts, axis=1)
    pos_ref[...] = jnp.where(picks > 0.0, place, -1.0)
    base = (expert % local_count) * owners + expert // local_count
    slot_of = (base * CAP).astype(F32) + place
    lines[...] = jnp.full(lines.shape, -1.0, F32)
    lines[0:1, :] = jnp.sum(jnp.where(hit_first, slot_of + 1.0, 0.0), axis=0, keepdims=True) - 1.0
    lines[1:2, :] = jnp.sum(jnp.where(hit_second, slot_of + 1.0, 0.0), axis=0, keepdims=True) - 1.0
    tgt_ref[...] = lines[...].T

    def gradient(i, carry):
        r = pl.ds(pl.multiple_of(i * TILE, TILE), TILE)
        gate = dot(member_block(bounds, i * TILE, TILE), stack[...])
        gb_ref[r, :] = (gate * cot_ref[r, :].astype(F32)).astype(BF16)
        return carry

    lax.fori_loop(0, slots // TILE, gradient, 0)
    row = iota((CAP, slots), 0).astype(F32)
    for j in range(experts):
        expert = (j % owners) * local_count + j // owners
        line = pos_ref[expert : expert + 1, :]
        hot[...] = (row == line).astype(F32).astype(BF16)
        rows_ref[j] = dot(hot[...], gb_ref[...]).astype(BF16)


def attention_kernel(
    owners,
    local_count,
    counts_ref,
    tokens_ref,
    mod_ref,
    qkv_w_ref,
    out_w_ref,
    out_b_ref,
    router_ref,
    routes_ref,
    pos_ref,
    qkv_ref,
    att_ref,
    lse_ref,
    hidden_ref,
    moe_ref,
    gates_ref,
    send_ref,
    stack,
    values_t,
    hot,
    lines,
    columns,
):
    slots, width = tokens_ref.shape
    experts = owners * local_count
    padded = qkv_ref.shape[0]
    bounds = image_bounds(counts_ref)
    stack_modulation(mod_ref[...], stack)
    scale = HDIM ** (-0.5)

    def part(member, index):
        return dot(member, stack[:, index * width : (index + 1) * width])

    qkv_ref[0:WINDOW, :] = jnp.zeros((WINDOW, 3 * width), BF16)
    qkv_ref[padded - WINDOW :, :] = jnp.zeros((WINDOW, 3 * width), BF16)

    def project(i, carry):
        r = pl.ds(pl.multiple_of(i * TILE, TILE), TILE)
        member = member_block(bounds, i * TILE, TILE)
        normed, _ = norm_rows(tokens_ref[r, :].astype(F32))
        mixed = (normed * (1.0 + part(member, 1)) + part(member, 0)).astype(BF16)
        to = pl.ds(pl.multiple_of(i * TILE + WINDOW, 64), TILE)
        qkv_ref[to, :] = dot(mixed, qkv_w_ref[...]).astype(BF16)
        return carry

    lax.fori_loop(0, slots // TILE, project, 0)
    for r in range(0, padded, BLOCK):
        values_t[:, r : r + BLOCK] = qkv_ref[r : r + BLOCK, 2 * width :].T

    first_half = iota((BLOCK, 128), 1) < HDIM

    def attend(i, carry):
        q_rows = pl.ds(pl.multiple_of(i * BLOCK + WINDOW, 64), BLOCK)
        k_rows = pl.ds(pl.multiple_of(i * BLOCK, BLOCK), SPAN)
        o_rows = pl.ds(pl.multiple_of(i * BLOCK, BLOCK), BLOCK)
        key_segment = segments(bounds, i * BLOCK - WINDOW + iota((SPAN, BLOCK), 0))
        query_segment = segments(bounds, i * BLOCK + iota((1, BLOCK), 1))
        allowed = key_segment == query_segment
        allowed = jnp.concatenate([allowed, allowed], axis=1)
        for pair in range(HEADS // 2):
            lanes = slice(pair * 128, (pair + 1) * 128)
            q = qkv_ref[q_rows, lanes]
            k = qkv_ref[k_rows, width + pair * 128 : width + (pair + 1) * 128]
            zero = jnp.zeros_like(q)
            q = jnp.concatenate(
                [jnp.where(first_half, q, zero), jnp.where(first_half, zero, q)], axis=0
            )
            scores = jnp.where(allowed, dot_t(k, q) * scale, MASK_FILL)
            top = jnp.max(scores, axis=0, keepdims=True)
            expo = jnp.exp(scores - top)
            total = jnp.sum(expo, axis=0, keepdims=True)
            out = dot(values_t[lanes, k_rows], expo.astype(BF16)) / total
            out = jnp.concatenate([out[:HDIM, :BLOCK], out[HDIM:, BLOCK:]], axis=0)
            att_ref[o_rows, lanes] = out.T.astype(BF16)
            log_total = top + jnp.log(total)
            lse_ref[2 * pair : 2 * pair + 1, o_rows] = log_total[:, :BLOCK]
            lse_ref[2 * pair + 1 : 2 * pair + 2, o_rows] = log_total[:, BLOCK:]
        return carry

    lax.fori_loop(0, slots // BLOCK, attend, 0)

    def mix(i, carry):
        r = pl.ds(pl.multiple_of(i * TILE, TILE), TILE)
        member = member_block(bounds, i * TILE, TILE)
        attn_out = dot(att_ref[r, :], out_w_ref[...]) + out_b_ref[...].reshape(1, -1)
        hidden = tokens_ref[r, :].astype(F32) + part(member, 2) * attn_out
        hidden_ref[r, :] = hidden
        normed, _ = norm_rows(hidden)
        moe_ref[r, :] = (normed * (1.0 + part(member, 4)) + part(member, 3)).astype(BF16)
        return carry

    lax.fori_loop(0, slots // TILE, mix, 0)

    logits = dot_t(router_ref[...], moe_ref[...])
    expert = iota((experts, slots), 0)
    chosen = (routes_ref[0:1, :] == expert) | (routes_ref[1:2, :] == expert)
    top = jnp.max(jnp.where(chosen, logits, MASK_FILL), axis=0, keepdims=True)
    expo = jnp.where(chosen, jnp.exp(logits - top), 0.0)
    gates_ref[...] = expo / jnp.sum(expo, axis=0, keepdims=True)

    row = iota((CAP, slots), 0).astype(F32)
    lane = iota((CAP, 128), 1)
    table = jnp.zeros((CAP, 128), F32)
    for j in range(experts):
        expert = (j % owners) * local_count + j // owners
        match = row == pos_ref[expert : expert + 1, :]
        hot[...] = match.astype(F32).astype(BF16)
        gate = jnp.sum(
            jnp.where(match, gates_ref[expert : expert + 1, :], 0.0), axis=1, keepdims=True
        )
        table = jnp.where(lane == j, gate, table)
        send_ref[j, :CAP, :] = dot(hot[...], moe_ref[...]).astype(BF16)
    columns[...] = jnp.zeros_like(columns)
    columns[:CAP, :] = table
    lines[...] = columns[...].T
    for j in range(experts):
        send_ref[j, CAP:, :] = tail_rows(lines[j : j + 1, :], width)


def tail_rows(line, width):
    high = line.astype(BF16).astype(F32)
    row = iota((PAD, line.shape[1]), 0)
    tail = jnp.where(row == 0, high, jnp.where(row == 1, line - high, 0.0))
    rest = jnp.zeros((PAD, width - line.shape[1]), F32)
    return jnp.concatenate([tail, rest], axis=1).astype(BF16)


def forward_kernel(owners, local_count, *refs):
    (
        counts_ref,
        labels_ref,
        time_ref,
        routes_ref,
        time_table_ref,
        label_table_ref,
        ada_ref,
        ada_bias_ref,
        cot_ref,
        tokens_ref,
        qkv_w_ref,
        out_w_ref,
        out_b_ref,
        router_ref,
        mod_ref,
        cond_ref,
        tgt_ref,
        gb_ref,
        owner_ref,
        qkv_ref,
        att_ref,
        lse_ref,
        hidden_ref,
        moe_ref,
        gates_ref,
        send_ref,
        act,
        pos,
        rows,
        small_stack,
        tall_lines,
        stack,
        values_t,
        hot,
        lines,
        columns,
        send_sems,
        recv_sems,
        own_sem,
    ) = refs
    offsets = group_offsets(owners)
    partners = [group_partner(owners, *offset)[0] for offset in offsets if any(offset)]
    barrier = pltpu.get_barrier_semaphore()
    for device in partners:
        pl.semaphore_signal(barrier, inc=1, device_id=device, device_id_type=MESH)
    front_kernel(
        owners,
        local_count,
        counts_ref,
        labels_ref,
        time_ref,
        routes_ref,
        time_table_ref,
        label_table_ref,
        ada_ref,
        ada_bias_ref,
        cot_ref,
        mod_ref,
        cond_ref,
        act,
        pos,
        tgt_ref,
        gb_ref,
        rows,
        small_stack,
        hot,
        tall_lines,
    )
    pl.semaphore_wait(barrier, len(partners))
    copies = [
        group_copy(owners, index, offset, rows, owner_ref, send_sems, recv_sems)
        for index, offset in enumerate(offsets)
        if any(offset)
    ]
    for copy in copies:
        copy.start()
    _, me = group_partner(owners, 0, 0, 0)
    own = pltpu.make_async_copy(rows.at[me], owner_ref.at[me], own_sem)
    own.start()
    attention_kernel(
        owners,
        local_count,
        counts_ref,
        tokens_ref,
        mod_ref,
        qkv_w_ref,
        out_w_ref,
        out_b_ref,
        router_ref,
        routes_ref,
        pos,
        qkv_ref,
        att_ref,
        lse_ref,
        hidden_ref,
        moe_ref,
        gates_ref,
        send_ref,
        stack,
        values_t,
        hot,
        lines,
        columns,
    )
    own.wait()
    finish_all(copies)


def forward(owners, experts, *args):
    tokens = args[9]
    slots, width = tokens.shape
    padded = slots + 2 * WINDOW
    rows = (experts, CAP, width)
    return pl.pallas_call(
        functools.partial(forward_kernel, owners, experts // owners),
        in_specs=[in_smem()] * 3 + [in_vmem()] * (len(args) - 3),
        out_specs=[in_vmem()] * 4 + [anywhere()] + [in_vmem()] * 7,
        out_shape=[
            like((8, 6 * width), F32),
            like((8, width), F32),
            like((slots, 128), F32),
            like((slots, width), BF16),
            like(rows, BF16),
            like((padded, 3 * width), BF16),
            like((slots, width), BF16),
            like((8, slots), F32),
            like((slots, width), F32),
            like((slots, width), BF16),
            like((experts, slots), F32),
            like((experts, CAP + PAD, width), BF16),
        ],
        scratch_shapes=[
            pltpu.VMEM((8, width), BF16),
            pltpu.VMEM((experts, slots), F32),
            pltpu.VMEM(rows, BF16),
            pltpu.VMEM((128, width), BF16),
            pltpu.VMEM((128, slots), F32),
            pltpu.VMEM((128, 6 * width), BF16),
            pltpu.VMEM((width, padded), BF16),
            pltpu.VMEM((CAP, slots), BF16),
            pltpu.VMEM((128, 256), F32),
            pltpu.VMEM((256, 128), F32),
            pltpu.SemaphoreType.DMA((experts,)),
            pltpu.SemaphoreType.DMA((experts,)),
            pltpu.SemaphoreType.DMA,
        ],
        compiler_params=pltpu.CompilerParams(
            vmem_limit_bytes=VMEM_BYTES, collective_id=5, has_side_effects=True
        ),
        name="forward",
    )(*args)


def axes_here():
    return [lax.axis_index(name) for name in ALL]


def group_partner(owners, a, b, c):
    zero, one, two, three = axes_here()
    first = lax.rem(one + a, 2)
    second = lax.rem(two + b, 2)
    third = lax.rem(three + c, owners)
    return (zero, first, second, third), (first * 2 + second) * owners + third


def group_offsets(owners):
    offsets = [(a, b, c) for a in range(2) for b in range(2) for c in range(owners)]
    return sorted(offsets, key=lambda o: -(o[0] + o[1] + (2 * o[2] >= owners)))


def sibling():
    zero, one, two, three = axes_here()
    odd = lax.rem(three, 2)
    return (zero, one, two, three + 1 - 2 * odd)


def plane_partner(b, h):
    zero, one, two, three = axes_here()
    odd = lax.rem(three, 2)
    second = lax.rem(two + b, 2)
    half = lax.rem(three // 2 + h, 2)
    return (zero, one, second, half * 2 + odd), second, half


def line_partner(a, b):
    zero, one, two, three = axes_here()
    first = lax.rem(zero + a, 2)
    second = lax.rem(one + b, 2)
    return (first, second, two, three), first * 2 + second


def owner_partner(a, b):
    zero, one, two, three = axes_here()
    first = lax.rem(one + a, 2)
    second = lax.rem(two + b, 2)
    return (zero, first, second, three), first * 2 + second


def column_partner(a, b, c):
    zero, one, two, three = axes_here()
    first = lax.rem(zero + a, 2)
    second = lax.rem(one + b, 2)
    third = lax.rem(two + c, 2)
    return (first, second, third, three), (first * 2 + second) * 2 + third


OTHERS = [(1, 1), (0, 1), (1, 0)]
COLUMN = [(1, 1, 1), (1, 1, 0), (1, 0, 1), (1, 0, 0), (0, 1, 1), (0, 1, 0), (0, 0, 1)]


def greet(devices):
    barrier = pltpu.get_barrier_semaphore()
    for device in devices:
        pl.semaphore_signal(barrier, inc=1, device_id=device, device_id_type=MESH)
    pl.semaphore_wait(barrier, len(devices))


def push(source, target, send_sem, recv_sem, device):
    copy = pltpu.make_async_remote_copy(
        src_ref=source,
        dst_ref=target,
        send_sem=send_sem,
        recv_sem=recv_sem,
        device_id=device,
        device_id_type=MESH,
    )
    copy.start()
    return copy


def finish_all(copies):
    for copy in copies:
        copy.wait()


def group_copy(owners, index, offsets, source, target, send_sems, recv_sems):
    device, place = group_partner(owners, *offsets)
    _, me = group_partner(owners, 0, 0, 0)
    return pltpu.make_async_remote_copy(
        src_ref=source.at[place],
        dst_ref=target.at[me],
        send_sem=send_sems.at[index],
        recv_sem=recv_sems.at[index],
        device_id=device,
        device_id_type=MESH,
    )


def gelu_parts(pre, grad):
    square = pre * pre
    th = jnp.tanh(pre * (GELU_C + (GELU_C * GELU_K) * square))
    half = 0.5 + 0.5 * th
    slope = half + (0.5 * pre) * (1.0 - th * th) * (GELU_C + (3 * GELU_C * GELU_K) * square)
    return (pre * half).astype(BF16), (grad * slope).astype(BF16)


def shared_kernel(
    owners,
    reduce,
    x_ref,
    g_ref,
    up_ref,
    bu_ref,
    dn_ref,
    bd_ref,
    rows_ref,
    y_ref,
    dx_ref,
    wire_ref,
    dbu_ref,
    dbd_ref,
    owner_ref,
    xt,
    gt,
    send_sems,
    recv_sems,
    own_sem,
    wire,
    got,
    swap_sends,
    swap_recvs,
):
    net = pl.program_id(0)
    chunk = pl.program_id(1)
    rows, width = x_ref.shape
    lanes = up_ref.shape[2]
    offsets = group_offsets(owners)
    odd = lax.rem(lax.axis_index("expert"), 2)

    def swap(n, h):
        here = pl.ds(pl.multiple_of(h * lanes, 128), lanes)
        step = n * (wire.shape[3] // lanes) + h
        return pltpu.make_async_remote_copy(
            src_ref=wire.at[1 - odd, n, :, here],
            dst_ref=got.at[n, :, here],
            send_sem=swap_sends.at[step],
            recv_sem=swap_recvs.at[step],
            device_id=sibling(),
            device_id_type=MESH,
        )

    copies = [
        group_copy(owners, index, offset, rows_ref, owner_ref, send_sems, recv_sems)
        for index, offset in enumerate(offsets)
        if any(offset)
    ]
    _, me = group_partner(owners, 0, 0, 0)
    own = pltpu.make_async_copy(rows_ref.at[me], owner_ref.at[me], own_sem)

    @pl.when((net == 0) & (chunk == 0))
    def _():
        greet([group_partner(owners, *offset)[0] for offset in offsets if any(offset)])
        own.start()
        for copy in copies:
            copy.start()
        for r in range(0, rows, 256):
            xt[:width, r : r + 256] = x_ref[r : r + 256, :].T
            gt[:, r : r + 256] = g_ref[r : r + 256, :].T
        xt[width:, :] = jnp.ones((xt.shape[0] - width, rows), BF16)
        y_ref[...] = jnp.zeros_like(y_ref)
        dx_ref[...] = jnp.zeros_like(dx_ref)
        dbd_ref[...] = jnp.sum(g_ref[...].astype(F32), axis=0, keepdims=True)

    up = up_ref[0]
    dn = dn_ref[0]
    bias = bu_ref[pl.ds(net, 1), pl.ds(pl.multiple_of(chunk * lanes, 128), lanes)]
    pre = dot(x_ref[...], up) + bias
    act, dpre = gelu_parts(pre, dot_t(g_ref[...], dn))
    y_ref[...] += dot(act, dn)
    dx_ref[...] += dot_t(dpre, up)
    dup = dot(xt[...], dpre)
    here = pl.ds(pl.multiple_of(chunk * lanes, 128), lanes)
    wire[0, net, :, here] = dup[:width].astype(BF16)
    dbu_ref[0] = dup[width : width + 1]
    wire[1, net, :, here] = dot(gt[...], act).astype(BF16)
    if reduce:
        swap(net, chunk).start()

    @pl.when((net == pl.num_programs(0) - 1) & (chunk == pl.num_programs(1) - 1))
    def _():
        y_ref[...] += jnp.sum(bd_ref[...], axis=0, keepdims=True)
        if reduce:
            for n in range(wire.shape[1]):
                for h in range(wire.shape[3] // lanes):
                    swap(n, h).wait()
                    place = slice(h * lanes, (h + 1) * lanes)
                    for r in range(0, width, 64):
                        line = slice(r, r + 64)
                        summed = wire[odd, n, line, place].astype(F32) + got[n, line, place].astype(F32)
                        wire_ref[n, line, place] = summed.astype(BF16)
        else:
            wire_ref[...] = wire[...].reshape(wire_ref.shape)
        own.wait()
        for copy in copies:
            copy.wait()


def shared_nets(owners, reduce, x, g, up, bias_up, down, bias_down, rows_out, chunk=768):
    nets, width, hidden = up.shape
    rows = x.shape[0]
    count = rows_out.shape[0]
    kept = nets if reduce else 2 * nets
    steps = nets * (hidden // chunk)

    def whole(shape):
        return pl.BlockSpec(shape, lambda n, h: (0,) * len(shape))

    return pl.pallas_call(
        functools.partial(shared_kernel, owners, reduce),
        grid=(nets, hidden // chunk),
        in_specs=[
            whole(x.shape),
            whole(g.shape),
            pl.BlockSpec((1, width, chunk), lambda n, h: (n, 0, h)),
            whole((nets, hidden)),
            pl.BlockSpec((1, chunk, width), lambda n, h: (n, h, 0)),
            whole((nets, width)),
            anywhere(),
        ],
        out_specs=[
            whole((rows, width)),
            whole((rows, width)),
            whole((kept, width, hidden)),
            pl.BlockSpec((1, 1, chunk), lambda n, h: (n, 0, h)),
            whole((1, width)),
            anywhere(),
        ],
        out_shape=[
            like((rows, width), F32),
            like((rows, width), F32),
            like((kept, width, hidden), BF16),
            like((nets, 1, hidden), F32),
            like((1, width), F32),
            like(rows_out.shape, BF16),
        ],
        scratch_shapes=[
            pltpu.VMEM((width + 16, rows), BF16),
            pltpu.VMEM((width, rows), BF16),
            pltpu.SemaphoreType.DMA((count,)),
            pltpu.SemaphoreType.DMA((count,)),
            pltpu.SemaphoreType.DMA,
            pltpu.VMEM((2, nets, width, hidden), BF16),
            pltpu.VMEM((nets, width, hidden), BF16),
            pltpu.SemaphoreType.DMA((steps,)),
            pltpu.SemaphoreType.DMA((steps,)),
        ],
        compiler_params=pltpu.CompilerParams(
            vmem_limit_bytes=VMEM_BYTES, collective_id=1, has_side_effects=True
        ),
        name="shared_nets",
    )(x, g, up, bias_up, down, bias_down, rows_out)


def routed_kernel(
    owners,
    reduce,
    x_ref,
    g_ref,
    up_any,
    bu_ref,
    dn_any,
    bd_ref,
    wire_any,
    y_ref,
    dup_ref,
    ddn_ref,
    side_ref,
    back_ref,
    part_ref,
    up,
    dn,
    xt,
    gt,
    acts,
    dpres,
    outgoing,
    lines,
    columns,
    load_sems,
    send_sems,
    recv_sems,
    own_sem,
    mine,
    pieces,
    keep_sem,
    sum_sends,
    sum_recvs,
    zgot,
    zsum,
    bias_line,
):
    width, hidden = up.shape
    chunk = 768
    pick = lax.axis_index("p1") * 2 + lax.axis_index("p2")
    loads = [
        pltpu.make_async_copy(up_any.at[pick], up, load_sems.at[0]),
        pltpu.make_async_copy(dn_any.at[pick], dn, load_sems.at[1]),
    ]
    for load in loads:
        load.start()
    offsets = group_offsets(owners)
    places = [group_partner(owners, *offset)[1] for offset in offsets]
    near = [group_partner(owners, *offset)[0] for offset in offsets if any(offset)]
    if reduce:
        near = near + [line_partner(1, 1)[0], line_partner(1, 0)[0]]
    greet(near)
    copies = [
        group_copy(owners, index, offset, outgoing, back_ref, send_sems, recv_sems)
        if any(offset)
        else pltpu.make_async_copy(outgoing.at[places[index]], back_ref.at[places[index]], own_sem)
        for index, offset in enumerate(offsets)
    ]
    sums = []
    if reduce:
        _, own_net, own_half = plane_partner(0, 0)
        size = width // 2
        for index, (b, h) in enumerate(OTHERS):
            device, net, half = plane_partner(b, h)
            source = wire_any.at[net, pl.ds(half * size, size), pl.ds(0, hidden // 2)]
            sums.append(
                push(source, pieces.at[index], sum_sends.at[index], sum_recvs.at[index], device)
            )
        take = pltpu.make_async_copy(
            wire_any.at[own_net, pl.ds(own_half * size, size), pl.ds(0, hidden // 2)], mine, keep_sem
        )
        take.start()
        _, line_here = line_partner(0, 0)
        line_rows = zsum.shape[0]
        own_line = pl.ds(pl.multiple_of(line_here * line_rows, 16), line_rows)

    lines[...] = jnp.zeros_like(lines)
    for index, place in enumerate(places):
        tail = x_ref[place, CAP:, :256].astype(F32)
        lines[index : index + 1, :] = tail[0:1] + tail[1:2]
    columns[...] = lines[...].T
    gates = columns[:CAP, :]
    for load in loads:
        load.wait()
    bu = bu_ref[pl.ds(pick, 1), :]
    bd = bd_ref[pl.ds(pick, 1), :]
    lane = iota((CAP, 128), 1)
    group = owners
    size = group * CAP
    line_sums = []
    line_all = []
    xt[width:, :] = jnp.ones((xt.shape[0] - width, xt.shape[1]), BF16)
    dbd = jnp.zeros((1, width), F32)
    for first in range(0, len(offsets), group):
        members = range(first, first + group)
        span = slice(first * CAP, first * CAP + size)
        x = jnp.concatenate([x_ref[places[k], :CAP, :] for k in members], axis=0)
        raw = [g_ref[places[k]].astype(F32) for k in members]
        g = jnp.concatenate([raw[k - first] * gates[:, k : k + 1] for k in members], axis=0)
        g = g.astype(BF16)
        dbd = dbd + jnp.sum(g.astype(F32), axis=0, keepdims=True)
        xt[:width, span] = x.T
        gt[:, span] = g.T
        y = jnp.zeros((size, width), F32)
        dx = jnp.zeros((size, width), F32)
        for h in range(0, hidden, chunk):
            pre = dot(x, up[:, h : h + chunk]) + bu[:, h : h + chunk]
            act, dpre = gelu_parts(pre, dot_t(g, dn[h : h + chunk, :]))
            acts[span, h : h + chunk] = act
            dpres[span, h : h + chunk] = dpre
            y = y + dot(act, dn[h : h + chunk, :])
            dx = dx + dot_t(dpre, up[:, h : h + chunk])
        table = jnp.zeros((CAP, 128), F32)
        for k in members:
            r = slice((k - first) * CAP, (k - first + 1) * CAP)
            res = (y[r] + bd).astype(BF16).astype(F32)
            y_ref[places[k]] = (res * gates[:, k : k + 1]).astype(BF16)
            inner = jnp.sum(res * raw[k - first], axis=1, keepdims=True)
            table = jnp.where(lane == k - first, inner, table)
            outgoing[places[k], :CAP, :] = dx[r].astype(BF16)
        columns[:CAP, :] = table
        lines[...] = columns[...].T
        for k in members:
            outgoing[places[k], CAP:, :] = tail_rows(lines[k - first : k - first + 1, :], width)
            copies[k].start()
        if reduce and first == 2 * group:
            take.wait()
            finish_all(sums)
            summed = mine[...].astype(F32)
            for index in range(len(OTHERS)):
                summed = summed + pieces[index].astype(F32)
            mine[...] = summed.astype(BF16)
            for index, offset in enumerate(OTHERS):
                device, place = line_partner(*offset)
                source = mine.at[pl.ds(place * line_rows, line_rows)]
                line_sums.append(
                    push(
                        source,
                        zgot.at[index],
                        sum_sends.at[4 + index],
                        sum_recvs.at[4 + index],
                        device,
                    )
                )
    bias_line[...] = jnp.zeros_like(bias_line)
    for k in range(width // 128):
        bias_line[hidden // 128 + k : hidden // 128 + k + 1, :] = dbd[:, k * 128 : (k + 1) * 128]
    for h in range(0, hidden, 512):
        dup = dot(xt[...], dpres[:, h : h + 512])
        dup_ref[:, h : h + 512] = dup[:width].astype(BF16)
        for k in range(4):
            bias_line[h // 128 + k : h // 128 + k + 1, :] = dup[
                width : width + 1, k * 128 : (k + 1) * 128
            ]
        ddn_ref[h : h + 512, :] = dot(gt[...], acts[:, h : h + 512]).T.astype(BF16)
        if reduce and h == 0:
            finish_all(line_sums)
            summed = mine[own_line].astype(F32)
            for index in range(len(OTHERS)):
                summed = summed + zgot[index].astype(F32)
            zsum[...] = summed.astype(BF16)
            part_ref[own_line] = zsum[...]
            target = part_ref.at[pl.ds(line_here * line_rows, line_rows)]
            for index, offset in enumerate(OTHERS):
                device, _ = line_partner(*offset)
                line_all.append(
                    push(zsum, target, sum_sends.at[7 + index], sum_recvs.at[7 + index], device)
                )
    side_ref[...] = bias_line[...].astype(BF16)
    if reduce:
        finish_all(line_all)
    finish_all(copies)


def routed_net(owners, reduce, x, g, up, bias_up, down, bias_down, wire):
    count = x.shape[0]
    rows = count * CAP
    width, hidden = up.shape[1:]
    piece = (width // 2, hidden // 2) if reduce else (16, 128)
    line = (width // 8, hidden // 2) if reduce else (16, 128)
    return pl.pallas_call(
        functools.partial(routed_kernel, owners, reduce),
        in_specs=[in_vmem(), in_vmem(), anywhere(), in_vmem(), anywhere(), in_vmem(), anywhere()],
        out_specs=[in_vmem()] * 4 + [anywhere(), in_vmem()],
        out_shape=[
            like((count, CAP, width), BF16),
            like((width, hidden), BF16),
            like((hidden, width), BF16),
            like((16, 128), BF16),
            like((count, CAP + PAD, width), BF16),
            like(piece, BF16),
        ],
        scratch_shapes=[
            pltpu.VMEM((width, hidden), BF16),
            pltpu.VMEM((hidden, width), BF16),
            pltpu.VMEM((width + 16, rows), BF16),
            pltpu.VMEM((width, rows), BF16),
            pltpu.VMEM((rows, hidden), BF16),
            pltpu.VMEM((rows, hidden), BF16),
            pltpu.VMEM((count, CAP + PAD, width), BF16),
            pltpu.VMEM((128, 256), F32),
            pltpu.VMEM((256, 128), F32),
            pltpu.SemaphoreType.DMA((2,)),
            pltpu.SemaphoreType.DMA((count,)),
            pltpu.SemaphoreType.DMA((count,)),
            pltpu.SemaphoreType.DMA,
            pltpu.VMEM(piece, BF16),
            pltpu.VMEM((3,) + piece, BF16),
            pltpu.SemaphoreType.DMA,
            pltpu.SemaphoreType.DMA((10,)),
            pltpu.SemaphoreType.DMA((10,)),
            pltpu.VMEM((3,) + line, BF16),
            pltpu.VMEM(line, BF16),
            pltpu.VMEM((16, 128), F32),
        ],
        compiler_params=pltpu.CompilerParams(
            vmem_limit_bytes=VMEM_BYTES, collective_id=2, has_side_effects=True
        ),
        name="routed_net",
    )(x, g, up, bias_up, down, bias_down, wire)


def member_rows(bounds, first, rows):
    image = iota((16, rows), 0)
    slot = first + iota((16, rows), 1)
    low = jnp.zeros((16, rows), jnp.int32)
    high = jnp.zeros((16, rows), jnp.int32)
    for index, (start, end) in enumerate(bounds):
        low = jnp.where(image == index, start, low)
        high = jnp.where(image == index, end, high)
    return ((slot >= low) & (slot < high)).astype(F32).astype(BF16)


def backward_kernel(
    owners,
    local_count,
    reduce,
    counts_ref,
    labels_ref,
    time_ref,
    tokens_any,
    cot_ref,
    mod_ref,
    cond_ref,
    qkv_any,
    att_ref,
    lse_ref,
    hidden_ref,
    moe_any,
    gates_ref,
    tgt_ref,
    shared_any,
    dmoe_ref,
    grads_ref,
    res_ref,
    qkv_w_ref,
    out_w_ref,
    out_b_ref,
    router_ref,
    ada_any,
    sup_b_ref,
    sdn_b_ref,
    side_ref,
    quarter_a,
    later_any,
    eup_any,
    edn_any,
    layer_ref,
    dtok_ref,
    rms_ref,
    full_a,
    full_b,
    done,
    notes,
    up_got,
    dn_got,
    sides,
    stack,
    hot,
    rows_ext,
    gate_cols,
    ghid,
    gatt,
    kt,
    dkeys,
    dvals,
    dqkv,
    turned,
    dlog,
    sums,
    lines,
    columns,
    router,
    res,
    send_sems,
    recv_sems,
    own_sem,
    load,
    keep,
    got,
    tail_pieces,
    zgot_wide,
    zgot,
    next_part,
    quarter_b,
    pieces,
    up_sum,
    up_mine,
    dn_sum,
    dn_mine,
    note_here,
    tokens_ref,
    qkv_ref,
    moe_ref,
    shared_ref,
    ada_ref,
    load_sems,
    sends,
    recvs,
    locals_,
):
    slots, width = tokens_ref.shape
    experts = owners * local_count
    padded = qkv_ref.shape[0]
    blocks = slots // TILE
    offsets = group_offsets(owners)
    zero, one, two, three = axes_here()
    odd = lax.rem(three, 2)
    _, _, half_here = plane_partner(0, 0)
    _, line_here = line_partner(0, 0)
    _, owner_here = owner_partner(0, 0)
    _, column_here = column_partner(0, 0, 0)
    rows, hidden = load.shape[1], 2 * load.shape[2]
    lane_half = hidden // 2
    quarter_rows = rows // 2
    quarter_lanes = lane_half // 2
    up_rows = up_sum.shape[0]
    dn_rows = dn_sum.shape[0]
    half_rows = quarter_a.shape[0]
    line_rows = half_rows // 4
    shared_rows = pl.ds(half_here * half_rows, half_rows)
    own_rows = pl.ds(pl.multiple_of(half_here * half_rows, 64), half_rows)
    own_line = pl.ds(pl.multiple_of(line_here * line_rows, 16), line_rows)
    counter = iter(range(sends.shape[0]))

    def give(source, target, device):
        index = next(counter)
        return push(source, target, sends.at[index], recvs.at[index], device)

    inputs = [
        pltpu.make_async_copy(source, target, load_sems.at[index])
        for index, (source, target) in enumerate(
            [
                (moe_any, moe_ref),
                (qkv_any, qkv_ref),
                (tokens_any, tokens_ref),
                (shared_any, shared_ref),
                (ada_any, ada_ref),
            ]
        )
    ]
    near = [group_partner(owners, *offset)[0] for offset in offsets if any(offset)]
    if reduce:
        near = near + [column_partner(1, b, c)[0] for b in range(2) for c in range(2)]
    greet(near)
    for copy in inputs:
        copy.start()
    _, me = group_partner(owners, 0, 0, 0)
    own = pltpu.make_async_copy(res_ref.at[me], res.at[me], own_sem)
    own.start()
    copies = [
        group_copy(owners, index, offset, res_ref, res, send_sems, recv_sems)
        for index, offset in enumerate(offsets)
        if any(offset)
    ]

    def line_exchange(source_ref, slot):
        started = []
        for index, offset in enumerate(OTHERS):
            device, place = line_partner(*offset)
            source = source_ref.at[pl.ds(place * line_rows, line_rows)]
            started.append(give(source, zgot.at[slot + index], device))
        return started

    def line_spread(source_ref, slot, target):
        summed = source_ref[own_line].astype(F32)
        for index in range(len(OTHERS)):
            summed = summed + zgot[slot + index].astype(F32)
        target[own_line] = summed.astype(BF16)
        here = target.at[pl.ds(line_here * line_rows, line_rows)]
        return [give(here, here, line_partner(*offset)[0]) for offset in OTHERS]

    def plane_spread(source_ref, full, index):
        target = full.at[odd, two, shared_rows]
        mine = pltpu.make_async_copy(source_ref, target, locals_.at[index])
        mine.start()
        beside = give(source_ref, target, plane_partner(1, 0)[0])
        return beside, [mine, give(source_ref, target, plane_partner(0, 1)[0])]

    def pass_on(received, block):
        received.wait()
        return give(block, block, plane_partner(0, 1)[0])

    if reduce:
        loads = [
            pltpu.make_async_copy(eup_any.at[pl.ds(zero * up_rows, up_rows)], up_mine, locals_.at[2]),
            pltpu.make_async_copy(edn_any.at[pl.ds(zero * dn_rows, dn_rows)], dn_mine, locals_.at[3]),
        ]
        for copy in loads:
            copy.start()
        plane_b = []
        for index, offset in enumerate(OTHERS):
            device, net, half = plane_partner(*offset)
            source = later_any.at[
                net, pl.ds(half * half_rows, half_rows), pl.ds(lane_half, lane_half)
            ]
            plane_b.append(give(source, pieces.at[index], device))
        for copy in copies:
            copy.start()
        across, _ = line_partner(1, 0)
        up_swap = give(eup_any.at[pl.ds((1 - zero) * up_rows, up_rows)], up_sum, across)
        own_b = pltpu.make_async_copy(later_any.at[two, shared_rows, pl.ds(lane_half, lane_half)], next_part, locals_.at[4])
        own_b.start()
        sides[column_here] = side_ref[...]
        side_all = [give(side_ref, sides.at[column_here], column_partner(*o)[0]) for o in COLUMN]
    else:
        for copy in copies:
            copy.start()
    bounds = image_bounds(counts_ref)
    total = bounds[-1][1]
    scale = HDIM ** (-0.5)
    stack_modulation(mod_ref[...], stack)
    sums[...] = jnp.zeros_like(sums)

    def part(member, index):
        return dot(member, stack[:, index * width : (index + 1) * width])

    def collect(turned_member, index, values):
        sums[:, index * width : (index + 1) * width] += dot(turned_member, values.astype(BF16))

    lines[...] = jnp.zeros_like(lines)
    for j in range(experts):
        tail = grads_ref[j, CAP:, :256].astype(F32)
        lines[j : j + 1, :] = tail[0:1] + tail[1:2]
    columns[...] = lines[...].T
    lane = iota((CAP, 128), 1)
    for j in range(experts):
        expert = (j % owners) * local_count + j // owners
        r = slice(j * CAP, (j + 1) * CAP)
        rows_ext[r, :width] = grads_ref[j, :CAP, :]
        inner = columns[:CAP, j : j + 1]
        high = inner.astype(BF16).astype(F32)
        spread_out = jnp.where(
            lane == expert, high, jnp.where(lane == experts + expert, inner - high, 0.0)
        )
        rows_ext[r, width:] = spread_out.astype(BF16)
    gate_cols[...] = jnp.zeros_like(gate_cols)
    gate_cols[:experts, :] = gates_ref[...]
    router[...] = jnp.zeros_like(router)
    router[:experts, :] = router_ref[...]

    def routing(i, carry):
        r = pl.ds(pl.multiple_of(i * TILE, TILE), TILE)
        first = tgt_ref[r, 0:1]
        second = tgt_ref[r, 1:2]
        slot = iota((TILE, hot.shape[1]), 1).astype(F32)
        hot[...] = ((slot == first) | (slot == second)).astype(F32).astype(BF16)
        back = dot(hot[...], rows_ext[...])
        inner = back[:, width : width + experts] + back[:, width + experts : width + 2 * experts]
        gates = gate_cols[:, r].T[:, :experts]
        grad = gates * (inner - jnp.sum(gates * inner, axis=1, keepdims=True))
        grad = jnp.concatenate([grad, jnp.zeros((TILE, 128 - experts), F32)], axis=1)
        grad = grad.astype(BF16)
        dlog[:, r] = grad.T
        gmoe = dmoe_ref[r, :] + back[:, :width] + dot(grad, router[...])
        member = member_block(bounds, i * TILE, TILE)
        turned_member = member_rows(bounds, i * TILE, TILE)
        normed, row_scale = norm_rows(hidden_ref[r, :])
        collect(turned_member, 3, gmoe)
        collect(turned_member, 4, gmoe * normed)
        grad_hidden = cot_ref[r, :].astype(F32) + norm_back(
            gmoe * (1.0 + part(member, 4)), normed, row_scale
        )
        ghid[r, :] = grad_hidden
        grad_attn = (part(member, 2) * grad_hidden).astype(BF16)
        attn_out = dot(att_ref[r, :], out_w_ref[...]) + out_b_ref[...].reshape(1, -1)
        collect(turned_member, 2, grad_hidden * attn_out)
        to = pl.ds(pl.multiple_of(i * TILE, TILE), TILE)
        gatt[to, :] = dot_t(grad_attn, out_w_ref[...]).astype(BF16)
        dqkv[r, :width] = grad_attn
        turned[:, r] = att_ref[r, :].T
        return carry

    lax.fori_loop(0, blocks, routing, 0)
    inputs[0].wait()
    drouter = dot(dlog[...], moe_ref[...])[:experts]
    dout_w = dot(turned[...], dqkv[:, :width])
    dout_b = jnp.sum(dqkv[:, :width].astype(F32), axis=0, keepdims=True)
    nets = sup_b_ref.shape[0]
    load[1, :width, lane_half - width :] = dout_w.astype(BF16)
    router_rows = jnp.concatenate([drouter, jnp.zeros((experts, hidden - width), F32)], axis=1)
    vectors = jnp.concatenate(
        [dout_b, sdn_b_ref[...], jnp.zeros((1, hidden - 2 * width), F32)], axis=1
    )
    filler = jnp.zeros((rows - width - experts - nets - 1, hidden), F32)
    bottom = jnp.concatenate(
        [router_rows] + [sup_b_ref[n] for n in range(nets)] + [vectors, filler], axis=0
    ).astype(BF16)
    for half in range(2):
        load[half, width:] = bottom[:, half * lane_half : (half + 1) * lane_half]

    inputs[1].wait()
    for r in range(0, padded, BLOCK):
        kt[:, r : r + BLOCK] = qkv_ref[r : r + BLOCK, width : 2 * width].T
    dkeys[...] = jnp.zeros_like(dkeys)
    dvals[...] = jnp.zeros_like(dvals)
    first_half = iota((BLOCK, 128), 1) < HDIM

    def split(pair_rows):
        zero = jnp.zeros_like(pair_rows)
        return jnp.concatenate(
            [jnp.where(first_half, pair_rows, zero), jnp.where(first_half, zero, pair_rows)],
            axis=0,
        )

    def attend(i, carry):
        q_rows = pl.ds(pl.multiple_of(i * BLOCK + WINDOW, 64), BLOCK)
        k_rows = pl.ds(pl.multiple_of(i * BLOCK, BLOCK), SPAN)
        o_rows = pl.ds(pl.multiple_of(i * BLOCK, BLOCK), BLOCK)
        key_segment = segments(bounds, i * BLOCK - WINDOW + iota((SPAN, BLOCK), 0))
        query_segment = segments(bounds, i * BLOCK + iota((1, BLOCK), 1))
        allowed = key_segment == query_segment
        allowed = jnp.concatenate([allowed, allowed], axis=1)
        for pair in range(HEADS // 2):
            lanes = slice(pair * 128, (pair + 1) * 128)
            q = split(qkv_ref[q_rows, lanes])
            out_grad = split(gatt[o_rows, lanes])
            k = qkv_ref[k_rows, width + pair * 128 : width + (pair + 1) * 128]
            v = qkv_ref[k_rows, 2 * width + pair * 128 : 2 * width + (pair + 1) * 128]
            log_total = jnp.concatenate(
                [lse_ref[2 * pair : 2 * pair + 1, o_rows], lse_ref[2 * pair + 1 : 2 * pair + 2, o_rows]],
                axis=1,
            )
            probs = jnp.exp(jnp.where(allowed, dot_t(k, q) * scale, MASK_FILL) - log_total)
            grad_probs = dot_t(v, out_grad)
            inner = jnp.sum(probs * grad_probs, axis=0, keepdims=True)
            grad_scores = (probs * (grad_probs - inner)).astype(BF16)
            dvals[k_rows, lanes] += dot(probs.astype(BF16), out_grad)
            dkeys[k_rows, lanes] += dot(grad_scores, q) * scale
            turned_query = dot(kt[lanes, k_rows], grad_scores) * scale
            turned_query = jnp.concatenate(
                [turned_query[:HDIM, :BLOCK], turned_query[HDIM:, BLOCK:]], axis=0
            )
            dqkv[o_rows, lanes] = turned_query.T.astype(BF16)
        return carry

    lax.fori_loop(0, 4, attend, 0)
    if reduce:
        finish_all(plane_b)
        own_b.wait()
        summed = next_part[...].astype(F32)
        for index in range(len(OTHERS)):
            summed = summed + pieces[index].astype(F32)
        next_part[...] = summed.astype(BF16)
        line_b = line_exchange(next_part, 0)
    lax.fori_loop(4, slots // BLOCK, attend, 0)
    if reduce:
        finish_all(line_b)
        all_b = line_spread(next_part, 0, quarter_b)
        down_swap = give(edn_any.at[pl.ds((1 - zero) * dn_rows, dn_rows)], dn_sum, across)

    inputs[2].wait()

    def project(i, carry):
        r = pl.ds(pl.multiple_of(i * TILE, TILE), TILE)
        from_rows = pl.ds(pl.multiple_of(i * TILE + WINDOW, 64), TILE)
        dqkv[r, width : 2 * width] = dkeys[from_rows, :].astype(BF16)
        dqkv[r, 2 * width :] = dvals[from_rows, :].astype(BF16)
        member = member_block(bounds, i * TILE, TILE)
        normed, _ = norm_rows(tokens_ref[r, :].astype(F32))
        turned[:, r] = (normed * (1.0 + part(member, 1)) + part(member, 0)).astype(BF16).T
        return carry

    lax.fori_loop(0, blocks, project, 0)
    dqkv_w = dot(turned[...], dqkv[...]).astype(BF16)
    load[0, :width] = dqkv_w[:, :lane_half]
    load[1, :width, : lane_half - width] = dqkv_w[:, lane_half:]
    if reduce:
        swap = give(load.at[1 - odd], got, sibling())
    else:
        done[...] = load[...]

    def finish(i, carry):
        r = pl.ds(pl.multiple_of(i * TILE, TILE), TILE)
        member = member_block(bounds, i * TILE, TILE)
        turned_member = member_rows(bounds, i * TILE, TILE)
        gmix = dot_t(dqkv[r, :], qkv_w_ref[...])
        normed, row_scale = norm_rows(tokens_ref[r, :].astype(F32))
        gain = 1.0 + part(member, 1)
        collect(turned_member, 0, gmix)
        collect(turned_member, 1, gmix * normed)
        dtok_ref[r, :] = ghid[r, :] + norm_back(gmix * gain, normed, row_scale)
        return carry

    lax.fori_loop(0, blocks, finish, 0)
    if reduce:
        swap.wait()
        keep[...] = (load[odd].astype(F32) + got[...].astype(F32)).astype(BF16)
        plane_sums = []
        for index, offset in enumerate(OTHERS):
            device, second, half = plane_partner(*offset)
            source = keep.at[
                pl.ds(second * quarter_rows, quarter_rows),
                pl.ds(pl.multiple_of(half * quarter_lanes, 128), quarter_lanes),
            ]
            plane_sums.append(give(source, tail_pieces.at[index], device))
        plane_all_a = plane_spread(quarter_a, full_a, 0)
    inputs[3].wait()
    inputs[4].wait()
    own.wait()
    finish_all(copies)
    for j in range(experts):
        rows_ext[j * CAP : (j + 1) * CAP, :width] = res[j]

    def result(i, carry):
        r = pl.ds(pl.multiple_of(i * TILE, TILE), TILE)
        member = member_block(bounds, i * TILE, TILE)
        first = tgt_ref[r, 0:1]
        second = tgt_ref[r, 1:2]
        slot = iota((TILE, hot.shape[1]), 1).astype(F32)
        hot[...] = ((slot == first) | (slot == second)).astype(F32).astype(BF16)
        branch = dot(hot[...], rows_ext[:, :width]) + shared_ref[r, :]
        layer = hidden_ref[r, :] + part(member, 5) * branch
        layer_ref[r, :] = layer.astype(BF16)
        valid = (i * TILE + iota((TILE, width), 0)) < total
        collect(member_rows(bounds, i * TILE, TILE), 5, cot_ref[r, :].astype(F32) * branch)
        layer_squares = jnp.sum(jnp.where(valid, layer * layer, 0.0), axis=0, keepdims=True)
        branch_squares = jnp.sum(jnp.where(valid, branch * branch, 0.0), axis=0, keepdims=True)
        return (carry[0] + layer_squares, carry[1] + branch_squares)

    nothing = jnp.zeros((1, width), F32)
    squares = lax.fori_loop(0, blocks, result, (nothing, nothing))
    count = jnp.full((1, 1), total * width, jnp.int32).astype(F32)
    roots = [jnp.sqrt(jnp.sum(line, axis=1, keepdims=True) / count) for line in squares]
    rms_ref[...] = jnp.where(iota((1, 128), 1) == 0, roots[0], roots[1])

    grad_mod = sums[0:8, :]
    high, low = high_low(grad_mod)
    grad_act = dot_t(high, ada_ref[...]) + dot_t(low, ada_ref[...])
    condition = cond_ref[...]
    sigmoid = 1.0 / (1.0 + jnp.exp(-condition))
    grad_cond = grad_act * (sigmoid * (1.0 + condition * (1.0 - sigmoid)))
    row = iota((8, 128), 0)
    lane = iota((8, 128), 1)
    label = jnp.zeros((8, 128), jnp.int32)
    for image in range(len(bounds)):
        label = jnp.where(row == image, labels_ref[0, image], label)
    time = jnp.full((8, 128), time_ref[0], jnp.int32)
    digits = [label // 32, label % 32, time // 32, time % 32]
    marks = jnp.zeros((8, 128), jnp.int32)
    for index, piece in enumerate(digits):
        marks = jnp.where(lane == index, piece, marks)
    real = row < len(bounds)
    marks = jnp.where(real, marks, jnp.where(lane < 4, 255, 0)).astype(F32)
    inside = (iota((8, width), 0) < len(bounds)).astype(F32)
    note = jnp.concatenate([grad_mod, grad_cond * inside, marks], axis=1)
    middle = note.shape[1] // 2
    note_here[...] = jnp.concatenate([note[:, :middle], note[:, middle:]], axis=0).astype(BF16)
    if not reduce:
        notes[0, 0, 0, 0] = note_here[...]
        return

    notes[odd, two, half_here, line_here] = note_here[...]
    target = notes.at[odd, two, half_here, line_here]
    note_line = [give(note_here, target, line_partner(*o)[0]) for o in OTHERS]
    finish_all(plane_sums)
    here_rows = pl.ds(pl.multiple_of(two * quarter_rows, 16), quarter_rows)
    here_lanes = pl.ds(pl.multiple_of(half_here * quarter_lanes, 128), quarter_lanes)
    summed = keep[here_rows, here_lanes].astype(F32)
    for index in range(len(OTHERS)):
        summed = summed + tail_pieces[index].astype(F32)
    zgot_wide[0] = summed.astype(BF16)
    beside = give(zgot_wide.at[0], zgot_wide.at[1], line_partner(0, 1)[0])
    up_swap.wait()
    loads[0].wait()
    for r in range(0, up_rows, 64):
        s = slice(r, r + 64)
        up_sum[s] = (up_mine[s].astype(F32) + up_sum[s].astype(F32)).astype(BF16)
    up_part = up_rows // 4
    dn_part = dn_rows // 4
    spread_rows = []
    for offset in OTHERS:
        device, place = owner_partner(*offset)
        source = up_sum.at[pl.ds(place * up_part, up_part)]
        spread_rows.append(give(source, up_got.at[owner_here], device))
    up_got[owner_here] = up_sum[pl.ds(pl.multiple_of(owner_here * up_part, 16), up_part)]
    to_second_a, others_a = plane_all_a
    others_a.append(pass_on(to_second_a, full_a.at[odd, 1 - two, shared_rows]))
    finish_all(all_b)
    plane_all_b = plane_spread(quarter_b, full_b, 1)
    finish_all(note_line)
    target = notes.at[odd, two, half_here]
    to_second_n = give(target, target, plane_partner(1, 0)[0])
    others_n = [give(target, target, plane_partner(0, 1)[0])]
    beside.wait()
    summed = zgot_wide[0].astype(F32) + zgot_wide[1].astype(F32)
    zgot_wide[2] = summed.astype(BF16)
    beyond = give(zgot_wide.at[2], zgot_wide.at[3], across)
    to_second_b, others_b = plane_all_b
    others_b.append(pass_on(to_second_b, full_b.at[odd, 1 - two, shared_rows]))
    finish_all(others_a)
    last = [give(full_a.at[odd], full_a.at[odd], sibling())]
    others_n.append(pass_on(to_second_n, notes.at[odd, 1 - two, half_here]))
    beyond.wait()
    summed = zgot_wide[2].astype(F32) + zgot_wide[3].astype(F32)
    done[odd, here_rows, here_lanes] = summed.astype(BF16)
    place = done.at[
        odd,
        pl.ds(two * quarter_rows, quarter_rows),
        pl.ds(pl.multiple_of(half_here * quarter_lanes, 128), quarter_lanes),
    ]
    to_second_d = give(place, place, plane_partner(1, 0)[0])
    others_d = [give(place, place, plane_partner(0, 1)[0])]
    second_block = done.at[
        odd,
        pl.ds((1 - two) * quarter_rows, quarter_rows),
        pl.ds(pl.multiple_of(half_here * quarter_lanes, 128), quarter_lanes),
    ]

    down_swap.wait()
    loads[1].wait()
    for r in range(0, dn_rows, 64):
        s = slice(r, r + 64)
        dn_sum[s] = (dn_mine[s].astype(F32) + dn_sum[s].astype(F32)).astype(BF16)
    for offset in OTHERS:
        device, place = owner_partner(*offset)
        source = dn_sum.at[pl.ds(place * dn_part, dn_part)]
        spread_rows.append(give(source, dn_got.at[owner_here], device))
    dn_got[owner_here] = dn_sum[pl.ds(pl.multiple_of(owner_here * dn_part, 16), dn_part)]

    others_d.append(pass_on(to_second_d, second_block))
    finish_all(others_n)
    last.append(give(notes.at[odd], notes.at[odd], sibling()))
    finish_all(others_b)
    last.append(give(full_b.at[odd], full_b.at[odd], sibling()))
    finish_all(others_d)
    last.append(give(done.at[odd], done.at[odd], sibling()))
    finish_all(side_all)
    finish_all(spread_rows)
    finish_all(last)


def backward(owners, reduce, *args):
    tokens, mod, qkv_pad, gates = (args[k] for k in (3, 5, 7, 12))
    part, eup, edown = (args[k] for k in (26, 28, 29))
    slots, width = tokens.shape
    padded = qkv_pad.shape[0]
    experts = gates.shape[0]
    hidden = edown.shape[0]
    nets = args[23].shape[0]
    rows = width + 32
    lanes = hidden // 2
    note = (16, (7 * width + 128) // 2)
    in_specs = [in_smem()] * 3 + [in_vmem()] * (len(args) - 3)
    for index in (3, 7, 11, 14, 17, 22, 27, 28, 29):
        in_specs[index] = anywhere()
    full = like((2, nets, width, lanes) if reduce else (1, 1, 16, 128), BF16)

    def sized(*shape):
        return pltpu.VMEM(shape if reduce else (16,) * (len(shape) - 1) + (128,), BF16)

    return pl.pallas_call(
        functools.partial(backward_kernel, owners, experts // owners, reduce),
        in_specs=in_specs,
        out_specs=[in_vmem()] * 3 + [anywhere()] * 2 + [in_vmem()] * 5,
        out_shape=[
            like((slots, width), BF16),
            like((slots, width), F32),
            like((1, 128), F32),
            full,
            full,
            like((2, rows, lanes), BF16),
            like((2, 2, 2, 4) + note, BF16),
            like((4, width // 8, hidden), BF16),
            like((4, hidden // 8, width), BF16),
            like((8, 16, 128), BF16),
        ],
        scratch_shapes=[
            pltpu.VMEM((128, 6 * width), BF16),
            pltpu.VMEM((TILE, experts * CAP), BF16),
            pltpu.VMEM((experts * CAP, width + 128), BF16),
            pltpu.VMEM((128, slots), F32),
            pltpu.VMEM((slots, width), F32),
            pltpu.VMEM((slots, width), BF16),
            pltpu.VMEM((width, padded), BF16),
            pltpu.VMEM((padded, width), F32),
            pltpu.VMEM((padded, width), F32),
            pltpu.VMEM((slots, 3 * width), BF16),
            pltpu.VMEM((width, slots), BF16),
            pltpu.VMEM((128, slots), BF16),
            pltpu.VMEM((16, 6 * width), F32),
            pltpu.VMEM((128, 256), F32),
            pltpu.VMEM((256, 128), F32),
            pltpu.VMEM((128, width), BF16),
            pltpu.VMEM((experts, CAP, width), BF16),
            pltpu.SemaphoreType.DMA((experts,)),
            pltpu.SemaphoreType.DMA((experts,)),
            pltpu.SemaphoreType.DMA,
            pltpu.VMEM((2, rows, lanes), BF16),
            sized(rows, lanes),
            sized(rows, lanes),
            sized(3, rows // 2, lanes // 2),
            sized(4, rows // 2, lanes // 2),
            sized(3, width // 8, lanes),
            sized(width // 2, lanes),
            sized(width // 2, lanes),
            sized(3, width // 2, lanes),
            sized(width // 2, hidden),
            sized(width // 2, hidden),
            sized(hidden // 2, width),
            sized(hidden // 2, width),
            pltpu.VMEM(note, BF16),
            pltpu.VMEM(tokens.shape, tokens.dtype),
            pltpu.VMEM(qkv_pad.shape, qkv_pad.dtype),
            pltpu.VMEM(args[11].shape, args[11].dtype),
            pltpu.VMEM(args[14].shape, args[14].dtype),
            pltpu.VMEM(args[22].shape, args[22].dtype),
            pltpu.SemaphoreType.DMA((5,)),
            pltpu.SemaphoreType.DMA((56,)),
            pltpu.SemaphoreType.DMA((56,)),
            pltpu.SemaphoreType.DMA((5,)),
        ],
        compiler_params=pltpu.CompilerParams(
            vmem_limit_bytes=VMEM_BYTES, collective_id=3, has_side_effects=True
        ),
        name="backward",
    )(*args)


def finish_kernel(
    nets,
    dp_count,
    full_a_any,
    full_b_any,
    done_ref,
    notes_ref,
    up_ref,
    dn_ref,
    sides_ref,
    time_table_ref,
    label_table_ref,
    time_any,
    label_any,
    ada_any,
    ada_b_ref,
    qkv_any,
    out_any,
    out_b_ref,
    router_ref,
    eup_any,
    eup_b_ref,
    edn_any,
    edn_b_ref,
    sup_any,
    sup_b_ref,
    sdn_any,
    sdn_b_ref,
    full_a,
    full_b,
    time_out,
    label_out,
    ada_out,
    qkv_out,
    weight_out,
    eup_out,
    edn_out,
    sup_out,
    sdn_out,
    in_sems,
    out_sems,
):
    width = out_any.shape[0]
    lanes = done_ref.shape[2]
    experts = router_ref.shape[1]
    ins = [
        pltpu.make_async_copy(full_a_any, full_a, in_sems.at[0]),
        pltpu.make_async_copy(full_b_any, full_b, in_sems.at[1]),
    ]
    for copy in ins:
        copy.start()
    outs = []

    def write(source, target):
        copy = pltpu.make_async_copy(source, target, out_sems.at[len(outs)])
        copy.start()
        outs.append(copy)

    eup_out[...] = up_ref[...].astype(F32)
    write(eup_out, eup_any)
    edn_out[...] = dn_ref[...].astype(F32)
    write(edn_out, edn_any)
    rest = qkv_any.shape[1] - lanes
    qkv_out[:, :lanes] = done_ref[0, :width].astype(F32)
    qkv_out[:, lanes:] = done_ref[1, :width, :rest].astype(F32)
    write(qkv_out, qkv_any)
    weight_out[...] = done_ref[1, :width, rest:].astype(F32)
    write(weight_out, out_any)

    for index, half in enumerate((full_a, full_b)):
        ins[index].wait()
        for net in range(nets):
            first = index * lanes
            sup_out[net, :, first : first + lanes] = half[0, net].astype(F32)
            sdn_out[net, first : first + lanes, :] = half[1, net].astype(F32).T
            write(
                sdn_out.at[net, pl.ds(first, lanes)], sdn_any.at[net, pl.ds(first, lanes)]
            )
    write(sup_out, sup_any)

    notes = notes_ref[...].reshape(-1, notes_ref.shape[4], notes_ref.shape[5])
    high = notes[:, 0:8, :].reshape(-1, notes.shape[2])
    low = notes[:, 8:16, :].reshape(-1, notes.shape[2])
    rows = jnp.concatenate([high, low], axis=1)
    count = rows.shape[0]
    grad_mod = rows[:, : 6 * width]
    grad_cond = rows[:, 6 * width : 7 * width]
    marks = rows[:, 7 * width :].astype(F32)
    label = marks[:, 0:1] * 32.0 + marks[:, 1:2]
    time = marks[:, 2:3] * 32.0 + marks[:, 3:4]

    def table(marked, out_ref):
        line = jnp.broadcast_to(marked, (count, 128)).T[0:1, :]
        tall = (iota((out_ref.shape[0], count), 0).astype(F32) == line).astype(F32).astype(BF16)
        out_ref[...] = dot(tall, grad_cond)

    table(label, label_out)
    write(label_out, label_any)
    table(time, time_out)
    write(time_out, time_any)
    label_hot = (iota((count, label_table_ref.shape[0]), 1).astype(F32) == label).astype(F32)
    time_hot = (iota((count, time_table_ref.shape[0]), 1).astype(F32) == time).astype(F32)
    condition = dot(label_hot.astype(BF16), label_table_ref[...])
    condition = condition + dot(time_hot.astype(BF16), time_table_ref[...])
    act = condition / (1.0 + jnp.exp(-condition))
    ada_out[...] = dot(act.T.astype(BF16), grad_mod)
    write(ada_out, ada_any)
    ada_b_ref[...] = jnp.sum(grad_mod.astype(F32), axis=0, keepdims=True).reshape(-1)

    rest_a = done_ref[0, width:].astype(F32)
    rest_b = done_ref[1, width:].astype(F32)
    router = jnp.concatenate(
        [rest_a[:experts, :width], jnp.zeros((128 - experts, width), F32)], axis=0
    )
    router_ref[...] = router.T[:, :experts]
    sup_b_ref[:, :lanes] = rest_a[experts : experts + nets]
    sup_b_ref[:, lanes:] = rest_b[experts : experts + nets]
    last = rest_a[experts + nets : experts + nets + 1]
    out_b_ref[...] = last[:, :width].reshape(-1)
    sdn_b_ref[...] = jnp.broadcast_to(last[:, width:], sdn_b_ref.shape)
    place = lax.axis_index(("p0", "p1", "p2"))
    for index in range(4):
        total = sides_ref[index].astype(F32) + sides_ref[4 + index].astype(F32)
        up_size = lanes // 64
        up_line = jnp.concatenate([total[k : k + 1] for k in range(up_size)], axis=1)
        dn_line = jnp.concatenate([total[up_size + k : up_size + k + 1] for k in range(width // 128)], axis=1)
        up_rows = eup_b_ref.shape[1]
        dn_rows = edn_b_ref.shape[1]
        up_line = jnp.broadcast_to(up_line, (8, up_line.shape[1]))
        dn_line = jnp.broadcast_to(dn_line, (8, dn_line.shape[1]))
        turned = pltpu.roll(up_line, up_line.shape[1] - place * up_rows, 1)
        eup_b_ref[index : index + 1, :] = turned[0:1, :up_rows]
        turned = pltpu.roll(dn_line, dn_line.shape[1] - place * dn_rows, 1)
        edn_b_ref[index : index + 1, :] = turned[0:1, :dn_rows]
    finish_all(outs)


def finish(gathered, time_table, label_table, experts, width, hidden, nets, dp_count):
    time_shape = time_table.shape
    label_shape = label_table.shape
    shapes = [
        time_shape,
        label_shape,
        (width, 6 * width),
        (6 * width,),
        (width, 3 * width),
        (width, width),
        (width,),
        (width, experts),
        (4, width // 8, hidden),
        (4, hidden // dp_count),
        (4, hidden // 8, width),
        (4, width // dp_count),
        (nets, width, hidden),
        (nets, hidden),
        (nets, hidden, width),
        (nets, width),
    ]
    large = (0, 1, 2, 4, 5, 8, 10, 12, 14)
    specs = [anywhere() if index in large else in_vmem() for index in range(len(shapes))]
    return pl.pallas_call(
        functools.partial(finish_kernel, nets, dp_count),
        in_specs=[anywhere()] * 2 + [in_vmem()] * 7,
        out_specs=specs,
        out_shape=[like(shape, F32) for shape in shapes],
        scratch_shapes=[pltpu.VMEM(gathered[0].shape, BF16), pltpu.VMEM(gathered[1].shape, BF16)]
        + [pltpu.VMEM(shapes[index], F32) for index in large]
        + [pltpu.SemaphoreType.DMA((2,)), pltpu.SemaphoreType.DMA((16,))],
        compiler_params=pltpu.CompilerParams(vmem_limit_bytes=VMEM_BYTES),
        name="finish",
    )(*gathered, time_table, label_table)


def exchange(blocks, axes):
    return lax.all_to_all(blocks, axes, split_axis=0, concat_axis=0, tiled=True)


def spread(block, axes):
    count = lax.axis_size(axes)
    return exchange(jnp.broadcast_to(block[None], (count,) + block.shape), axes)


def sum_blocks(blocks):
    return jnp.sum(blocks.astype(F32), axis=0)


def sum_everywhere(payload):
    rows, width = payload.shape
    near = ("p2", "expert")
    far = ("p0", "p1")
    near_count = lax.axis_size(near)
    far_count = lax.axis_size(far)
    piece = rows // near_count
    part = exchange(payload.astype(BF16).reshape(near_count, piece, width), near)
    part = sum_blocks(part).astype(BF16)
    part = part.reshape(piece, far_count, width // far_count).transpose(1, 0, 2)
    part = sum_blocks(exchange(part, far)).astype(BF16)
    part = spread(part, far).transpose(1, 0, 2).reshape(piece, width)
    return spread(part, near).reshape(rows, width)


def body(
    tokens,
    cotangent,
    patch_counts,
    time_buckets,
    image_labels,
    expert_routes,
    time_table,
    label_table,
    ada_weight,
    ada_bias,
    qkv_weight,
    out_weight,
    out_bias,
    router_weight,
    expert_up,
    expert_up_bias,
    expert_down,
    expert_down_bias,
    shared_up,
    shared_up_bias,
    shared_down,
    shared_down_bias,
):
    slot_count, width = tokens.shape
    expert_count = router_weight.shape[1]
    local_count, _, hidden = expert_up.shape
    nets = shared_up.shape[0]
    owners = lax.axis_size("expert")
    outer = lax.axis_size("p0")
    dp_count = lax.axis_size(("p0", "p1", "p2"))
    dp_here = lax.axis_index(("p0", "p1", "p2"))
    small = outer == 2 and owners == 4

    routes = expert_routes[0].T
    router_turned = router_weight.T
    (
        modulation,
        condition,
        targets,
        grad_branch,
        owner_branch,
        qkv_pad,
        attended,
        log_totals,
        hidden_one,
        moe_in,
        gates,
        send_rows,
    ) = forward(
        owners,
        expert_count,
        patch_counts,
        image_labels,
        time_buckets,
        routes,
        time_table,
        label_table,
        ada_weight,
        ada_bias,
        cotangent,
        tokens,
        qkv_weight,
        out_weight,
        out_bias,
        router_turned,
    )
    shared_total, grad_moe_in, wire, grad_sup_bias, grad_sdown_bias, owner_rows = shared_nets(
        owners,
        small,
        moe_in,
        grad_branch,
        shared_up,
        shared_up_bias,
        shared_down,
        shared_down_bias,
        send_rows,
    )
    owner_res, grad_eup, grad_edown, side, returned_grads, part = routed_net(
        owners,
        small,
        owner_rows,
        owner_branch,
        expert_up,
        expert_up_bias,
        expert_down,
        expert_down_bias,
        wire,
    )
    (
        layer_out,
        grad_tokens,
        rms_row,
        full_a,
        full_b,
        last_rows,
        notes,
        up_rows,
        down_rows,
        side_rows,
    ) = backward(
        owners,
        small,
        patch_counts,
        image_labels,
        time_buckets,
        tokens,
        cotangent,
        modulation,
        condition,
        qkv_pad,
        attended,
        log_totals,
        hidden_one,
        moe_in,
        gates,
        targets,
        shared_total,
        grad_moe_in,
        returned_grads,
        owner_res,
        qkv_weight,
        out_weight,
        out_bias,
        router_turned,
        ada_weight,
        grad_sup_bias,
        grad_sdown_bias,
        side,
        part,
        wire,
        grad_eup,
        grad_edown,
    )
    if small:
        gathered = (full_a, full_b, last_rows, notes, up_rows, down_rows, side_rows)
        (
            sum_time,
            sum_label,
            sum_ada,
            sum_ada_bias,
            sum_qkv,
            sum_out_weight,
            sum_out_bias,
            sum_router,
            sum_eup,
            sum_eup_bias,
            sum_edown,
            sum_edown_bias,
            sum_sup,
            sum_sup_bias,
            sum_sdown,
            sum_sdown_bias,
        ) = finish(
            gathered, time_table, label_table, expert_count, width, hidden, nets, dp_count
        )
    else:
        up_blocks = exchange(grad_eup.reshape(outer, width // outer, hidden), "p0")
        up_part = sum_blocks(up_blocks).astype(BF16).reshape(-1, width // dp_count, hidden)
        sum_eup = exchange(up_part, ("p1", "p2")).astype(F32)
        down_blocks = exchange(grad_edown.reshape(outer, hidden // outer, width), "p0")
        down_part = sum_blocks(down_blocks).astype(BF16).reshape(-1, hidden // dp_count, width)
        sum_edown = exchange(down_part, ("p1", "p2")).astype(F32)
        sides = lax.psum(side.astype(F32), "p0")
        sides = spread(sides, ("p1", "p2"))
        sides = sides.reshape(sides.shape[0], -1)
        side_up = sides[:, :hidden]
        side_down = sides[:, hidden : hidden + width]

        shared_sums = sum_everywhere(wire.reshape(-1, hidden)).astype(F32)
        shared_sums = shared_sums.reshape((2, nets, width, hidden))
        sum_sup = shared_sums[0]
        sum_sdown = shared_sums[1].transpose(0, 2, 1)

        note = notes[0, 0, 0, 0]
        all_rows = spread(jnp.concatenate([note[:8], note[8:]], axis=1), ALL)
        all_rows = all_rows.reshape(-1, 2 * note.shape[1])
        all_modulation = all_rows[:, : 6 * width]
        all_condition = all_rows[:, 6 * width : 7 * width]
        marks = all_rows[:, 7 * width : 7 * width + 4].astype(jnp.int32)
        label_ids = jnp.arange(label_table.shape[0], dtype=jnp.int32)
        label_hot = ((marks[:, 0:1] * 32 + marks[:, 1:2]) == label_ids).astype(BF16)
        time_ids = jnp.arange(time_table.shape[0], dtype=jnp.int32)
        time_hot = ((marks[:, 2:3] * 32 + marks[:, 3:4]) == time_ids).astype(BF16)
        all_act = jax.nn.silu(
            jnp.dot(label_hot, label_table, preferred_element_type=F32)
            + jnp.dot(time_hot, time_table, preferred_element_type=F32)
        ).astype(BF16)
        sum_ada = lax.dot_general(all_act, all_modulation, ROWS_FIRST, preferred_element_type=F32)
        sum_ada_bias = jnp.sum(all_modulation.astype(F32), axis=0)
        sum_label = lax.dot_general(
            label_hot, all_condition, ROWS_FIRST, preferred_element_type=F32
        )
        sum_time = lax.dot_general(time_hot, all_condition, ROWS_FIRST, preferred_element_type=F32)

        last = jnp.concatenate([last_rows[0], last_rows[1]], axis=1)
        last = sum_everywhere(last).astype(F32)
        sum_qkv = last[:width, : 3 * width]
        sum_out_weight = last[:width, 3 * width :]
        rest = last[width:]
        sum_eup_bias = lax.dynamic_slice_in_dim(
            side_up, dp_here * (hidden // dp_count), hidden // dp_count, 1
        )
        sum_edown_bias = lax.dynamic_slice_in_dim(
            side_down, dp_here * (width // dp_count), width // dp_count, 1
        )
        sum_router = rest[:expert_count, :width].T
        sum_sup_bias = rest[expert_count : expert_count + nets]
        sum_out_bias = rest[expert_count + nets, :width]
        sum_sdown_bias = jnp.broadcast_to(
            rest[expert_count + nets, width : 2 * width][None], (nets, width)
        )
    return (
        layer_out,
        grad_tokens,
        rms_row[:, :2],
        sum_time,
        sum_label,
        sum_ada,
        sum_ada_bias,
        sum_qkv,
        sum_out_weight,
        sum_out_bias,
        sum_router,
        sum_eup,
        sum_eup_bias,
        sum_edown,
        sum_edown_bias,
        sum_sup,
        sum_sup_bias,
        sum_sdown,
        sum_sdown_bias,
    )


def solution(mesh):
    dp_count = mesh.shape["dp"]
    owners = mesh.shape["expert"]
    split = Mesh(mesh.devices.reshape(dp_count // 4, 2, 2, owners), ALL)
    dp = ("p0", "p1", "p2")
    in_specs = (
        P(ALL, None),
        P(ALL, None),
        P(ALL, None),
        P(ALL),
        P(ALL, None),
        P(ALL, None, None),
        P(),
        P(),
        P(),
        P(),
        P(),
        P(),
        P(),
        P(),
        P("expert", None, None),
        P("expert", None),
        P("expert", None, None),
        P("expert", None),
        P(),
        P(),
        P(),
        P(),
    )
    out_specs = (
        P(ALL, None),
        P(ALL, None),
        P(ALL, None),
        P(),
        P(),
        P(),
        P(),
        P(),
        P(),
        P(),
        P(),
        P("expert", dp, None),
        P("expert", dp),
        P("expert", dp, None),
        P("expert", dp),
        P(),
        P(),
        P(),
        P(),
    )
    return jax.shard_map(body, mesh=split, in_specs=in_specs, out_specs=out_specs, check_vma=False)
```

```python
import functools

import jax
import jax.numpy as jnp
from jax import lax
from jax.experimental import pallas as pl
from jax.experimental.pallas import tpu as pltpu
from jax.sharding import Mesh, PartitionSpec as P

HEADS = 6
HDIM = 64
CAP = 160
PAD = 16
WINDOW = 192
BLOCK = 128
SPAN = BLOCK + 2 * WINDOW
TILE = 256
NORM_EPS = 1e-06
MASK_FILL = -1e30
ROWS_FIRST = (((0,), (0,)), ((), ()))
ROWS_LAST = (((1,), (1,)), ((), ()))
GELU_C = 0.7978845608028654
GELU_K = 0.044715
ALL = ("p0", "p1", "p2", "expert")
GROUP = ("p1", "p2", "expert")
MESH = pl.DeviceIdType.MESH
F32 = jnp.float32
BF16 = jnp.bfloat16
VMEM_BYTES = 56 * 2**20


def norm_rows(matrix):
    row_mean = jnp.mean(matrix, axis=-1, keepdims=True)
    centred = matrix - row_mean
    row_var = jnp.mean(centred * centred, axis=-1, keepdims=True)
    row_scale = lax.rsqrt(row_var + NORM_EPS)
    return (centred * row_scale, row_scale)


def norm_back(grad_in, normed, row_scale):
    grad_mean = jnp.mean(grad_in, axis=-1, keepdims=True)
    cross_mean = jnp.mean(grad_in * normed, axis=-1, keepdims=True)
    return (grad_in - grad_mean - normed * cross_mean) * row_scale


def high_low(values):
    high = values.astype(BF16)
    return (high, (values - high.astype(F32)).astype(BF16))


def iota(shape, dim):
    return lax.broadcasted_iota(jnp.int32, shape, dim)


def dot(left, right):
    return jnp.dot(left, right, preferred_element_type=F32)


def dot_t(left, right):
    return lax.dot_general(left, right, ROWS_LAST, preferred_element_type=F32)


def in_vmem():
    return pl.BlockSpec(memory_space=pltpu.VMEM)


def in_smem():
    return pl.BlockSpec(memory_space=pltpu.SMEM)


def anywhere():
    return pl.BlockSpec(memory_space=pl.ANY)


def like(shape, dtype):
    return jax.ShapeDtypeStruct(shape, dtype)


def image_bounds(counts_ref):
    bounds = []
    start = 0
    for image in range(counts_ref.shape[1]):
        end = start + counts_ref[0, image]
        bounds.append((start, end))
        start = end
    return bounds


def member_block(bounds, first, rows):
    lane = iota((1, 128), 1)
    low = jnp.zeros((1, 128), jnp.int32)
    high = jnp.zeros((1, 128), jnp.int32)
    for image, (start, end) in enumerate(bounds):
        hit = (lane == image) | (lane == 8 + image)
        low = jnp.where(hit, start, low)
        high = jnp.where(hit, end, high)
    slot = first + iota((rows, 128), 0)
    return ((slot >= low) & (slot < high)).astype(F32).astype(BF16)


def stack_modulation(mod, stack):
    high, low = high_low(mod)
    stack[...] = jnp.zeros_like(stack)
    stack[0:16, :] = jnp.concatenate([high.astype(F32), low.astype(F32)], axis=0).astype(BF16)


def segments(bounds, slot):
    total = bounds[-1][1]
    image = jnp.zeros(slot.shape, jnp.int32)
    for _, end in bounds[:-1]:
        image = image + (slot >= end).astype(jnp.int32)
    image = jnp.where(slot >= total, len(bounds) + slot, image)
    return jnp.where(slot < 0, -1, image)


def front_kernel(
    owners,
    local_count,
    counts_ref,
    labels_ref,
    time_ref,
    routes_ref,
    time_table_ref,
    label_table_ref,
    ada_ref,
    ada_bias_ref,
    cot_ref,
    mod_ref,
    cond_ref,
    act_ref,
    pos_ref,
    tgt_ref,
    gb_ref,
    rows_ref,
    stack,
    hot,
    lines,
):
    slots, width = cot_ref.shape
    experts = owners * local_count
    bounds = image_bounds(counts_ref)
    total = bounds[-1][1]

    label_count = label_table_ref.shape[0]
    time_count = time_table_ref.shape[0]
    row = iota((8, label_count), 0)
    wanted = jnp.full((8, label_count), -1, jnp.int32)
    for image in range(len(bounds)):
        wanted = jnp.where(row == image, labels_ref[0, image], wanted)
    label_hot = (iota((8, label_count), 1) == wanted).astype(F32).astype(BF16)
    time_hot = (iota((8, time_count), 1) == time_ref[0]).astype(F32).astype(BF16)
    condition = dot(label_hot, label_table_ref[...]) + dot(time_hot, time_table_ref[...])
    act = (condition / (1.0 + jnp.exp(-condition))).astype(BF16)
    mod = dot(act, ada_ref[...]) + ada_bias_ref[...].reshape(1, -1)
    cond_ref[...] = condition
    act_ref[...] = act
    mod_ref[...] = mod
    stack_modulation(mod[:, 5 * width :], stack)

    first = routes_ref[0:1, :]
    second = routes_ref[1:2, :]
    expert = iota((experts, slots), 0)
    valid = iota((experts, slots), 1) < total
    hit_first = (first == expert) & valid
    hit_second = (second == expert) & valid
    picks = (hit_first | hit_second).astype(F32)
    earlier = (iota((128, 128), 0) < iota((128, 128), 1)).astype(F32).astype(BF16)
    carry = jnp.zeros((experts, 1), F32)
    parts = []
    for lane in range(0, slots, 128):
        part = picks[:, lane : lane + 128]
        parts.append(dot(part.astype(BF16), earlier) + carry)
        carry = carry + jnp.sum(part, axis=1, keepdims=True)
    place = jnp.concatenate(parts, axis=1)
    pos_ref[...] = jnp.where(picks > 0.0, place, -1.0)
    base = (expert % local_count) * owners + expert // local_count
    slot_of = (base * CAP).astype(F32) + place
    lines[...] = jnp.full(lines.shape, -1.0, F32)
    lines[0:1, :] = jnp.sum(jnp.where(hit_first, slot_of + 1.0, 0.0), axis=0, keepdims=True) - 1.0
    lines[1:2, :] = jnp.sum(jnp.where(hit_second, slot_of + 1.0, 0.0), axis=0, keepdims=True) - 1.0
    tgt_ref[...] = lines[...].T

    def gradient(i, carry):
        r = pl.ds(pl.multiple_of(i * TILE, TILE), TILE)
        gate = dot(member_block(bounds, i * TILE, TILE), stack[...])
        gb_ref[r, :] = (gate * cot_ref[r, :].astype(F32)).astype(BF16)
        return carry

    lax.fori_loop(0, slots // TILE, gradient, 0)
    row = iota((CAP, slots), 0).astype(F32)
    for j in range(experts):
        expert = (j % owners) * local_count + j // owners
        line = pos_ref[expert : expert + 1, :]
        hot[...] = (row == line).astype(F32).astype(BF16)
        rows_ref[j] = dot(hot[...], gb_ref[...]).astype(BF16)


def attention_kernel(
    owners,
    local_count,
    counts_ref,
    tokens_ref,
    mod_ref,
    qkv_w_ref,
    out_w_ref,
    out_b_ref,
    router_ref,
    routes_ref,
    pos_ref,
    qkv_ref,
    att_ref,
    lse_ref,
    hidden_ref,
    moe_ref,
    gates_ref,
    send_ref,
    stack,
    values_t,
    hot,
    lines,
    columns,
):
    slots, width = tokens_ref.shape
    experts = owners * local_count
    padded = qkv_ref.shape[0]
    bounds = image_bounds(counts_ref)
    stack_modulation(mod_ref[...], stack)
    scale = HDIM ** (-0.5)

    def part(member, index):
        return dot(member, stack[:, index * width : (index + 1) * width])

    qkv_ref[0:WINDOW, :] = jnp.zeros((WINDOW, 3 * width), BF16)
    qkv_ref[padded - WINDOW :, :] = jnp.zeros((WINDOW, 3 * width), BF16)

    def project(i, carry):
        r = pl.ds(pl.multiple_of(i * TILE, TILE), TILE)
        member = member_block(bounds, i * TILE, TILE)
        normed, _ = norm_rows(tokens_ref[r, :].astype(F32))
        mixed = (normed * (1.0 + part(member, 1)) + part(member, 0)).astype(BF16)
        to = pl.ds(pl.multiple_of(i * TILE + WINDOW, 64), TILE)
        qkv_ref[to, :] = dot(mixed, qkv_w_ref[...]).astype(BF16)
        return carry

    lax.fori_loop(0, slots // TILE, project, 0)
    for r in range(0, padded, BLOCK):
        values_t[:, r : r + BLOCK] = qkv_ref[r : r + BLOCK, 2 * width :].T

    first_half = iota((BLOCK, 128), 1) < HDIM

    def attend(i, carry):
        q_rows = pl.ds(pl.multiple_of(i * BLOCK + WINDOW, 64), BLOCK)
        k_rows = pl.ds(pl.multiple_of(i * BLOCK, BLOCK), SPAN)
        o_rows = pl.ds(pl.multiple_of(i * BLOCK, BLOCK), BLOCK)
        key_segment = segments(bounds, i * BLOCK - WINDOW + iota((SPAN, BLOCK), 0))
        query_segment = segments(bounds, i * BLOCK + iota((1, BLOCK), 1))
        allowed = key_segment == query_segment
        allowed = jnp.concatenate([allowed, allowed], axis=1)
        for pair in range(HEADS // 2):
            lanes = slice(pair * 128, (pair + 1) * 128)
            q = qkv_ref[q_rows, lanes]
            k = qkv_ref[k_rows, width + pair * 128 : width + (pair + 1) * 128]
            zero = jnp.zeros_like(q)
            q = jnp.concatenate(
                [jnp.where(first_half, q, zero), jnp.where(first_half, zero, q)], axis=0
            )
            scores = jnp.where(allowed, dot_t(k, q) * scale, MASK_FILL)
            top = jnp.max(scores, axis=0, keepdims=True)
            expo = jnp.exp(scores - top)
            total = jnp.sum(expo, axis=0, keepdims=True)
            out = dot(values_t[lanes, k_rows], expo.astype(BF16)) / total
            out = jnp.concatenate([out[:HDIM, :BLOCK], out[HDIM:, BLOCK:]], axis=0)
            att_ref[o_rows, lanes] = out.T.astype(BF16)
            log_total = top + jnp.log(total)
            lse_ref[2 * pair : 2 * pair + 1, o_rows] = log_total[:, :BLOCK]
            lse_ref[2 * pair + 1 : 2 * pair + 2, o_rows] = log_total[:, BLOCK:]
        return carry

    lax.fori_loop(0, slots // BLOCK, attend, 0)

    def mix(i, carry):
        r = pl.ds(pl.multiple_of(i * TILE, TILE), TILE)
        member = member_block(bounds, i * TILE, TILE)
        attn_out = dot(att_ref[r, :], out_w_ref[...]) + out_b_ref[...].reshape(1, -1)
        hidden = tokens_ref[r, :].astype(F32) + part(member, 2) * attn_out
        hidden_ref[r, :] = hidden
        normed, _ = norm_rows(hidden)
        moe_ref[r, :] = (normed * (1.0 + part(member, 4)) + part(member, 3)).astype(BF16)
        return carry

    lax.fori_loop(0, slots // TILE, mix, 0)

    logits = dot_t(router_ref[...], moe_ref[...])
    expert = iota((experts, slots), 0)
    chosen = (routes_ref[0:1, :] == expert) | (routes_ref[1:2, :] == expert)
    top = jnp.max(jnp.where(chosen, logits, MASK_FILL), axis=0, keepdims=True)
    expo = jnp.where(chosen, jnp.exp(logits - top), 0.0)
    gates_ref[...] = expo / jnp.sum(expo, axis=0, keepdims=True)

    row = iota((CAP, slots), 0).astype(F32)
    lane = iota((CAP, 128), 1)
    table = jnp.zeros((CAP, 128), F32)
    for j in range(experts):
        expert = (j % owners) * local_count + j // owners
        match = row == pos_ref[expert : expert + 1, :]
        hot[...] = match.astype(F32).astype(BF16)
        gate = jnp.sum(
            jnp.where(match, gates_ref[expert : expert + 1, :], 0.0), axis=1, keepdims=True
        )
        table = jnp.where(lane == j, gate, table)
        send_ref[j, :CAP, :] = dot(hot[...], moe_ref[...]).astype(BF16)
    columns[...] = jnp.zeros_like(columns)
    columns[:CAP, :] = table
    lines[...] = columns[...].T
    for j in range(experts):
        send_ref[j, CAP:, :] = tail_rows(lines[j : j + 1, :], width)


def tail_rows(line, width):
    high = line.astype(BF16).astype(F32)
    row = iota((PAD, line.shape[1]), 0)
    tail = jnp.where(row == 0, high, jnp.where(row == 1, line - high, 0.0))
    rest = jnp.zeros((PAD, width - line.shape[1]), F32)
    return jnp.concatenate([tail, rest], axis=1).astype(BF16)


def forward_kernel(owners, local_count, *refs):
    (
        counts_ref,
        labels_ref,
        time_ref,
        routes_ref,
        time_table_ref,
        label_table_ref,
        ada_ref,
        ada_bias_ref,
        cot_ref,
        tokens_ref,
        qkv_w_ref,
        out_w_ref,
        out_b_ref,
        router_ref,
        mod_ref,
        cond_ref,
        tgt_ref,
        gb_ref,
        owner_ref,
        qkv_ref,
        att_ref,
        lse_ref,
        hidden_ref,
        moe_ref,
        gates_ref,
        send_ref,
        act,
        pos,
        rows,
        small_stack,
        tall_lines,
        stack,
        values_t,
        hot,
        lines,
        columns,
        send_sems,
        recv_sems,
        own_sem,
    ) = refs
    offsets = group_offsets(owners)
    partners = [group_partner(owners, *offset)[0] for offset in offsets if any(offset)]
    barrier = pltpu.get_barrier_semaphore()
    for device in partners:
        pl.semaphore_signal(barrier, inc=1, device_id=device, device_id_type=MESH)
    front_kernel(
        owners,
        local_count,
        counts_ref,
        labels_ref,
        time_ref,
        routes_ref,
        time_table_ref,
        label_table_ref,
        ada_ref,
        ada_bias_ref,
        cot_ref,
        mod_ref,
        cond_ref,
        act,
        pos,
        tgt_ref,
        gb_ref,
        rows,
        small_stack,
        hot,
        tall_lines,
    )
    pl.semaphore_wait(barrier, len(partners))
    copies = [
        group_copy(owners, index, offset, rows, owner_ref, send_sems, recv_sems)
        for index, offset in enumerate(offsets)
        if any(offset)
    ]
    for copy in copies:
        copy.start()
    _, me = group_partner(owners, 0, 0, 0)
    own = pltpu.make_async_copy(rows.at[me], owner_ref.at[me], own_sem)
    own.start()
    attention_kernel(
        owners,
        local_count,
        counts_ref,
        tokens_ref,
        mod_ref,
        qkv_w_ref,
        out_w_ref,
        out_b_ref,
        router_ref,
        routes_ref,
        pos,
        qkv_ref,
        att_ref,
        lse_ref,
        hidden_ref,
        moe_ref,
        gates_ref,
        send_ref,
        stack,
        values_t,
        hot,
        lines,
        columns,
    )
    own.wait()
    finish_all(copies)


def forward(owners, experts, *args):
    tokens = args[9]
    slots, width = tokens.shape
    padded = slots + 2 * WINDOW
    rows = (experts, CAP, width)
    return pl.pallas_call(
        functools.partial(forward_kernel, owners, experts // owners),
        in_specs=[in_smem()] * 3 + [in_vmem()] * (len(args) - 3),
        out_specs=[in_vmem()] * 4 + [anywhere()] + [in_vmem()] * 7,
        out_shape=[
            like((8, 6 * width), F32),
            like((8, width), F32),
            like((slots, 128), F32),
            like((slots, width), BF16),
            like(rows, BF16),
            like((padded, 3 * width), BF16),
            like((slots, width), BF16),
            like((8, slots), F32),
            like((slots, width), F32),
            like((slots, width), BF16),
            like((experts, slots), F32),
            like((experts, CAP + PAD, width), BF16),
        ],
        scratch_shapes=[
            pltpu.VMEM((8, width), BF16),
            pltpu.VMEM((experts, slots), F32),
            pltpu.VMEM(rows, BF16),
            pltpu.VMEM((128, width), BF16),
            pltpu.VMEM((128, slots), F32),
            pltpu.VMEM((128, 6 * width), BF16),
            pltpu.VMEM((width, padded), BF16),
            pltpu.VMEM((CAP, slots), BF16),
            pltpu.VMEM((128, 256), F32),
            pltpu.VMEM((256, 128), F32),
            pltpu.SemaphoreType.DMA((experts,)),
            pltpu.SemaphoreType.DMA((experts,)),
            pltpu.SemaphoreType.DMA,
        ],
        compiler_params=pltpu.CompilerParams(
            vmem_limit_bytes=VMEM_BYTES, collective_id=5, has_side_effects=True
        ),
        name="forward",
    )(*args)


def axes_here():
    return [lax.axis_index(name) for name in ALL]


def group_partner(owners, a, b, c):
    zero, one, two, three = axes_here()
    first = lax.rem(one + a, 2)
    second = lax.rem(two + b, 2)
    third = lax.rem(three + c, owners)
    return (zero, first, second, third), (first * 2 + second) * owners + third


def group_offsets(owners):
    offsets = [(a, b, c) for a in range(2) for b in range(2) for c in range(owners)]
    return sorted(offsets, key=lambda o: -(o[0] + o[1] + (2 * o[2] >= owners)))


def sibling():
    zero, one, two, three = axes_here()
    odd = lax.rem(three, 2)
    return (zero, one, two, three + 1 - 2 * odd)


def plane_partner(b, h):
    zero, one, two, three = axes_here()
    odd = lax.rem(three, 2)
    second = lax.rem(two + b, 2)
    half = lax.rem(three // 2 + h, 2)
    return (zero, one, second, half * 2 + odd), second, half


def line_partner(a, b):
    zero, one, two, three = axes_here()
    first = lax.rem(zero + a, 2)
    second = lax.rem(one + b, 2)
    return (first, second, two, three), first * 2 + second


def owner_partner(a, b):
    zero, one, two, three = axes_here()
    first = lax.rem(one + a, 2)
    second = lax.rem(two + b, 2)
    return (zero, first, second, three), first * 2 + second


def column_partner(a, b, c):
    zero, one, two, three = axes_here()
    first = lax.rem(zero + a, 2)
    second = lax.rem(one + b, 2)
    third = lax.rem(two + c, 2)
    return (first, second, third, three), (first * 2 + second) * 2 + third


OTHERS = [(1, 1), (0, 1), (1, 0)]
COLUMN = [(1, 1, 1), (1, 1, 0), (1, 0, 1), (1, 0, 0), (0, 1, 1), (0, 1, 0), (0, 0, 1)]


def greet(devices):
    barrier = pltpu.get_barrier_semaphore()
    for device in devices:
        pl.semaphore_signal(barrier, inc=1, device_id=device, device_id_type=MESH)
    pl.semaphore_wait(barrier, len(devices))


def push(source, target, send_sem, recv_sem, device):
    copy = pltpu.make_async_remote_copy(
        src_ref=source,
        dst_ref=target,
        send_sem=send_sem,
        recv_sem=recv_sem,
        device_id=device,
        device_id_type=MESH,
    )
    copy.start()
    return copy


def finish_all(copies):
    for copy in copies:
        copy.wait()


def group_copy(owners, index, offsets, source, target, send_sems, recv_sems):
    device, place = group_partner(owners, *offsets)
    _, me = group_partner(owners, 0, 0, 0)
    return pltpu.make_async_remote_copy(
        src_ref=source.at[place],
        dst_ref=target.at[me],
        send_sem=send_sems.at[index],
        recv_sem=recv_sems.at[index],
        device_id=device,
        device_id_type=MESH,
    )


def gelu_parts(pre, grad):
    square = pre * pre
    th = jnp.tanh(pre * (GELU_C + (GELU_C * GELU_K) * square))
    half = 0.5 + 0.5 * th
    slope = half + (0.5 * pre) * (1.0 - th * th) * (GELU_C + (3 * GELU_C * GELU_K) * square)
    return (pre * half).astype(BF16), (grad * slope).astype(BF16)


def shared_kernel(
    owners,
    reduce,
    x_ref,
    g_ref,
    up_ref,
    bu_ref,
    dn_ref,
    bd_ref,
    rows_ref,
    y_ref,
    dx_ref,
    wire_ref,
    dbu_ref,
    dbd_ref,
    owner_ref,
    xt,
    gt,
    send_sems,
    recv_sems,
    own_sem,
    wire,
    got,
    swap_sends,
    swap_recvs,
):
    net = pl.program_id(0)
    chunk = pl.program_id(1)
    rows, width = x_ref.shape
    lanes = up_ref.shape[2]
    offsets = group_offsets(owners)
    odd = lax.rem(lax.axis_index("expert"), 2)

    def swap(n, h):
        here = pl.ds(pl.multiple_of(h * lanes, 128), lanes)
        step = n * (wire.shape[3] // lanes) + h
        return pltpu.make_async_remote_copy(
            src_ref=wire.at[1 - odd, n, :, here],
            dst_ref=got.at[n, :, here],
            send_sem=swap_sends.at[step],
            recv_sem=swap_recvs.at[step],
            device_id=sibling(),
            device_id_type=MESH,
        )

    copies = [
        group_copy(owners, index, offset, rows_ref, owner_ref, send_sems, recv_sems)
        for index, offset in enumerate(offsets)
        if any(offset)
    ]
    _, me = group_partner(owners, 0, 0, 0)
    own = pltpu.make_async_copy(rows_ref.at[me], owner_ref.at[me], own_sem)

    @pl.when((net == 0) & (chunk == 0))
    def _():
        greet([group_partner(owners, *offset)[0] for offset in offsets if any(offset)])
        own.start()
        for copy in copies:
            copy.start()
        for r in range(0, rows, 256):
            xt[:width, r : r + 256] = x_ref[r : r + 256, :].T
            gt[:, r : r + 256] = g_ref[r : r + 256, :].T
        xt[width:, :] = jnp.ones((xt.shape[0] - width, rows), BF16)
        y_ref[...] = jnp.zeros_like(y_ref)
        dx_ref[...] = jnp.zeros_like(dx_ref)
        dbd_ref[...] = jnp.sum(g_ref[...].astype(F32), axis=0, keepdims=True)

    up = up_ref[0]
    dn = dn_ref[0]
    bias = bu_ref[pl.ds(net, 1), pl.ds(pl.multiple_of(chunk * lanes, 128), lanes)]
    pre = dot(x_ref[...], up) + bias
    act, dpre = gelu_parts(pre, dot_t(g_ref[...], dn))
    y_ref[...] += dot(act, dn)
    dx_ref[...] += dot_t(dpre, up)
    dup = dot(xt[...], dpre)
    here = pl.ds(pl.multiple_of(chunk * lanes, 128), lanes)
    wire[0, net, :, here] = dup[:width].astype(BF16)
    dbu_ref[0] = dup[width : width + 1]
    wire[1, net, :, here] = dot(gt[...], act).astype(BF16)
    if reduce:
        swap(net, chunk).start()

    @pl.when((net == pl.num_programs(0) - 1) & (chunk == pl.num_programs(1) - 1))
    def _():
        y_ref[...] += jnp.sum(bd_ref[...], axis=0, keepdims=True)
        if reduce:
            for n in range(wire.shape[1]):
                for h in range(wire.shape[3] // lanes):
                    swap(n, h).wait()
                    place = slice(h * lanes, (h + 1) * lanes)
                    for r in range(0, width, 64):
                        line = slice(r, r + 64)
                        summed = wire[odd, n, line, place].astype(F32) + got[n, line, place].astype(F32)
                        wire_ref[n, line, place] = summed.astype(BF16)
        else:
            wire_ref[...] = wire[...].reshape(wire_ref.shape)
        own.wait()
        for copy in copies:
            copy.wait()


def shared_nets(owners, reduce, x, g, up, bias_up, down, bias_down, rows_out, chunk=768):
    nets, width, hidden = up.shape
    rows = x.shape[0]
    count = rows_out.shape[0]
    kept = nets if reduce else 2 * nets
    steps = nets * (hidden // chunk)

    def whole(shape):
        return pl.BlockSpec(shape, lambda n, h: (0,) * len(shape))

    return pl.pallas_call(
        functools.partial(shared_kernel, owners, reduce),
        grid=(nets, hidden // chunk),
        in_specs=[
            whole(x.shape),
            whole(g.shape),
            pl.BlockSpec((1, width, chunk), lambda n, h: (n, 0, h)),
            whole((nets, hidden)),
            pl.BlockSpec((1, chunk, width), lambda n, h: (n, h, 0)),
            whole((nets, width)),
            anywhere(),
        ],
        out_specs=[
            whole((rows, width)),
            whole((rows, width)),
            whole((kept, width, hidden)),
            pl.BlockSpec((1, 1, chunk), lambda n, h: (n, 0, h)),
            whole((1, width)),
            anywhere(),
        ],
        out_shape=[
            like((rows, width), F32),
            like((rows, width), F32),
            like((kept, width, hidden), BF16),
            like((nets, 1, hidden), F32),
            like((1, width), F32),
            like(rows_out.shape, BF16),
        ],
        scratch_shapes=[
            pltpu.VMEM((width + 16, rows), BF16),
            pltpu.VMEM((width, rows), BF16),
            pltpu.SemaphoreType.DMA((count,)),
            pltpu.SemaphoreType.DMA((count,)),
            pltpu.SemaphoreType.DMA,
            pltpu.VMEM((2, nets, width, hidden), BF16),
            pltpu.VMEM((nets, width, hidden), BF16),
            pltpu.SemaphoreType.DMA((steps,)),
            pltpu.SemaphoreType.DMA((steps,)),
        ],
        compiler_params=pltpu.CompilerParams(
            vmem_limit_bytes=VMEM_BYTES, collective_id=1, has_side_effects=True
        ),
        name="shared_nets",
    )(x, g, up, bias_up, down, bias_down, rows_out)


def routed_kernel(
    owners,
    reduce,
    x_ref,
    g_ref,
    up_any,
    bu_ref,
    dn_any,
    bd_ref,
    wire_any,
    y_ref,
    dup_ref,
    ddn_ref,
    side_ref,
    back_ref,
    part_ref,
    up,
    dn,
    xt,
    gt,
    acts,
    dpres,
    outgoing,
    lines,
    columns,
    load_sems,
    send_sems,
    recv_sems,
    own_sem,
    mine,
    pieces,
    keep_sem,
    sum_sends,
    sum_recvs,
    bias_line,
):
    width, hidden = up.shape
    chunk = 768
    pick = lax.axis_index("p1") * 2 + lax.axis_index("p2")
    loads = [
        pltpu.make_async_copy(up_any.at[pick], up, load_sems.at[0]),
        pltpu.make_async_copy(dn_any.at[pick], dn, load_sems.at[1]),
    ]
    for load in loads:
        load.start()
    offsets = group_offsets(owners)
    places = [group_partner(owners, *offset)[1] for offset in offsets]
    near = [group_partner(owners, *offset)[0] for offset in offsets if any(offset)]
    greet(near)
    copies = [
        group_copy(owners, index, offset, outgoing, back_ref, send_sems, recv_sems)
        if any(offset)
        else pltpu.make_async_copy(outgoing.at[places[index]], back_ref.at[places[index]], own_sem)
        for index, offset in enumerate(offsets)
    ]
    sums = []
    if reduce:
        _, own_net, own_half = plane_partner(0, 0)
        size = width // 2
        for index, (b, h) in enumerate(OTHERS):
            device, net, half = plane_partner(b, h)
            source = wire_any.at[net, pl.ds(half * size, size), pl.ds(0, hidden // 2)]
            sums.append(
                push(source, pieces.at[index], sum_sends.at[index], sum_recvs.at[index], device)
            )
        take = pltpu.make_async_copy(
            wire_any.at[own_net, pl.ds(own_half * size, size), pl.ds(0, hidden // 2)], mine, keep_sem
        )
        take.start()

    lines[...] = jnp.zeros_like(lines)
    for index, place in enumerate(places):
        tail = x_ref[place, CAP:, :256].astype(F32)
        lines[index : index + 1, :] = tail[0:1] + tail[1:2]
    columns[...] = lines[...].T
    gates = columns[:CAP, :]
    for load in loads:
        load.wait()
    bu = bu_ref[pl.ds(pick, 1), :]
    bd = bd_ref[pl.ds(pick, 1), :]
    lane = iota((CAP, 128), 1)
    group = owners
    size = group * CAP
    xt[width:, :] = jnp.ones((xt.shape[0] - width, xt.shape[1]), BF16)
    dbd = jnp.zeros((1, width), F32)
    for first in range(0, len(offsets), group):
        members = range(first, first + group)
        span = slice(first * CAP, first * CAP + size)
        x = jnp.concatenate([x_ref[places[k], :CAP, :] for k in members], axis=0)
        raw = [g_ref[places[k]].astype(F32) for k in members]
        g = jnp.concatenate([raw[k - first] * gates[:, k : k + 1] for k in members], axis=0)
        g = g.astype(BF16)
        dbd = dbd + jnp.sum(g.astype(F32), axis=0, keepdims=True)
        xt[:width, span] = x.T
        gt[:, span] = g.T
        y = jnp.zeros((size, width), F32)
        dx = jnp.zeros((size, width), F32)
        for h in range(0, hidden, chunk):
            pre = dot(x, up[:, h : h + chunk]) + bu[:, h : h + chunk]
            act, dpre = gelu_parts(pre, dot_t(g, dn[h : h + chunk, :]))
            acts[span, h : h + chunk] = act
            dpres[span, h : h + chunk] = dpre
            y = y + dot(act, dn[h : h + chunk, :])
            dx = dx + dot_t(dpre, up[:, h : h + chunk])
        table = jnp.zeros((CAP, 128), F32)
        for k in members:
            r = slice((k - first) * CAP, (k - first + 1) * CAP)
            res = (y[r] + bd).astype(BF16).astype(F32)
            y_ref[places[k]] = (res * gates[:, k : k + 1]).astype(BF16)
            inner = jnp.sum(res * raw[k - first], axis=1, keepdims=True)
            table = jnp.where(lane == k - first, inner, table)
            outgoing[places[k], :CAP, :] = dx[r].astype(BF16)
        columns[:CAP, :] = table
        lines[...] = columns[...].T
        for k in members:
            outgoing[places[k], CAP:, :] = tail_rows(lines[k - first : k - first + 1, :], width)
            copies[k].start()
    bias_line[...] = jnp.zeros_like(bias_line)
    for k in range(width // 128):
        bias_line[hidden // 128 + k : hidden // 128 + k + 1, :] = dbd[:, k * 128 : (k + 1) * 128]
    for h in range(0, hidden, 512):
        dup = dot(xt[...], dpres[:, h : h + 512])
        dup_ref[:, h : h + 512] = dup[:width].astype(BF16)
        for k in range(4):
            bias_line[h // 128 + k : h // 128 + k + 1, :] = dup[
                width : width + 1, k * 128 : (k + 1) * 128
            ]
        ddn_ref[h : h + 512, :] = dot(gt[...], acts[:, h : h + 512]).T.astype(BF16)
    side_ref[...] = bias_line[...].astype(BF16)
    if reduce:
        take.wait()
        finish_all(sums)
        summed = mine[...].astype(F32)
        for index in range(len(OTHERS)):
            summed = summed + pieces[index].astype(F32)
        part_ref[...] = summed.astype(BF16)
    finish_all(copies)


def routed_net(owners, reduce, x, g, up, bias_up, down, bias_down, wire):
    count = x.shape[0]
    rows = count * CAP
    width, hidden = up.shape[1:]
    piece = (width // 2, hidden // 2) if reduce else (16, 128)
    return pl.pallas_call(
        functools.partial(routed_kernel, owners, reduce),
        in_specs=[in_vmem(), in_vmem(), anywhere(), in_vmem(), anywhere(), in_vmem(), anywhere()],
        out_specs=[in_vmem()] * 4 + [anywhere(), in_vmem()],
        out_shape=[
            like((count, CAP, width), BF16),
            like((width, hidden), BF16),
            like((hidden, width), BF16),
            like((16, 128), BF16),
            like((count, CAP + PAD, width), BF16),
            like(piece, BF16),
        ],
        scratch_shapes=[
            pltpu.VMEM((width, hidden), BF16),
            pltpu.VMEM((hidden, width), BF16),
            pltpu.VMEM((width + 16, rows), BF16),
            pltpu.VMEM((width, rows), BF16),
            pltpu.VMEM((rows, hidden), BF16),
            pltpu.VMEM((rows, hidden), BF16),
            pltpu.VMEM((count, CAP + PAD, width), BF16),
            pltpu.VMEM((128, 256), F32),
            pltpu.VMEM((256, 128), F32),
            pltpu.SemaphoreType.DMA((2,)),
            pltpu.SemaphoreType.DMA((count,)),
            pltpu.SemaphoreType.DMA((count,)),
            pltpu.SemaphoreType.DMA,
            pltpu.VMEM(piece, BF16),
            pltpu.VMEM((3,) + piece, BF16),
            pltpu.SemaphoreType.DMA,
            pltpu.SemaphoreType.DMA((10,)),
            pltpu.SemaphoreType.DMA((10,)),
            pltpu.VMEM((16, 128), F32),
        ],
        compiler_params=pltpu.CompilerParams(
            vmem_limit_bytes=VMEM_BYTES, collective_id=2, has_side_effects=True
        ),
        name="routed_net",
    )(x, g, up, bias_up, down, bias_down, wire)


def member_rows(bounds, first, rows):
    image = iota((16, rows), 0)
    slot = first + iota((16, rows), 1)
    low = jnp.zeros((16, rows), jnp.int32)
    high = jnp.zeros((16, rows), jnp.int32)
    for index, (start, end) in enumerate(bounds):
        low = jnp.where(image == index, start, low)
        high = jnp.where(image == index, end, high)
    return ((slot >= low) & (slot < high)).astype(F32).astype(BF16)


def backward_kernel(
    owners,
    local_count,
    reduce,
    counts_ref,
    labels_ref,
    time_ref,
    tokens_any,
    cot_ref,
    mod_ref,
    cond_ref,
    qkv_any,
    att_ref,
    lse_ref,
    hidden_ref,
    moe_any,
    gates_ref,
    tgt_ref,
    shared_any,
    dmoe_ref,
    grads_ref,
    res_ref,
    qkv_w_ref,
    out_w_ref,
    out_b_ref,
    router_ref,
    ada_any,
    sup_b_ref,
    sdn_b_ref,
    side_ref,
    part_ref,
    later_any,
    eup_any,
    edn_any,
    layer_ref,
    dtok_ref,
    rms_ref,
    full_a,
    full_b,
    done,
    notes,
    up_got,
    dn_got,
    sides,
    stack,
    hot,
    rows_ext,
    gate_cols,
    ghid,
    gatt,
    kt,
    dkeys,
    dvals,
    dqkv,
    turned,
    dlog,
    sums,
    lines,
    columns,
    router,
    res,
    send_sems,
    recv_sems,
    own_sem,
    load,
    keep,
    got,
    tail_pieces,
    zgot_wide,
    zgot,
    quarter_a,
    next_part,
    quarter_b,
    pieces,
    up_sum,
    up_mine,
    dn_sum,
    dn_mine,
    note_here,
    tokens_ref,
    qkv_ref,
    moe_ref,
    shared_ref,
    ada_ref,
    load_sems,
    sends,
    recvs,
    locals_,
):
    slots, width = tokens_ref.shape
    experts = owners * local_count
    padded = qkv_ref.shape[0]
    blocks = slots // TILE
    offsets = group_offsets(owners)
    zero, one, two, three = axes_here()
    odd = lax.rem(three, 2)
    _, _, half_here = plane_partner(0, 0)
    _, line_here = line_partner(0, 0)
    _, owner_here = owner_partner(0, 0)
    _, column_here = column_partner(0, 0, 0)
    rows, hidden = load.shape[1], 2 * load.shape[2]
    lane_half = hidden // 2
    quarter_rows = rows // 2
    quarter_lanes = lane_half // 2
    up_rows = up_sum.shape[0]
    dn_rows = dn_sum.shape[0]
    half_rows = quarter_a.shape[0]
    line_rows = half_rows // 4
    shared_rows = pl.ds(half_here * half_rows, half_rows)
    own_rows = pl.ds(pl.multiple_of(half_here * half_rows, 64), half_rows)
    own_line = pl.ds(pl.multiple_of(line_here * line_rows, 16), line_rows)
    counter = iter(range(sends.shape[0]))

    def give(source, target, device):
        index = next(counter)
        return push(source, target, sends.at[index], recvs.at[index], device)

    inputs = [
        pltpu.make_async_copy(source, target, load_sems.at[index])
        for index, (source, target) in enumerate(
            [
                (moe_any, moe_ref),
                (qkv_any, qkv_ref),
                (tokens_any, tokens_ref),
                (shared_any, shared_ref),
                (ada_any, ada_ref),
            ]
        )
    ]
    near = [group_partner(owners, *offset)[0] for offset in offsets if any(offset)]
    if reduce:
        near = near + [column_partner(1, b, c)[0] for b in range(2) for c in range(2)]
    greet(near)
    for copy in inputs:
        copy.start()
    _, me = group_partner(owners, 0, 0, 0)
    own = pltpu.make_async_copy(res_ref.at[me], res.at[me], own_sem)
    own.start()
    copies = [
        group_copy(owners, index, offset, res_ref, res, send_sems, recv_sems)
        for index, offset in enumerate(offsets)
        if any(offset)
    ]

    def line_exchange(source_ref, slot):
        started = []
        for index, offset in enumerate(OTHERS):
            device, place = line_partner(*offset)
            source = source_ref.at[pl.ds(place * line_rows, line_rows)]
            started.append(give(source, zgot.at[slot + index], device))
        return started

    def line_spread(source_ref, slot, target):
        summed = source_ref[own_line].astype(F32)
        for index in range(len(OTHERS)):
            summed = summed + zgot[slot + index].astype(F32)
        target[own_line] = summed.astype(BF16)
        here = target.at[pl.ds(line_here * line_rows, line_rows)]
        return [give(here, here, line_partner(*offset)[0]) for offset in OTHERS]

    def swap_part(source_ref, target, k):
        count = target.shape[0] // 4
        source = source_ref.at[pl.ds((1 - zero) * target.shape[0] + k * count, count)]
        return give(source, target.at[pl.ds(k * count, count)], line_partner(1, 0)[0])

    def plane_spread(source_ref, full, index):
        target = full.at[odd, two, shared_rows]
        mine = pltpu.make_async_copy(source_ref, target, locals_.at[index])
        mine.start()
        beside = give(source_ref, target, plane_partner(1, 0)[0])
        return beside, [mine, give(source_ref, target, plane_partner(0, 1)[0])]

    def pass_on(received, block):
        received.wait()
        return give(block, block, plane_partner(0, 1)[0])

    if reduce:
        loads = [
            pltpu.make_async_copy(eup_any.at[pl.ds(zero * up_rows, up_rows)], up_mine, locals_.at[2]),
            pltpu.make_async_copy(edn_any.at[pl.ds(zero * dn_rows, dn_rows)], dn_mine, locals_.at[3]),
        ]
        for copy in loads:
            copy.start()
        line_a = line_exchange(part_ref, 0)
        plane_b = []
        for index, offset in enumerate(OTHERS):
            device, net, half = plane_partner(*offset)
            source = later_any.at[
                net, pl.ds(half * half_rows, half_rows), pl.ds(lane_half, lane_half)
            ]
            plane_b.append(give(source, pieces.at[index], device))
        for copy in copies:
            copy.start()
        across, _ = line_partner(1, 0)
        up_swap = [swap_part(eup_any, up_sum, k) for k in range(2)]
        own_b = pltpu.make_async_copy(later_any.at[two, shared_rows, pl.ds(lane_half, lane_half)], next_part, locals_.at[4])
        own_b.start()
        sides[column_here] = side_ref[...]
        side_all = [give(side_ref, sides.at[column_here], column_partner(*o)[0]) for o in COLUMN]
    else:
        for copy in copies:
            copy.start()
    bounds = image_bounds(counts_ref)
    total = bounds[-1][1]
    scale = HDIM ** (-0.5)
    stack_modulation(mod_ref[...], stack)
    sums[...] = jnp.zeros_like(sums)

    def part(member, index):
        return dot(member, stack[:, index * width : (index + 1) * width])

    def collect(turned_member, index, values):
        sums[:, index * width : (index + 1) * width] += dot(turned_member, values.astype(BF16))

    lines[...] = jnp.zeros_like(lines)
    for j in range(experts):
        tail = grads_ref[j, CAP:, :256].astype(F32)
        lines[j : j + 1, :] = tail[0:1] + tail[1:2]
    columns[...] = lines[...].T
    lane = iota((CAP, 128), 1)
    for j in range(experts):
        expert = (j % owners) * local_count + j // owners
        r = slice(j * CAP, (j + 1) * CAP)
        rows_ext[r, :width] = grads_ref[j, :CAP, :]
        inner = columns[:CAP, j : j + 1]
        high = inner.astype(BF16).astype(F32)
        spread_out = jnp.where(
            lane == expert, high, jnp.where(lane == experts + expert, inner - high, 0.0)
        )
        rows_ext[r, width:] = spread_out.astype(BF16)
    gate_cols[...] = jnp.zeros_like(gate_cols)
    gate_cols[:experts, :] = gates_ref[...]
    router[...] = jnp.zeros_like(router)
    router[:experts, :] = router_ref[...]

    def routing(i, carry):
        r = pl.ds(pl.multiple_of(i * TILE, TILE), TILE)
        first = tgt_ref[r, 0:1]
        second = tgt_ref[r, 1:2]
        slot = iota((TILE, hot.shape[1]), 1).astype(F32)
        hot[...] = ((slot == first) | (slot == second)).astype(F32).astype(BF16)
        back = dot(hot[...], rows_ext[...])
        inner = back[:, width : width + experts] + back[:, width + experts : width + 2 * experts]
        gates = gate_cols[:, r].T[:, :experts]
        grad = gates * (inner - jnp.sum(gates * inner, axis=1, keepdims=True))
        grad = jnp.concatenate([grad, jnp.zeros((TILE, 128 - experts), F32)], axis=1)
        grad = grad.astype(BF16)
        dlog[:, r] = grad.T
        gmoe = dmoe_ref[r, :] + back[:, :width] + dot(grad, router[...])
        member = member_block(bounds, i * TILE, TILE)
        turned_member = member_rows(bounds, i * TILE, TILE)
        normed, row_scale = norm_rows(hidden_ref[r, :])
        collect(turned_member, 3, gmoe)
        collect(turned_member, 4, gmoe * normed)
        grad_hidden = cot_ref[r, :].astype(F32) + norm_back(
            gmoe * (1.0 + part(member, 4)), normed, row_scale
        )
        ghid[r, :] = grad_hidden
        grad_attn = (part(member, 2) * grad_hidden).astype(BF16)
        attn_out = dot(att_ref[r, :], out_w_ref[...]) + out_b_ref[...].reshape(1, -1)
        collect(turned_member, 2, grad_hidden * attn_out)
        to = pl.ds(pl.multiple_of(i * TILE, TILE), TILE)
        gatt[to, :] = dot_t(grad_attn, out_w_ref[...]).astype(BF16)
        dqkv[r, :width] = grad_attn
        turned[:, r] = att_ref[r, :].T
        return carry

    lax.fori_loop(0, blocks, routing, 0)
    if reduce:
        up_swap += [swap_part(eup_any, up_sum, k) for k in range(2, 4)]
    inputs[0].wait()
    drouter = dot(dlog[...], moe_ref[...])[:experts]
    dout_w = dot(turned[...], dqkv[:, :width])
    dout_b = jnp.sum(dqkv[:, :width].astype(F32), axis=0, keepdims=True)
    nets = sup_b_ref.shape[0]
    load[1, :width, lane_half - width :] = dout_w.astype(BF16)
    router_rows = jnp.concatenate([drouter, jnp.zeros((experts, hidden - width), F32)], axis=1)
    vectors = jnp.concatenate(
        [dout_b, sdn_b_ref[...], jnp.zeros((1, hidden - 2 * width), F32)], axis=1
    )
    filler = jnp.zeros((rows - width - experts - nets - 1, hidden), F32)
    bottom = jnp.concatenate(
        [router_rows] + [sup_b_ref[n] for n in range(nets)] + [vectors, filler], axis=0
    ).astype(BF16)
    for half in range(2):
        load[half, width:] = bottom[:, half * lane_half : (half + 1) * lane_half]

    inputs[1].wait()
    for r in range(0, padded, BLOCK):
        kt[:, r : r + BLOCK] = qkv_ref[r : r + BLOCK, width : 2 * width].T
    dkeys[...] = jnp.zeros_like(dkeys)
    dvals[...] = jnp.zeros_like(dvals)
    first_half = iota((BLOCK, 128), 1) < HDIM

    def split(pair_rows):
        zero = jnp.zeros_like(pair_rows)
        return jnp.concatenate(
            [jnp.where(first_half, pair_rows, zero), jnp.where(first_half, zero, pair_rows)],
            axis=0,
        )

    def attend(i, carry):
        q_rows = pl.ds(pl.multiple_of(i * BLOCK + WINDOW, 64), BLOCK)
        k_rows = pl.ds(pl.multiple_of(i * BLOCK, BLOCK), SPAN)
        o_rows = pl.ds(pl.multiple_of(i * BLOCK, BLOCK), BLOCK)
        key_segment = segments(bounds, i * BLOCK - WINDOW + iota((SPAN, BLOCK), 0))
        query_segment = segments(bounds, i * BLOCK + iota((1, BLOCK), 1))
        allowed = key_segment == query_segment
        allowed = jnp.concatenate([allowed, allowed], axis=1)
        for pair in range(HEADS // 2):
            lanes = slice(pair * 128, (pair + 1) * 128)
            q = split(qkv_ref[q_rows, lanes])
            out_grad = split(gatt[o_rows, lanes])
            k = qkv_ref[k_rows, width + pair * 128 : width + (pair + 1) * 128]
            v = qkv_ref[k_rows, 2 * width + pair * 128 : 2 * width + (pair + 1) * 128]
            log_total = jnp.concatenate(
                [lse_ref[2 * pair : 2 * pair + 1, o_rows], lse_ref[2 * pair + 1 : 2 * pair + 2, o_rows]],
                axis=1,
            )
            probs = jnp.exp(jnp.where(allowed, dot_t(k, q) * scale, MASK_FILL) - log_total)
            grad_probs = dot_t(v, out_grad)
            inner = jnp.sum(probs * grad_probs, axis=0, keepdims=True)
            grad_scores = (probs * (grad_probs - inner)).astype(BF16)
            dvals[k_rows, lanes] += dot(probs.astype(BF16), out_grad)
            dkeys[k_rows, lanes] += dot(grad_scores, q) * scale
            turned_query = dot(kt[lanes, k_rows], grad_scores) * scale
            turned_query = jnp.concatenate(
                [turned_query[:HDIM, :BLOCK], turned_query[HDIM:, BLOCK:]], axis=0
            )
            dqkv[o_rows, lanes] = turned_query.T.astype(BF16)
        return carry

    lax.fori_loop(0, 4, attend, 0)
    if reduce:
        finish_all(line_a)
        all_a = line_spread(part_ref, 0, quarter_a)
        finish_all(plane_b)
        own_b.wait()
        summed = next_part[...].astype(F32)
        for index in range(len(OTHERS)):
            summed = summed + pieces[index].astype(F32)
        next_part[...] = summed.astype(BF16)
        line_b = line_exchange(next_part, 3)
        down_swap = [swap_part(edn_any, dn_sum, 0)]
    lax.fori_loop(4, slots // BLOCK, attend, 0)
    if reduce:
        finish_all(line_b)
        all_b = line_spread(next_part, 3, quarter_b)
        down_swap += [swap_part(edn_any, dn_sum, k) for k in range(1, 3)]

    inputs[2].wait()

    def project(i, carry):
        r = pl.ds(pl.multiple_of(i * TILE, TILE), TILE)
        from_rows = pl.ds(pl.multiple_of(i * TILE + WINDOW, 64), TILE)
        dqkv[r, width : 2 * width] = dkeys[from_rows, :].astype(BF16)
        dqkv[r, 2 * width :] = dvals[from_rows, :].astype(BF16)
        member = member_block(bounds, i * TILE, TILE)
        normed, _ = norm_rows(tokens_ref[r, :].astype(F32))
        turned[:, r] = (normed * (1.0 + part(member, 1)) + part(member, 0)).astype(BF16).T
        return carry

    lax.fori_loop(0, blocks, project, 0)
    dqkv_w = dot(turned[...], dqkv[...]).astype(BF16)
    load[0, :width] = dqkv_w[:, :lane_half]
    load[1, :width, : lane_half - width] = dqkv_w[:, lane_half:]
    if reduce:
        swap = give(load.at[1 - odd], got, sibling())
    else:
        done[...] = load[...]

    def finish(i, carry):
        r = pl.ds(pl.multiple_of(i * TILE, TILE), TILE)
        member = member_block(bounds, i * TILE, TILE)
        turned_member = member_rows(bounds, i * TILE, TILE)
        gmix = dot_t(dqkv[r, :], qkv_w_ref[...])
        normed, row_scale = norm_rows(tokens_ref[r, :].astype(F32))
        gain = 1.0 + part(member, 1)
        collect(turned_member, 0, gmix)
        collect(turned_member, 1, gmix * normed)
        dtok_ref[r, :] = ghid[r, :] + norm_back(gmix * gain, normed, row_scale)
        return carry

    lax.fori_loop(0, blocks, finish, 0)
    if reduce:
        swap.wait()
        keep[...] = (load[odd].astype(F32) + got[...].astype(F32)).astype(BF16)
        plane_sums = []
        for index, offset in enumerate(OTHERS):
            device, second, half = plane_partner(*offset)
            source = keep.at[
                pl.ds(second * quarter_rows, quarter_rows),
                pl.ds(pl.multiple_of(half * quarter_lanes, 128), quarter_lanes),
            ]
            plane_sums.append(give(source, tail_pieces.at[index], device))
        finish_all(all_a)
        plane_all_a = plane_spread(quarter_a, full_a, 0)
        down_swap += [swap_part(edn_any, dn_sum, 3)]
    inputs[3].wait()
    inputs[4].wait()
    own.wait()
    finish_all(copies)
    for j in range(experts):
        rows_ext[j * CAP : (j + 1) * CAP, :width] = res[j]

    def result(i, carry):
        r = pl.ds(pl.multiple_of(i * TILE, TILE), TILE)
        member = member_block(bounds, i * TILE, TILE)
        first = tgt_ref[r, 0:1]
        second = tgt_ref[r, 1:2]
        slot = iota((TILE, hot.shape[1]), 1).astype(F32)
        hot[...] = ((slot == first) | (slot == second)).astype(F32).astype(BF16)
        branch = dot(hot[...], rows_ext[:, :width]) + shared_ref[r, :]
        layer = hidden_ref[r, :] + part(member, 5) * branch
        layer_ref[r, :] = layer.astype(BF16)
        valid = (i * TILE + iota((TILE, width), 0)) < total
        collect(member_rows(bounds, i * TILE, TILE), 5, cot_ref[r, :].astype(F32) * branch)
        layer_squares = jnp.sum(jnp.where(valid, layer * layer, 0.0), axis=0, keepdims=True)
        branch_squares = jnp.sum(jnp.where(valid, branch * branch, 0.0), axis=0, keepdims=True)
        return (carry[0] + layer_squares, carry[1] + branch_squares)

    nothing = jnp.zeros((1, width), F32)
    squares = lax.fori_loop(0, blocks, result, (nothing, nothing))
    count = jnp.full((1, 1), total * width, jnp.int32).astype(F32)
    roots = [jnp.sqrt(jnp.sum(line, axis=1, keepdims=True) / count) for line in squares]
    rms_ref[...] = jnp.where(iota((1, 128), 1) == 0, roots[0], roots[1])

    grad_mod = sums[0:8, :]
    high, low = high_low(grad_mod)
    grad_act = dot_t(high, ada_ref[...]) + dot_t(low, ada_ref[...])
    condition = cond_ref[...]
    sigmoid = 1.0 / (1.0 + jnp.exp(-condition))
    grad_cond = grad_act * (sigmoid * (1.0 + condition * (1.0 - sigmoid)))
    row = iota((8, 128), 0)
    lane = iota((8, 128), 1)
    label = jnp.zeros((8, 128), jnp.int32)
    for image in range(len(bounds)):
        label = jnp.where(row == image, labels_ref[0, image], label)
    time = jnp.full((8, 128), time_ref[0], jnp.int32)
    digits = [label // 32, label % 32, time // 32, time % 32]
    marks = jnp.zeros((8, 128), jnp.int32)
    for index, piece in enumerate(digits):
        marks = jnp.where(lane == index, piece, marks)
    real = row < len(bounds)
    marks = jnp.where(real, marks, jnp.where(lane < 4, 255, 0)).astype(F32)
    inside = (iota((8, width), 0) < len(bounds)).astype(F32)
    note = jnp.concatenate([grad_mod, grad_cond * inside, marks], axis=1)
    middle = note.shape[1] // 2
    note_here[...] = jnp.concatenate([note[:, :middle], note[:, middle:]], axis=0).astype(BF16)
    if not reduce:
        notes[0, 0, 0, 0] = note_here[...]
        return

    notes[odd, two, half_here, line_here] = note_here[...]
    target = notes.at[odd, two, half_here, line_here]
    note_line = [give(note_here, target, line_partner(*o)[0]) for o in OTHERS]
    finish_all(plane_sums)
    here_rows = pl.ds(pl.multiple_of(two * quarter_rows, 16), quarter_rows)
    here_lanes = pl.ds(pl.multiple_of(half_here * quarter_lanes, 128), quarter_lanes)
    summed = keep[here_rows, here_lanes].astype(F32)
    for index in range(len(OTHERS)):
        summed = summed + tail_pieces[index].astype(F32)
    zgot_wide[0] = summed.astype(BF16)
    beside = give(zgot_wide.at[0], zgot_wide.at[1], line_partner(0, 1)[0])
    finish_all(up_swap)
    loads[0].wait()
    for r in range(0, up_rows, 64):
        s = slice(r, r + 64)
        up_sum[s] = (up_mine[s].astype(F32) + up_sum[s].astype(F32)).astype(BF16)
    up_part = up_rows // 4
    dn_part = dn_rows // 4
    spread_rows = []
    for offset in OTHERS:
        device, place = owner_partner(*offset)
        source = up_sum.at[pl.ds(place * up_part, up_part)]
        spread_rows.append(give(source, up_got.at[owner_here], device))
    up_got[owner_here] = up_sum[pl.ds(pl.multiple_of(owner_here * up_part, 16), up_part)]
    to_second_a, others_a = plane_all_a
    others_a.append(pass_on(to_second_a, full_a.at[odd, 1 - two, shared_rows]))
    finish_all(all_b)
    plane_all_b = plane_spread(quarter_b, full_b, 1)
    finish_all(note_line)
    target = notes.at[odd, two, half_here]
    to_second_n = give(target, target, plane_partner(1, 0)[0])
    others_n = [give(target, target, plane_partner(0, 1)[0])]
    beside.wait()
    summed = zgot_wide[0].astype(F32) + zgot_wide[1].astype(F32)
    zgot_wide[2] = summed.astype(BF16)
    beyond = give(zgot_wide.at[2], zgot_wide.at[3], across)
    to_second_b, others_b = plane_all_b
    others_b.append(pass_on(to_second_b, full_b.at[odd, 1 - two, shared_rows]))
    finish_all(others_a)
    last = [give(full_a.at[odd], full_a.at[odd], sibling())]
    others_n.append(pass_on(to_second_n, notes.at[odd, 1 - two, half_here]))
    beyond.wait()
    summed = zgot_wide[2].astype(F32) + zgot_wide[3].astype(F32)
    done[odd, here_rows, here_lanes] = summed.astype(BF16)
    place = done.at[
        odd,
        pl.ds(two * quarter_rows, quarter_rows),
        pl.ds(pl.multiple_of(half_here * quarter_lanes, 128), quarter_lanes),
    ]
    to_second_d = give(place, place, plane_partner(1, 0)[0])
    others_d = [give(place, place, plane_partner(0, 1)[0])]
    second_block = done.at[
        odd,
        pl.ds((1 - two) * quarter_rows, quarter_rows),
        pl.ds(pl.multiple_of(half_here * quarter_lanes, 128), quarter_lanes),
    ]

    finish_all(down_swap)
    loads[1].wait()
    for r in range(0, dn_rows, 64):
        s = slice(r, r + 64)
        dn_sum[s] = (dn_mine[s].astype(F32) + dn_sum[s].astype(F32)).astype(BF16)
    for offset in OTHERS:
        device, place = owner_partner(*offset)
        source = dn_sum.at[pl.ds(place * dn_part, dn_part)]
        spread_rows.append(give(source, dn_got.at[owner_here], device))
    dn_got[owner_here] = dn_sum[pl.ds(pl.multiple_of(owner_here * dn_part, 16), dn_part)]

    others_d.append(pass_on(to_second_d, second_block))
    finish_all(others_n)
    last.append(give(notes.at[odd], notes.at[odd], sibling()))
    finish_all(others_b)
    last.append(give(full_b.at[odd], full_b.at[odd], sibling()))
    finish_all(others_d)
    last.append(give(done.at[odd], done.at[odd], sibling()))
    finish_all(side_all)
    finish_all(spread_rows)
    finish_all(last)


def backward(owners, reduce, *args):
    tokens, mod, qkv_pad, gates = (args[k] for k in (3, 5, 7, 12))
    part, eup, edown = (args[k] for k in (26, 28, 29))
    slots, width = tokens.shape
    padded = qkv_pad.shape[0]
    experts = gates.shape[0]
    hidden = edown.shape[0]
    nets = args[23].shape[0]
    rows = width + 32
    lanes = hidden // 2
    note = (16, (7 * width + 128) // 2)
    in_specs = [in_smem()] * 3 + [in_vmem()] * (len(args) - 3)
    for index in (3, 7, 11, 14, 17, 22, 27, 28, 29):
        in_specs[index] = anywhere()
    full = like((2, nets, width, lanes) if reduce else (1, 1, 16, 128), BF16)

    def sized(*shape):
        return pltpu.VMEM(shape if reduce else (16,) * (len(shape) - 1) + (128,), BF16)

    return pl.pallas_call(
        functools.partial(backward_kernel, owners, experts // owners, reduce),
        in_specs=in_specs,
        out_specs=[in_vmem()] * 3 + [anywhere()] * 2 + [in_vmem()] * 5,
        out_shape=[
            like((slots, width), BF16),
            like((slots, width), F32),
            like((1, 128), F32),
            full,
            full,
            like((2, rows, lanes), BF16),
            like((2, 2, 2, 4) + note, BF16),
            like((4, width // 8, hidden), BF16),
            like((4, hidden // 8, width), BF16),
            like((8, 16, 128), BF16),
        ],
        scratch_shapes=[
            pltpu.VMEM((128, 6 * width), BF16),
            pltpu.VMEM((TILE, experts * CAP), BF16),
            pltpu.VMEM((experts * CAP, width + 128), BF16),
            pltpu.VMEM((128, slots), F32),
            pltpu.VMEM((slots, width), F32),
            pltpu.VMEM((slots, width), BF16),
            pltpu.VMEM((width, padded), BF16),
            pltpu.VMEM((padded, width), F32),
            pltpu.VMEM((padded, width), F32),
            pltpu.VMEM((slots, 3 * width), BF16),
            pltpu.VMEM((width, slots), BF16),
            pltpu.VMEM((128, slots), BF16),
            pltpu.VMEM((16, 6 * width), F32),
            pltpu.VMEM((128, 256), F32),
            pltpu.VMEM((256, 128), F32),
            pltpu.VMEM((128, width), BF16),
            pltpu.VMEM((experts, CAP, width), BF16),
            pltpu.SemaphoreType.DMA((experts,)),
            pltpu.SemaphoreType.DMA((experts,)),
            pltpu.SemaphoreType.DMA,
            pltpu.VMEM((2, rows, lanes), BF16),
            sized(rows, lanes),
            sized(rows, lanes),
            sized(3, rows // 2, lanes // 2),
            sized(4, rows // 2, lanes // 2),
            sized(6, width // 8, lanes),
            sized(width // 2, lanes),
            sized(width // 2, lanes),
            sized(width // 2, lanes),
            sized(3, width // 2, lanes),
            sized(width // 2, hidden),
            sized(width // 2, hidden),
            sized(hidden // 2, width),
            sized(hidden // 2, width),
            pltpu.VMEM(note, BF16),
            pltpu.VMEM(tokens.shape, tokens.dtype),
            pltpu.VMEM(qkv_pad.shape, qkv_pad.dtype),
            pltpu.VMEM(args[11].shape, args[11].dtype),
            pltpu.VMEM(args[14].shape, args[14].dtype),
            pltpu.VMEM(args[22].shape, args[22].dtype),
            pltpu.SemaphoreType.DMA((5,)),
            pltpu.SemaphoreType.DMA((80,)),
            pltpu.SemaphoreType.DMA((80,)),
            pltpu.SemaphoreType.DMA((5,)),
        ],
        compiler_params=pltpu.CompilerParams(
            vmem_limit_bytes=VMEM_BYTES, collective_id=3, has_side_effects=True
        ),
        name="backward",
    )(*args)


def finish_kernel(
    nets,
    dp_count,
    full_a_any,
    full_b_any,
    done_any,
    notes_any,
    up_any,
    dn_any,
    sides_ref,
    time_table_any,
    label_table_any,
    layer_in,
    tokens_in,
    time_any,
    label_any,
    ada_any,
    ada_b_ref,
    qkv_any,
    out_any,
    out_b_ref,
    router_ref,
    eup_any,
    eup_b_ref,
    edn_any,
    edn_b_ref,
    sup_any,
    sup_b_ref,
    sdn_any,
    sdn_b_ref,
    layer_out,
    tokens_out,
    full_a,
    full_b,
    done_ref,
    notes_ref,
    up_ref,
    dn_ref,
    time_table_ref,
    label_table_ref,
    layer_here,
    tokens_here,
    time_out,
    label_out,
    ada_out,
    qkv_out,
    weight_out,
    eup_out,
    edn_out,
    sup_out,
    sdn_out,
    in_sems,
    out_sems,
):
    width = out_any.shape[0]
    lanes = done_ref.shape[2]
    experts = router_ref.shape[0]
    pairs = [
        (up_any, up_ref),
        (dn_any, dn_ref),
        (notes_any, notes_ref),
        (label_table_any, label_table_ref),
        (time_table_any, time_table_ref),
        (done_any, done_ref),
        (full_a_any, full_a),
        (full_b_any, full_b),
        (tokens_in, tokens_here),
        (layer_in, layer_here),
    ]
    ins = [
        pltpu.make_async_copy(source, target, in_sems.at[index])
        for index, (source, target) in enumerate(pairs)
    ]
    for copy in ins:
        copy.start()
    outs = []

    def write(source, target):
        copy = pltpu.make_async_copy(source, target, out_sems.at[len(outs)])
        copy.start()
        outs.append(copy)

    ins[0].wait()
    eup_out[...] = up_ref[...].astype(F32)
    write(eup_out, eup_any)
    ins[1].wait()
    edn_out[...] = dn_ref[...].astype(F32)
    write(edn_out, edn_any)
    for index in range(2, 5):
        ins[index].wait()

    notes = notes_ref[...].reshape(-1, notes_ref.shape[4], notes_ref.shape[5])
    high = notes[:, 0:8, :].reshape(-1, notes.shape[2])
    low = notes[:, 8:16, :].reshape(-1, notes.shape[2])
    rows = jnp.concatenate([high, low], axis=1)
    count = rows.shape[0]
    grad_mod = rows[:, : 6 * width]
    grad_cond = rows[:, 6 * width : 7 * width]
    marks = rows[:, 7 * width :].astype(F32)
    label = marks[:, 0:1] * 32.0 + marks[:, 1:2]
    time = marks[:, 2:3] * 32.0 + marks[:, 3:4]

    def table(marked, out_ref):
        line = jnp.broadcast_to(marked, (count, 128)).T[0:1, :]
        tall = (iota((out_ref.shape[0], count), 0).astype(F32) == line).astype(F32).astype(BF16)
        out_ref[...] = dot(tall, grad_cond)

    table(label, label_out)
    write(label_out, label_any)
    table(time, time_out)
    write(time_out, time_any)
    label_hot = (iota((count, label_table_ref.shape[0]), 1).astype(F32) == label).astype(F32)
    time_hot = (iota((count, time_table_ref.shape[0]), 1).astype(F32) == time).astype(F32)
    condition = dot(label_hot.astype(BF16), label_table_ref[...])
    condition = condition + dot(time_hot.astype(BF16), time_table_ref[...])
    act = condition / (1.0 + jnp.exp(-condition))
    ada_out[...] = dot(act.T.astype(BF16), grad_mod)
    write(ada_out, ada_any)
    ada_b_ref[...] = jnp.sum(grad_mod.astype(F32), axis=0, keepdims=True).reshape(-1)

    ins[5].wait()
    rest = qkv_any.shape[1] - lanes
    qkv_out[:, :lanes] = done_ref[0, :width].astype(F32)
    qkv_out[:, lanes:] = done_ref[1, :width, :rest].astype(F32)
    write(qkv_out, qkv_any)
    weight_out[...] = done_ref[1, :width, rest:].astype(F32)
    write(weight_out, out_any)
    for index, half in enumerate((full_a, full_b)):
        ins[6 + index].wait()
        for net in range(nets):
            first = index * lanes
            sdn_out[net, first : first + lanes, :] = half[1, net].astype(F32).T
            write(sdn_out.at[net, pl.ds(first, lanes)], sdn_any.at[net, pl.ds(first, lanes)])
            sup_out[net, :, first : first + lanes] = half[0, net].astype(F32)
            if index:
                write(sup_out.at[net], sup_any.at[net])

    ins[8].wait()
    write(tokens_here, tokens_out)
    ins[9].wait()
    write(layer_here, layer_out)

    rest_a = done_ref[0, width:].astype(F32)
    rest_b = done_ref[1, width:].astype(F32)
    router_ref[...] = rest_a[:experts, :width]
    sup_b_ref[:, :lanes] = rest_a[experts : experts + nets]
    sup_b_ref[:, lanes:] = rest_b[experts : experts + nets]
    last = rest_a[experts + nets : experts + nets + 1]
    out_b_ref[...] = last[:, :width].reshape(-1)
    sdn_b_ref[...] = jnp.broadcast_to(last[:, width:], sdn_b_ref.shape)
    place = lax.axis_index(("p0", "p1", "p2"))
    for index in range(4):
        total = sides_ref[index].astype(F32) + sides_ref[4 + index].astype(F32)
        up_size = lanes // 64
        up_line = jnp.concatenate([total[k : k + 1] for k in range(up_size)], axis=1)
        dn_line = jnp.concatenate([total[up_size + k : up_size + k + 1] for k in range(width // 128)], axis=1)
        up_rows = eup_b_ref.shape[1]
        dn_rows = edn_b_ref.shape[1]
        up_line = jnp.broadcast_to(up_line, (8, up_line.shape[1]))
        dn_line = jnp.broadcast_to(dn_line, (8, dn_line.shape[1]))
        turned = pltpu.roll(up_line, up_line.shape[1] - place * up_rows, 1)
        eup_b_ref[index : index + 1, :] = turned[0:1, :up_rows]
        turned = pltpu.roll(dn_line, dn_line.shape[1] - place * dn_rows, 1)
        edn_b_ref[index : index + 1, :] = turned[0:1, :dn_rows]
    finish_all(outs)


def finish(gathered, time_table, label_table, layer, tokens, experts, width, hidden, nets, dp_count):
    time_shape = time_table.shape
    label_shape = label_table.shape
    shapes = [
        time_shape,
        label_shape,
        (width, 6 * width),
        (6 * width,),
        (width, 3 * width),
        (width, width),
        (width,),
        (experts, width),
        (4, width // 8, hidden),
        (4, hidden // dp_count),
        (4, hidden // 8, width),
        (4, width // dp_count),
        (nets, width, hidden),
        (nets, hidden),
        (nets, hidden, width),
        (nets, width),
    ]
    large = (0, 1, 2, 4, 5, 8, 10, 12, 14)
    specs = [anywhere() if index in large else in_vmem() for index in range(len(shapes))]
    kept = [gathered[k] for k in range(6)] + [time_table, label_table, layer, tokens]
    return pl.pallas_call(
        functools.partial(finish_kernel, nets, dp_count),
        in_specs=[anywhere()] * 6 + [in_vmem()] + [anywhere()] * 4,
        out_specs=specs + [anywhere()] * 2,
        out_shape=[like(shape, F32) for shape in shapes]
        + [like(layer.shape, layer.dtype), like(tokens.shape, tokens.dtype)],
        scratch_shapes=[pltpu.VMEM(array.shape, array.dtype) for array in kept]
        + [pltpu.VMEM(shapes[index], F32) for index in large]
        + [pltpu.SemaphoreType.DMA((10,)), pltpu.SemaphoreType.DMA((20,))],
        compiler_params=pltpu.CompilerParams(vmem_limit_bytes=VMEM_BYTES),
        name="finish",
    )(*gathered, time_table, label_table, layer, tokens)


def exchange(blocks, axes):
    return lax.all_to_all(blocks, axes, split_axis=0, concat_axis=0, tiled=True)


def spread(block, axes):
    count = lax.axis_size(axes)
    return exchange(jnp.broadcast_to(block[None], (count,) + block.shape), axes)


def sum_blocks(blocks):
    return jnp.sum(blocks.astype(F32), axis=0)


def sum_everywhere(payload):
    rows, width = payload.shape
    near = ("p2", "expert")
    far = ("p0", "p1")
    near_count = lax.axis_size(near)
    far_count = lax.axis_size(far)
    piece = rows // near_count
    part = exchange(payload.astype(BF16).reshape(near_count, piece, width), near)
    part = sum_blocks(part).astype(BF16)
    part = part.reshape(piece, far_count, width // far_count).transpose(1, 0, 2)
    part = sum_blocks(exchange(part, far)).astype(BF16)
    part = spread(part, far).transpose(1, 0, 2).reshape(piece, width)
    return spread(part, near).reshape(rows, width)


def body(
    tokens,
    cotangent,
    patch_counts,
    time_buckets,
    image_labels,
    expert_routes,
    time_table,
    label_table,
    ada_weight,
    ada_bias,
    qkv_weight,
    out_weight,
    out_bias,
    router_weight,
    expert_up,
    expert_up_bias,
    expert_down,
    expert_down_bias,
    shared_up,
    shared_up_bias,
    shared_down,
    shared_down_bias,
):
    slot_count, width = tokens.shape
    expert_count = router_weight.shape[1]
    local_count, _, hidden = expert_up.shape
    nets = shared_up.shape[0]
    owners = lax.axis_size("expert")
    outer = lax.axis_size("p0")
    dp_count = lax.axis_size(("p0", "p1", "p2"))
    dp_here = lax.axis_index(("p0", "p1", "p2"))
    small = outer == 2 and owners == 4

    routes = expert_routes[0].T
    router_turned = router_weight.T
    (
        modulation,
        condition,
        targets,
        grad_branch,
        owner_branch,
        qkv_pad,
        attended,
        log_totals,
        hidden_one,
        moe_in,
        gates,
        send_rows,
    ) = forward(
        owners,
        expert_count,
        patch_counts,
        image_labels,
        time_buckets,
        routes,
        time_table,
        label_table,
        ada_weight,
        ada_bias,
        cotangent,
        tokens,
        qkv_weight,
        out_weight,
        out_bias,
        router_turned,
    )
    shared_total, grad_moe_in, wire, grad_sup_bias, grad_sdown_bias, owner_rows = shared_nets(
        owners,
        small,
        moe_in,
        grad_branch,
        shared_up,
        shared_up_bias,
        shared_down,
        shared_down_bias,
        send_rows,
    )
    owner_res, grad_eup, grad_edown, side, returned_grads, part = routed_net(
        owners,
        small,
        owner_rows,
        owner_branch,
        expert_up,
        expert_up_bias,
        expert_down,
        expert_down_bias,
        wire,
    )
    (
        layer_out,
        grad_tokens,
        rms_row,
        full_a,
        full_b,
        last_rows,
        notes,
        up_rows,
        down_rows,
        side_rows,
    ) = backward(
        owners,
        small,
        patch_counts,
        image_labels,
        time_buckets,
        tokens,
        cotangent,
        modulation,
        condition,
        qkv_pad,
        attended,
        log_totals,
        hidden_one,
        moe_in,
        gates,
        targets,
        shared_total,
        grad_moe_in,
        returned_grads,
        owner_res,
        qkv_weight,
        out_weight,
        out_bias,
        router_turned,
        ada_weight,
        grad_sup_bias,
        grad_sdown_bias,
        side,
        part,
        wire,
        grad_eup,
        grad_edown,
    )
    if small:
        gathered = (full_a, full_b, last_rows, notes, up_rows, down_rows, side_rows)
        (
            sum_time,
            sum_label,
            sum_ada,
            sum_ada_bias,
            sum_qkv,
            sum_out_weight,
            sum_out_bias,
            sum_router,
            sum_eup,
            sum_eup_bias,
            sum_edown,
            sum_edown_bias,
            sum_sup,
            sum_sup_bias,
            sum_sdown,
            sum_sdown_bias,
            layer_out,
            grad_tokens,
        ) = finish(
            gathered,
            time_table,
            label_table,
            layer_out,
            grad_tokens,
            expert_count,
            width,
            hidden,
            nets,
            dp_count,
        )
        sum_router = sum_router.T
    else:
        up_blocks = exchange(grad_eup.reshape(outer, width // outer, hidden), "p0")
        up_part = sum_blocks(up_blocks).astype(BF16).reshape(-1, width // dp_count, hidden)
        sum_eup = exchange(up_part, ("p1", "p2")).astype(F32)
        down_blocks = exchange(grad_edown.reshape(outer, hidden // outer, width), "p0")
        down_part = sum_blocks(down_blocks).astype(BF16).reshape(-1, hidden // dp_count, width)
        sum_edown = exchange(down_part, ("p1", "p2")).astype(F32)
        sides = lax.psum(side.astype(F32), "p0")
        sides = spread(sides, ("p1", "p2"))
        sides = sides.reshape(sides.shape[0], -1)
        side_up = sides[:, :hidden]
        side_down = sides[:, hidden : hidden + width]

        shared_sums = sum_everywhere(wire.reshape(-1, hidden)).astype(F32)
        shared_sums = shared_sums.reshape((2, nets, width, hidden))
        sum_sup = shared_sums[0]
        sum_sdown = shared_sums[1].transpose(0, 2, 1)

        note = notes[0, 0, 0, 0]
        all_rows = spread(jnp.concatenate([note[:8], note[8:]], axis=1), ALL)
        all_rows = all_rows.reshape(-1, 2 * note.shape[1])
        all_modulation = all_rows[:, : 6 * width]
        all_condition = all_rows[:, 6 * width : 7 * width]
        marks = all_rows[:, 7 * width : 7 * width + 4].astype(jnp.int32)
        label_ids = jnp.arange(label_table.shape[0], dtype=jnp.int32)
        label_hot = ((marks[:, 0:1] * 32 + marks[:, 1:2]) == label_ids).astype(BF16)
        time_ids = jnp.arange(time_table.shape[0], dtype=jnp.int32)
        time_hot = ((marks[:, 2:3] * 32 + marks[:, 3:4]) == time_ids).astype(BF16)
        all_act = jax.nn.silu(
            jnp.dot(label_hot, label_table, preferred_element_type=F32)
            + jnp.dot(time_hot, time_table, preferred_element_type=F32)
        ).astype(BF16)
        sum_ada = lax.dot_general(all_act, all_modulation, ROWS_FIRST, preferred_element_type=F32)
        sum_ada_bias = jnp.sum(all_modulation.astype(F32), axis=0)
        sum_label = lax.dot_general(
            label_hot, all_condition, ROWS_FIRST, preferred_element_type=F32
        )
        sum_time = lax.dot_general(time_hot, all_condition, ROWS_FIRST, preferred_element_type=F32)

        last = jnp.concatenate([last_rows[0], last_rows[1]], axis=1)
        last = sum_everywhere(last).astype(F32)
        sum_qkv = last[:width, : 3 * width]
        sum_out_weight = last[:width, 3 * width :]
        rest = last[width:]
        sum_eup_bias = lax.dynamic_slice_in_dim(
            side_up, dp_here * (hidden // dp_count), hidden // dp_count, 1
        )
        sum_edown_bias = lax.dynamic_slice_in_dim(
            side_down, dp_here * (width // dp_count), width // dp_count, 1
        )
        sum_router = rest[:expert_count, :width].T
        sum_sup_bias = rest[expert_count : expert_count + nets]
        sum_out_bias = rest[expert_count + nets, :width]
        sum_sdown_bias = jnp.broadcast_to(
            rest[expert_count + nets, width : 2 * width][None], (nets, width)
        )
    return (
        layer_out,
        grad_tokens,
        rms_row[:, :2],
        sum_time,
        sum_label,
        sum_ada,
        sum_ada_bias,
        sum_qkv,
        sum_out_weight,
        sum_out_bias,
        sum_router,
        sum_eup,
        sum_eup_bias,
        sum_edown,
        sum_edown_bias,
        sum_sup,
        sum_sup_bias,
        sum_sdown,
        sum_sdown_bias,
    )


def solution(mesh):
    dp_count = mesh.shape["dp"]
    owners = mesh.shape["expert"]
    split = Mesh(mesh.devices.reshape(dp_count // 4, 2, 2, owners), ALL)
    dp = ("p0", "p1", "p2")
    in_specs = (
        P(ALL, None),
        P(ALL, None),
        P(ALL, None),
        P(ALL),
        P(ALL, None),
        P(ALL, None, None),
        P(),
        P(),
        P(),
        P(),
        P(),
        P(),
        P(),
        P(),
        P("expert", None, None),
        P("expert", None),
        P("expert", None, None),
        P("expert", None),
        P(),
        P(),
        P(),
        P(),
    )
    out_specs = (
        P(ALL, None),
        P(ALL, None),
        P(ALL, None),
        P(),
        P(),
        P(),
        P(),
        P(),
        P(),
        P(),
        P(),
        P("expert", dp, None),
        P("expert", dp),
        P("expert", dp, None),
        P("expert", dp),
        P(),
        P(),
        P(),
        P(),
    )
    return jax.shard_map(body, mesh=split, in_specs=in_specs, out_specs=out_specs, check_vma=False)
```
